32 devices in a mesh: cols: 2 (over core), patch: 16 (over z, y, x).
Axes of the slice: x: 2, y: 2, z: 4, core: 2. Of those that a mesh axis runs over, the one named last changes fastest.
Arguments:
- vectors: bfloat16 [65536, 512], P('patch', 'cols'), may hold values from -6 to 6
- blocks: bfloat16 [512, 8, 128, 128], P('patch'), may hold values from -0.09375 to 0.09375
- tile_cols: int32 [512, 8], P('patch'), may hold values from 0 to 511, as said below
- live_tiles: int32 [16], P('patch'), may hold values from 1 to 32, as said below
Outputs:
- result: bfloat16 [65536, 512], P('patch', 'cols')
The draws below stay inside these ranges and needn't reach their ends.
Inputs may be any that keep to these rules, and one draw needn't show every extreme that they name: `tile_cols`: each listed tile lies within 4 tiles of its own tile row; entries may repeat, and repeated blocks add. `live_tiles`: some patch is full in every draw.
All inputs are finite; a program needn't handle non-finite values.
Results may differ from the reference program's by a relative error of at most 0.0064.
Values may be sent and summed in bfloat16 or wider, within the bound.
No kernel may reach another device: no remote copies, remote signals or barrier semaphores. Data moves between devices by JAX's collectives and lax.ppermute only.
A program may use at most 128 MiB of HBM per device.

```python
import jax
import jax.numpy as jnp
from jax import lax

K = 512
TILE = 128
TILES_DEV = 32
NNZ = 8
HALO_T = 4
STEPS = 3
ITERS = 8
TILES = 512
NV = 65536
N_PATCH = 16


def draw_tile_cols(key, part):
    first = jax.random.fold_in(key, 11)
    second = jax.random.fold_in(key, 12)
    own_ids = jnp.arange(TILES, dtype=jnp.int32)
    offsets = jax.random.randint(first, (TILES, NNZ), -HALO_T, HALO_T + 1, dtype=jnp.int32)
    signs = 2 * jax.random.randint(second, (TILES,), 0, 2, dtype=jnp.int32) - 1
    offsets = offsets.at[:, 0].set(signs * HALO_T)
    return jnp.clip(own_ids[:, None] + offsets, 0, TILES - 1).astype(jnp.int32)


def draw_live_tiles(key, part):
    first = jax.random.fold_in(key, 21)
    second = jax.random.fold_in(key, 22)
    counts = jax.random.randint(first, (N_PATCH,), 1, TILES_DEV + 1, dtype=jnp.int32)
    fullone = jax.random.randint(second, (), 0, N_PATCH, dtype=jnp.int32)
    return jnp.where(jnp.arange(N_PATCH, dtype=jnp.int32) == fullone, TILES_DEV, counts).astype(jnp.int32)


def shard_levels(key, shape, cuts, smallest, high):
    factor_of, own = 1.0, jax.random.fold_in(key, 6)
    for dim, shards_of in cuts:
        steps = jnp.exp(jax.random.uniform(jax.random.fold_in(own, dim), (shards_of,), jnp.float32, smallest / len(cuts), high / len(cuts)))
        factor_of = factor_of * jnp.repeat(steps, shape[dim] // shards_of).reshape([-1 if axis == dim else 1 for axis in range(len(shape))])
    return factor_of


def centred(own_key, shape, deviation, bound, cuts=(), held_as=jnp.bfloat16):
    drawn = jax.random.normal(own_key, shape, jnp.float32) * deviation
    if len(cuts) > 0:
        drawn = shard_levels(own_key, shape, cuts, -0.22, 0.18) * drawn
    return jnp.clip(drawn, min=-bound, max=bound).astype(held_as)


def setup_inputs(seed: int = 0) -> dict:
    splits = jax.random.split(jax.random.key(seed), 5)
    return {
        "vectors": centred(splits[0], (NV, K), 1.0, 6.0, ((0, 16), (1, 2))),
        "blocks": centred(splits[1], (TILES, NNZ, TILE, TILE), (4 * TILE * NNZ) ** -0.5, 0.09375, ((0, 16),)),
        "tile_cols": draw_tile_cols(jax.random.fold_in(splits[4], 71), 0),
        "live_tiles": draw_live_tiles(jax.random.fold_in(splits[4], 71), 0),
    }


def newton_schulz(gram):
    norm = jnp.sqrt(jnp.sum(gram * gram))
    approx = gram / norm
    identity = jnp.eye(gram.shape[0], dtype=jnp.float32)
    inverse = identity
    for sweep in range(ITERS):
        middle = 1.5 * identity - 0.5 * jnp.dot(inverse, approx, precision=lax.Precision.HIGHEST)
        approx = jnp.dot(approx, middle, precision=lax.Precision.HIGHEST)
        inverse = jnp.dot(middle, inverse, precision=lax.Precision.HIGHEST)
    return (inverse, norm)

def reference(vectors, blocks, tile_cols, live_tiles):
    tile_ids = jnp.arange(TILES, dtype=jnp.int32)
    alive = tile_ids % TILES_DEV < live_tiles[tile_ids // TILES_DEV]
    weight = alive.astype(jnp.float32)[:, None, None]
    current = (vectors.reshape(TILES, TILE, K).astype(jnp.float32) * weight).astype(jnp.bfloat16)

    def operate(field):

        def group(index):
            start = (index * TILES_DEV).astype(jnp.int32)
            listed = lax.dynamic_slice_in_dim(tile_cols, start, TILES_DEV, 0)
            stored = lax.dynamic_slice_in_dim(blocks, start, TILES_DEV, 0)
            picked = field[listed]
            return jnp.einsum('tnij,tnjc->tic', stored.astype(jnp.float32), picked.astype(jnp.float32))
        return lax.map(group, jnp.arange(N_PATCH, dtype=jnp.int32)).reshape(TILES, TILE, K)
    previous = current
    following = (weight * operate(current)).astype(jnp.bfloat16)
    for step in range(STEPS - 1):
        nextone = (weight * (2.0 * operate(following) - previous.astype(jnp.float32))).astype(jnp.bfloat16)
        previous, following = (following, nextone)
    filtered = following.reshape(NV, K)
    gram = lax.dot_general(filtered, filtered, (((0,), (0,)), ((), ())), preferred_element_type=jnp.float32)
    inverse, norm = newton_schulz(gram)
    factor = jnp.sqrt(NV / norm)
    product = jnp.dot(filtered, inverse.astype(jnp.bfloat16), preferred_element_type=jnp.float32)
    return (product * factor).astype(jnp.bfloat16)
```

```python
import functools

import jax
import jax.numpy as jnp
from jax import lax
from jax.experimental import pallas as pl
from jax.experimental.pallas import tpu as pltpu
from jax.sharding import PartitionSpec as P

HALO_T = 4
STEPS = 3
ITERS = 8
GROUP = 4

VMEM_LIMIT = 48 * 1024 * 1024
ANY = pl.BlockSpec(memory_space=pl.ANY)
SMEM = pl.BlockSpec(memory_space=pltpu.SMEM)
F32, BF16 = jnp.float32, jnp.bfloat16


def dot(a, b):
    return jnp.dot(a, b, preferred_element_type=F32)


def tile_row(blocks, listed, field):
    wide = jnp.concatenate([blocks(n) for n in range(len(listed))], axis=1)
    tall = jnp.concatenate([field(tile) for tile in listed], axis=0)
    return dot(wide, tall)


def finish(acc, prev, alive):
    value = acc if prev is None else 2.0 * acc - prev.astype(F32)
    return jnp.where(alive, value, 0.0).astype(BF16)


def interior_kernel(first, tiles, nnz, tile, cols_ref, live_ref, *refs):
    if first:
        whole_ref, blocks_ref, out_ref, held, sem = refs
        copies = [pltpu.make_async_copy(whole_ref, held, sem.at[0])]
    else:
        lo_ref, mid_ref, hi_ref, prev_ref, blocks_ref, out_ref, held, sem = refs
        edge = HALO_T
        copies = [
            pltpu.make_async_copy(lo_ref, held.at[pl.ds(0, edge)], sem.at[0]),
            pltpu.make_async_copy(mid_ref, held.at[pl.ds(edge, tiles - 2 * edge)], sem.at[1]),
            pltpu.make_async_copy(hi_ref, held.at[pl.ds(tiles - edge, edge)], sem.at[2]),
        ]
    live = live_ref[0]
    step = pl.program_id(0)

    @pl.when(step == 0)
    def _():
        for copy in copies:
            copy.start()
        for copy in copies:
            copy.wait()
        if first:
            def clear(index, carry):
                held[index] = jnp.zeros(held.shape[1:], BF16)
                return carry
            lax.fori_loop(live, tiles, clear, 0)

    for r in range(GROUP):
        row = HALO_T + step * GROUP + r
        listed = [cols_ref[row, n] for n in range(nnz)]
        acc = tile_row(lambda n: blocks_ref[r, n], listed, lambda c: held[c])
        prev = None if first else prev_ref[r]
        out_ref[r] = finish(acc, prev, row < live)


def interior(first, cols, live, blocks, fields, prev):
    tiles, nnz, tile, _ = blocks.shape
    width = fields[0].shape[-1]
    inner = tiles - 2 * HALO_T
    body = functools.partial(interior_kernel, first, tiles, nnz, tile)
    block_spec = pl.BlockSpec((GROUP, nnz, tile, tile), lambda i: (i + HALO_T // GROUP, 0, 0, 0))
    row_spec = pl.BlockSpec((GROUP, tile, width), lambda i: (i, 0, 0))
    in_specs = [SMEM, SMEM] + [ANY] * len(fields)
    args = [cols, live] + list(fields)
    if not first:
        shift = HALO_T // GROUP if prev.shape[0] == tiles else 0
        in_specs.append(pl.BlockSpec((GROUP, tile, width), lambda i: (i + shift, 0, 0)))
        args.append(prev)
    return pl.pallas_call(
        body,
        grid=(inner // GROUP,),
        in_specs=in_specs + [block_spec],
        out_specs=row_spec,
        out_shape=jax.ShapeDtypeStruct((inner, tile, width), BF16),
        scratch_shapes=[
            pltpu.VMEM((tiles, tile, width), BF16),
            pltpu.SemaphoreType.DMA((3,)),
        ],
        compiler_params=pltpu.CompilerParams(vmem_limit_bytes=VMEM_LIMIT),
        cost_estimate=pl.CostEstimate(
            flops=2 * inner * nnz * tile * tile * width,
            bytes_accessed=inner * nnz * tile * tile * 2 + 3 * tiles * tile * width * 2,
            transcendentals=0,
        ),
        name="interior",
    )(*args, blocks)


def boundary_kernel(first, tiles, nnz, tile, cols_ref, live_ref, *refs):
    edge = HALO_T
    if first:
        below_ref, above_ref, whole_ref, blocks_ref = refs[:4]
        rest = refs[4:]
        own = [
            (whole_ref.at[pl.ds(0, 2 * edge)], edge, 2 * edge),
            (whole_ref.at[pl.ds(tiles - 2 * edge, 2 * edge)], 3 * edge, 2 * edge),
        ]
        lo_out, hi_out, held, stored, sem, block_sem = rest
    else:
        below_ref, above_ref, lo_ref, mid_ref, hi_ref, plo_ref, phi_ref, blocks_ref = refs[:8]
        lo_out, hi_out, held, stored, sem, block_sem, before = refs[8:]
        inner = tiles - 2 * edge
        own = [
            (lo_ref, edge, edge),
            (mid_ref.at[pl.ds(0, edge)], 2 * edge, edge),
            (mid_ref.at[pl.ds(inner - edge, edge)], 3 * edge, edge),
            (hi_ref, 4 * edge, edge),
        ]
    moves = [(src, held.at[pl.ds(at, count)]) for src, at, count in own]
    if not first:
        shift = phi_ref.shape[0] - edge
        moves.append((plo_ref.at[pl.ds(0, edge)], before.at[pl.ds(0, edge)]))
        moves.append((phi_ref.at[pl.ds(shift, edge)], before.at[pl.ds(edge, edge)]))
    moves.append((below_ref, held.at[pl.ds(0, edge)]))
    moves.append((above_ref, held.at[pl.ds(5 * edge, edge)]))
    copies = [
        pltpu.make_async_copy(src, dst, sem.at[i]) for i, (src, dst) in enumerate(moves)
    ]
    for copy in copies:
        copy.start()
    rows = list(range(edge)) + list(range(tiles - edge, tiles))
    fetches = [
        pltpu.make_async_copy(blocks_ref.at[row], stored.at[i], block_sem.at[i])
        for i, row in enumerate(rows)
    ]
    for fetch in fetches:
        fetch.start()
    live = live_ref[0]
    for copy in copies:
        copy.wait()
    if first:
        for own_tile in list(range(2 * edge)) + list(range(tiles - 2 * edge, tiles)):
            at = own_tile + edge if own_tile < 2 * edge else own_tile - tiles + 5 * edge

            @pl.when(own_tile >= live)
            def _():
                held[at] = jnp.zeros(held.shape[1:], BF16)

    for i, row in enumerate(rows):
        fetches[i].wait()
        shift = edge if row < edge else 5 * edge - tiles
        listed = [cols_ref[row, n] + shift for n in range(nnz)]
        acc = tile_row(lambda n: stored[i, n], listed, lambda c: held[c])
        prev = None if first else before[i]
        if row < edge:
            lo_out[row] = finish(acc, prev, row < live)
        else:
            hi_out[row - tiles + edge] = finish(acc, prev, row < live)


def boundary(first, cols, live, blocks, halos, fields, prev):
    tiles, nnz, tile, _ = blocks.shape
    width = fields[0].shape[-1]
    body = functools.partial(boundary_kernel, first, tiles, nnz, tile)
    shape = jax.ShapeDtypeStruct((HALO_T, tile, width), BF16)
    in_specs = [SMEM, SMEM] + [ANY] * (2 + len(fields))
    args = [cols, live] + list(halos) + list(fields)
    scratch = [
        pltpu.VMEM((6 * HALO_T, tile, width), BF16),
        pltpu.VMEM((2 * HALO_T, nnz, tile, tile), BF16),
        pltpu.SemaphoreType.DMA((8,)),
        pltpu.SemaphoreType.DMA((2 * HALO_T,)),
    ]
    if not first:
        in_specs += [ANY] * 2
        args += list(prev)
        scratch.append(pltpu.VMEM((2 * HALO_T, tile, width), BF16))
    out_spec = pl.BlockSpec(memory_space=pltpu.VMEM)
    return pl.pallas_call(
        body,
        in_specs=in_specs + [ANY],
        out_specs=(out_spec, out_spec),
        out_shape=(shape, shape),
        scratch_shapes=scratch,
        compiler_params=pltpu.CompilerParams(vmem_limit_bytes=VMEM_LIMIT),
        cost_estimate=pl.CostEstimate(
            flops=2 * 2 * HALO_T * nnz * tile * tile * width,
            bytes_accessed=2 * HALO_T * nnz * tile * tile * 2 + 10 * HALO_T * tile * width * 2,
            transcendentals=0,
        ),
        name="boundary",
    )(*args, blocks)


def gram_kernel(pairs, chunk, part_ref, *refs):
    fields = refs[: 2 * pairs]
    has_start = len(refs) == 2 * pairs + 4
    out_ref, square, cross = refs[-3:]
    half = square.shape[0] // 2
    square[...] = jnp.zeros(square.shape, F32)
    cross[...] = jnp.zeros(cross.shape, F32)
    is_first = part_ref[0] == 0
    across = (((0,), (0,)), ((), ()))
    for own_ref, other_ref in zip(fields[:pairs], fields[pairs:]):

        def add(index, carry):
            rows = pl.ds(pl.multiple_of(index * chunk, chunk), chunk)
            own, other = own_ref[rows, :], other_ref[rows, :]
            square[...] += lax.dot_general(own, own, across, preferred_element_type=F32)
            left = jnp.where(is_first, own[:, :half], other[:, half:])
            right = jnp.where(is_first, other, own)
            cross[...] += lax.dot_general(left, right, across, preferred_element_type=F32)
            return carry

        lax.fori_loop(0, own_ref.shape[0] // chunk, add, 0)
    blocks = [
        square[:half, :half], square[:half, half:], square[half:, half:],
        cross[:, :half], cross[:, half:],
    ]
    for i, block in enumerate(blocks):
        at = pl.ds(i * half, half)
        out_ref[at, :] = block + refs[2 * pairs][at, :] if has_start else block


def gram_share(part, owns, others, start):
    width = owns[0].shape[1]
    half = width // 2
    chunk = min(owns[0].shape[0], 512)
    body = functools.partial(gram_kernel, len(owns), chunk)
    args = [part] + list(owns) + list(others) + ([] if start is None else [start])
    rows = sum(own.shape[0] for own in owns)
    return pl.pallas_call(
        body,
        in_specs=[SMEM] + [pl.BlockSpec(memory_space=pltpu.VMEM)] * (len(args) - 1),
        out_specs=pl.BlockSpec(memory_space=pltpu.VMEM),
        out_shape=jax.ShapeDtypeStruct((5 * half, half), F32),
        scratch_shapes=[pltpu.VMEM((width, width), F32), pltpu.VMEM((half, width), F32)],
        compiler_params=pltpu.CompilerParams(vmem_limit_bytes=VMEM_LIMIT),
        cost_estimate=pl.CostEstimate(
            flops=2 * rows * width * 3 * half,
            bytes_accessed=2 * rows * width * 2 + 10 * half * half * 4,
            transcendentals=0,
        ),
        name="gram_share",
    )(*args)


def sum_over_patch(share):
    count = lax.axis_size("patch")
    me = lax.axis_index("patch")
    ways = 4
    quarter = me % ways

    def exchange(value, distance):
        return lax.ppermute(value, "patch", [(i, i ^ distance) for i in range(count)])

    parts = share.reshape(ways, -1, share.shape[1])
    pick = lambda d: lax.dynamic_index_in_dim(parts, quarter ^ d, 0, keepdims=False)
    got = [exchange(pick(d), d) for d in range(1, ways)]
    total = (pick(0) + got[0]) + (got[1] + got[2])
    stride = ways
    while stride < count:
        got = [exchange(total, d * stride) for d in range(1, ways)]
        total = (total + got[0]) + (got[1] + got[2])
        stride *= ways
    return jnp.stack([total] + [exchange(total, d) for d in range(1, ways)])


def split(value):
    high = value.astype(BF16)
    return high, (value - high.astype(F32)).astype(BF16)


def product3(left, right_stack):
    high, low = split(left)
    return dot(jnp.concatenate([high, high, low], axis=1), right_stack)


def finish_kernel(
    total_rows, chunk, place_ref, mine_ref, theirs_ref, *refs
):
    fields, out_ref = refs[:6], refs[6]
    shares, x_ref, z_ref, m_ref, stack, wide, result, sem, out_sem = refs[7:]
    part, quarter = place_ref[0], place_ref[1]
    size = x_ref.shape[0]
    width = size // 2
    half = width // 2
    copies = []
    for side in range(2):
        at = 0
        for source in fields[3 * side : 3 * side + 3]:
            rows = source.shape[0]
            target = wide.at[pl.ds(at, rows), pl.ds(side * width, width)]
            copies.append(pltpu.make_async_copy(source, target, sem.at[len(copies)]))
            at += rows
    for copy in copies:
        copy.start()

    piece = mine_ref.shape[1]
    for d in range(4):
        rows = pl.ds(pl.multiple_of((quarter ^ d) * piece, 8), piece)
        shares[part, rows, :] = mine_ref[d]
        shares[1 - part, rows, :] = theirs_ref[d]

    def block(side, index):
        return shares[side, pl.ds(index * half, half), :]

    def place(row, col, value):
        x_ref[pl.ds(row * half, half), pl.ds(col * half, half)] = value
        if row != col:
            x_ref[pl.ds(col * half, half), pl.ds(row * half, half)] = value.T

    for side in range(2):
        place(2 * side, 2 * side, block(side, 0))
        place(2 * side, 2 * side + 1, block(side, 1))
        place(2 * side + 1, 2 * side + 1, block(side, 2))
        place(side, 2, block(side, 3))
        place(side, 3, block(side, 4))

    gram = x_ref[...]
    norm = jnp.sqrt(jnp.sum(gram * gram, keepdims=True))
    x_ref[...] = gram / norm

    def set_middle():
        x = x_ref[...]
        row = lax.broadcasted_iota(jnp.int32, x.shape, 0)
        col = lax.broadcasted_iota(jnp.int32, x.shape, 1)
        middle = jnp.where(row == col, 1.5, 0.0) - 0.5 * x
        high, low = split(middle)
        stack[0:size, :] = high
        stack[size : 2 * size, :] = low
        stack[2 * size :, :] = high
        return middle

    def step_x():
        m_ref[...] = product3(x_ref[...], stack[...])
        x_ref[...] = product3(m_ref[...], stack[...])

    z_ref[...] = set_middle()
    step_x()

    def sweep(index, carry):
        set_middle()
        z_ref[...] = product3(z_ref[...], stack[...])
        step_x()
        return carry

    lax.fori_loop(1, ITERS - 1, sweep, 0)
    set_middle()
    z_ref[...] = product3(z_ref[...], stack[...])

    own = pl.ds(pl.multiple_of(part * width, width), width)
    other = pl.ds(pl.multiple_of((1 - part) * width, width), width)
    rotation = jnp.concatenate([z_ref[own, own], z_ref[other, own]], axis=0).astype(BF16)
    factor = jnp.sqrt(total_rows / norm)
    for copy in copies:
        copy.wait()
    count = wide.shape[0] // chunk
    outs = []
    for i in range(count):
        rows = pl.ds(i * chunk, chunk)
        result[rows, :] = (dot(wide[rows, :], rotation) * factor).astype(BF16)
        outs.append(pltpu.make_async_copy(result.at[rows], out_ref.at[rows], out_sem.at[i]))
        outs[-1].start()
    for out in outs:
        out.wait()


def rotate(place, mine, theirs, owns, others, total_rows):
    width = owns[0].shape[1]
    rows = sum(own.shape[0] for own in owns)
    size = 2 * width
    chunk = min(rows, 512)
    body = functools.partial(finish_kernel, float(total_rows), chunk)
    vmem = pl.BlockSpec(memory_space=pltpu.VMEM)
    matrix = pltpu.VMEM((size, size), F32)
    return pl.pallas_call(
        body,
        in_specs=[SMEM, vmem, vmem] + [ANY] * 6,
        out_specs=ANY,
        out_shape=jax.ShapeDtypeStruct((rows, width), BF16),
        scratch_shapes=[
            pltpu.VMEM((2, 5 * width // 2, width // 2), F32),
            matrix, matrix, matrix,
            pltpu.VMEM((3 * size, size), BF16),
            pltpu.VMEM((rows, size), BF16),
            pltpu.VMEM((rows, width), BF16),
            pltpu.SemaphoreType.DMA((6,)),
            pltpu.SemaphoreType.DMA((rows // chunk,)),
        ],
        compiler_params=pltpu.CompilerParams(vmem_limit_bytes=VMEM_LIMIT),
        cost_estimate=pl.CostEstimate(
            flops=21 * 6 * size**3 + 2 * rows * size * width,
            bytes_accessed=3 * rows * width * 2,
            transcendentals=0,
        ),
        name="rotate",
    )(place, mine, theirs, *owns, *others)


def on_device(vectors, blocks, tile_cols, live_tiles):
    tiles, nnz, tile, _ = blocks.shape
    width = vectors.shape[1]
    edge = HALO_T
    count = lax.axis_size("patch")
    part = lax.axis_index("cols")
    patch = lax.axis_index("patch")
    listed = tile_cols - patch * tiles
    up = [(i, i + 1) for i in range(count - 1)]
    down = [(i + 1, i) for i in range(count - 1)]

    def halos(lo, hi):
        return lax.ppermute(hi, "patch", up), lax.ppermute(lo, "patch", down)

    def sibling(value):
        return lax.ppermute(value, "cols", [(0, 1), (1, 0)])

    start = vectors.reshape(tiles, tile, width)
    alive = (jnp.arange(tiles, dtype=jnp.int32) < live_tiles[0])[:, None, None]
    low = jnp.where(alive[:edge], start[:edge], jnp.zeros((), BF16))
    high = jnp.where(alive[-edge:], start[-edge:], jnp.zeros((), BF16))

    around = halos(low, high)
    mid = interior(True, listed, live_tiles, blocks, (start,), None)
    lo, hi = boundary(True, listed, live_tiles, blocks, around, (start,), None)
    prev = (start, start, start)
    for step in range(STEPS - 1):
        fields = (lo, mid, hi)
        around = halos(lo, hi)
        new_mid = interior(False, listed, live_tiles, blocks, fields, prev[1])
        if step == STEPS - 2:
            flat = new_mid.reshape(-1, width)
            other_mid = sibling(flat)
            part_arg = part.astype(jnp.int32)[None]
            inner_share = gram_share(part_arg, [flat], [other_mid], None)
        lo, hi = boundary(
            False, listed, live_tiles, blocks, around, fields, (prev[0], prev[2])
        )
        prev, mid = fields, new_mid
    lo, mid, hi = (value.reshape(-1, width) for value in (lo, mid, hi))
    other_lo, other_hi = sibling(lo), sibling(hi)
    share = gram_share(part_arg, [lo, hi], [other_lo, other_hi], inner_share)
    mine = sum_over_patch(share)
    theirs = sibling(mine)
    place = jnp.stack([part, patch % 4]).astype(jnp.int32)
    total_rows = tiles * tile * count
    return rotate(
        place, mine, theirs, [lo, mid, hi], [other_lo, other_mid, other_hi], total_rows
    )


def solution(mesh):
    in_specs = (P("patch", "cols"), P("patch", None, None, None), P("patch", None), P("patch"))
    return jax.shard_map(
        on_device, mesh=mesh, in_specs=in_specs, out_specs=P("patch", "cols"), check_vma=False
    )
```

```python
import functools

import jax
import jax.numpy as jnp
from jax import lax
from jax.experimental import pallas as pl
from jax.experimental.pallas import tpu as pltpu
from jax.sharding import PartitionSpec as P

HALO_T = 4
STEPS = 3
ITERS = 8
GROUP = 4

SMALL = pl.CostEstimate(flops=1000, bytes_accessed=1000, transcendentals=0)
ANY = pl.BlockSpec(memory_space=pl.ANY)
SMEM = pl.BlockSpec(memory_space=pltpu.SMEM)
F32, BF16 = jnp.float32, jnp.bfloat16


def dot(a, b):
    return jnp.dot(a, b, preferred_element_type=F32)


def tile_row(blocks, listed, field):
    wide = jnp.concatenate([blocks(n) for n in range(len(listed))], axis=1)
    tall = jnp.concatenate([field(tile) for tile in listed], axis=0)
    return dot(wide, tall)


def finish(acc, prev, alive):
    value = acc if prev is None else 2.0 * acc - prev.astype(F32)
    return jnp.where(alive, value, 0.0).astype(BF16)


def rows_kernel(pieces, nnz, has_prev, cols_ref, place_ref, *refs):
    sources = refs[: len(pieces)]
    rest = list(refs[len(pieces) :])
    prev_ref = rest.pop(0) if has_prev else None
    blocks_ref, out_ref, held = rest
    for i, (source, count) in enumerate(zip(sources, pieces)):
        held[pl.ds(place_ref[2 * i + 1], count)] = source[pl.ds(place_ref[2 * i + 2], count)]
    live = place_ref[0]

    def group(index, carry):
        for r in range(GROUP):
            row = index * GROUP + r
            listed = [cols_ref[row, n] for n in range(nnz)]
            acc = tile_row(lambda n: blocks_ref[row, n], listed, lambda c: held[c])
            prev = prev_ref[row] if has_prev else None
            out_ref[row] = finish(acc, prev, row < live)
        return carry

    lax.fori_loop(0, out_ref.shape[0] // GROUP, group, 0)


def tile_rows(cols, live, blocks, window, pieces, prev, name):
    rows, nnz, tile, _ = blocks.shape
    width = pieces[0][0].shape[-1]
    numbers = [live]
    for _, begin, _, slot in pieces:
        numbers += [slot, begin]
    place = jnp.stack([jnp.asarray(number, jnp.int32) for number in numbers])
    whole = pl.BlockSpec(memory_space=pltpu.VMEM)
    args = [cols, place] + [piece[0] for piece in pieces] + ([] if prev is None else [prev])
    return pl.pallas_call(
        functools.partial(rows_kernel, [piece[2] for piece in pieces], nnz, prev is not None),
        in_specs=[SMEM, SMEM] + [whole] * (len(args) - 1),
        out_specs=whole,
        out_shape=jax.ShapeDtypeStruct((rows, tile, width), BF16),
        scratch_shapes=[pltpu.VMEM((window, tile, width), BF16)],
        compiler_params=pltpu.CompilerParams(vmem_limit_bytes=8 * 1024 * 1024),
        cost_estimate=SMALL,
        name=name,
    )(*args, blocks)


def gram_kernel(pairs, chunk, part_ref, *refs):
    fields = refs[: 2 * pairs]
    has_start = len(refs) == 2 * pairs + 4
    out_ref, square, cross = refs[-3:]
    half = square.shape[0] // 2
    square[...] = jnp.zeros(square.shape, F32)
    cross[...] = jnp.zeros(cross.shape, F32)
    is_first = part_ref[0] == 0
    across = (((0,), (0,)), ((), ()))
    for own_ref, other_ref in zip(fields[:pairs], fields[pairs:]):

        def add(index, carry):
            rows = pl.ds(pl.multiple_of(index * chunk, chunk), chunk)
            own, other = own_ref[rows, :], other_ref[rows, :]
            square[...] += lax.dot_general(own, own, across, preferred_element_type=F32)
            left = jnp.where(is_first, own[:, :half], other[:, half:])
            right = jnp.where(is_first, other, own)
            cross[...] += lax.dot_general(left, right, across, preferred_element_type=F32)
            return carry

        lax.fori_loop(0, own_ref.shape[0] // chunk, add, 0)
    blocks = [
        square[:half, :half], square[:half, half:], square[half:, half:],
        cross[:, :half], cross[:, half:],
    ]
    for i, block in enumerate(blocks):
        at = pl.ds(i * half, half)
        out_ref[at, :] = block + refs[2 * pairs][at, :] if has_start else block


def gram_share(part, owns, others, start):
    width = owns[0].shape[1]
    half = width // 2
    chunk = min(own.shape[0] for own in owns)
    body = functools.partial(gram_kernel, len(owns), chunk)
    args = [part] + list(owns) + list(others) + ([] if start is None else [start])
    return pl.pallas_call(
        body,
        in_specs=[SMEM] + [pl.BlockSpec(memory_space=pltpu.VMEM)] * (len(args) - 1),
        out_specs=pl.BlockSpec(memory_space=pltpu.VMEM),
        out_shape=jax.ShapeDtypeStruct((5 * half, half), F32),
        scratch_shapes=[pltpu.VMEM((width, width), F32), pltpu.VMEM((half, width), F32)],
        compiler_params=pltpu.CompilerParams(vmem_limit_bytes=8 * 1024 * 1024),
        cost_estimate=SMALL,
        name="gram_share",
    )(*args)


def sum_over_patch(share):
    count = lax.axis_size("patch")
    me = lax.axis_index("patch")
    ways = 4
    quarter = me % ways

    def exchange(value, distance):
        return lax.ppermute(value, "patch", [(i, i ^ distance) for i in range(count)])

    parts = share.reshape(ways, -1, share.shape[1])
    pick = lambda d: lax.dynamic_index_in_dim(parts, quarter ^ d, 0, keepdims=False)
    got = [exchange(pick(d), d) for d in range(1, ways)]
    total = (pick(0) + got[0]) + (got[1] + got[2])
    stride = ways
    while stride < count:
        got = [exchange(total, d * stride) for d in range(1, ways)]
        total = (total + got[0]) + (got[1] + got[2])
        stride *= ways
    return jnp.stack([total] + [exchange(total, d) for d in range(1, ways)])


def split(value):
    high = value.astype(BF16)
    return high, (value - high.astype(F32)).astype(BF16)


def product3(left, right_stack):
    high, low = split(left)
    return dot(jnp.concatenate([high, high, low], axis=1), right_stack)


def finish_kernel(
    total_rows, chunk, place_ref, mine_ref, theirs_ref, *refs
):
    fields, out_ref = refs[:8], refs[8]
    shares, x_ref, z_ref, m_ref, stack, wide, result, sem, out_sem = refs[9:]
    part, quarter = place_ref[0], place_ref[1]
    size = x_ref.shape[0]
    width = size // 2
    half = width // 2
    copies = []
    for i, source in enumerate(fields):
        rows = source.shape[0]
        at = pl.multiple_of(place_ref[2 + i % 4], rows // 3 if i % 4 in (1, 2) else rows)
        side = i // 4
        target = wide.at[pl.ds(at, rows), pl.ds(side * width, width)]
        copies.append(pltpu.make_async_copy(source, target, sem.at[i]))
    for copy in copies:
        copy.start()

    piece = mine_ref.shape[1]
    for d in range(4):
        rows = pl.ds(pl.multiple_of((quarter ^ d) * piece, 8), piece)
        shares[part, rows, :] = mine_ref[d]
        shares[1 - part, rows, :] = theirs_ref[d]

    def block(side, index):
        return shares[side, pl.ds(index * half, half), :]

    def place(row, col, value):
        x_ref[pl.ds(row * half, half), pl.ds(col * half, half)] = value
        if row != col:
            x_ref[pl.ds(col * half, half), pl.ds(row * half, half)] = value.T

    for side in range(2):
        place(2 * side, 2 * side, block(side, 0))
        place(2 * side, 2 * side + 1, block(side, 1))
        place(2 * side + 1, 2 * side + 1, block(side, 2))
        place(side, 2, block(side, 3))
        place(side, 3, block(side, 4))

    gram = x_ref[...]
    norm = jnp.sqrt(jnp.sum(gram * gram, keepdims=True))
    x_ref[...] = gram / norm

    def set_middle():
        x = x_ref[...]
        row = lax.broadcasted_iota(jnp.int32, x.shape, 0)
        col = lax.broadcasted_iota(jnp.int32, x.shape, 1)
        middle = jnp.where(row == col, 1.5, 0.0) - 0.5 * x
        high, low = split(middle)
        stack[0:size, :] = high
        stack[size : 2 * size, :] = low
        stack[2 * size :, :] = high
        return middle

    def step_x():
        m_ref[...] = product3(x_ref[...], stack[...])
        x_ref[...] = product3(m_ref[...], stack[...])

    z_ref[...] = set_middle()
    step_x()

    def sweep(index, carry):
        set_middle()
        z_ref[...] = product3(z_ref[...], stack[...])
        step_x()
        return carry

    lax.fori_loop(1, ITERS - 1, sweep, 0)
    set_middle()
    z_ref[...] = product3(z_ref[...], stack[...])

    own = pl.ds(pl.multiple_of(part * width, width), width)
    other = pl.ds(pl.multiple_of((1 - part) * width, width), width)
    rotation = jnp.concatenate([z_ref[own, own], z_ref[other, own]], axis=0).astype(BF16)
    factor = jnp.sqrt(total_rows / norm)
    for copy in copies:
        copy.wait()
    count = wide.shape[0] // chunk
    outs = []
    for i in range(count):
        rows = pl.ds(i * chunk, chunk)
        result[rows, :] = (dot(wide[rows, :], rotation) * factor).astype(BF16)
        outs.append(pltpu.make_async_copy(result.at[rows], out_ref.at[rows], out_sem.at[i]))
        outs[-1].start()
    for out in outs:
        out.wait()


def rotate(place, mine, theirs, owns, others, total_rows):
    width = owns[0].shape[1]
    rows = sum(own.shape[0] for own in owns)
    size = 2 * width
    chunk = min(rows, 512)
    body = functools.partial(finish_kernel, float(total_rows), chunk)
    vmem = pl.BlockSpec(memory_space=pltpu.VMEM)
    matrix = pltpu.VMEM((size, size), F32)
    return pl.pallas_call(
        body,
        in_specs=[SMEM, vmem, vmem] + [ANY] * 8,
        out_specs=ANY,
        out_shape=jax.ShapeDtypeStruct((rows, width), BF16),
        scratch_shapes=[
            pltpu.VMEM((2, 5 * width // 2, width // 2), F32),
            matrix, matrix, matrix,
            pltpu.VMEM((3 * size, size), BF16),
            pltpu.VMEM((rows, size), BF16),
            pltpu.VMEM((rows, width), BF16),
            pltpu.SemaphoreType.DMA((8,)),
            pltpu.SemaphoreType.DMA((rows // chunk,)),
        ],
        compiler_params=pltpu.CompilerParams(vmem_limit_bytes=20 * 1024 * 1024),
        cost_estimate=pl.CostEstimate(
            flops=21 * 6 * size**3 + 2 * rows * size * width,
            bytes_accessed=3 * rows * width * 2,
            transcendentals=0,
        ),
        name="rotate",
    )(place, mine, theirs, *owns, *others)


def after(value, *others):
    return lax.optimization_barrier((value, others))[0]


def on_device(vectors, blocks, tile_cols, live_tiles):
    tiles, nnz, tile, _ = blocks.shape
    width = vectors.shape[1]
    edge = HALO_T
    half = tiles // 2 - edge
    count = lax.axis_size("patch")
    part = lax.axis_index("cols")
    patch = lax.axis_index("patch")
    live = live_tiles[0]
    odd = patch % 2
    pairs = {
        "even": [(i, i ^ 1) for i in range(count)],
        "odd": [(i, ((i + 1) ^ 1) - 1) for i in range(1, count - 1)],
    }
    at_end = {"even": 1 - odd, "odd": odd}
    first_row = {name: end * (tiles - edge) for name, end in at_end.items()}
    listed = tile_cols - patch * tiles

    def exchange(name, value):
        return lax.ppermute(value, "patch", pairs[name])

    def sibling(value):
        return lax.ppermute(value, "cols", [(0, 1), (1, 0)])

    start = vectors.reshape(tiles, tile, width)
    alive = (jnp.arange(tiles, dtype=jnp.int32) < live)[:, None, None]

    def masked(begin, rows):
        part_of = lax.dynamic_slice_in_dim(start, begin, rows, 0)
        kept = lax.dynamic_slice_in_dim(alive, begin, rows, 0)
        return jnp.where(kept, part_of, jnp.zeros((), BF16))

    edge_blocks = {
        name: lax.dynamic_slice_in_dim(blocks, row, edge, 0) for name, row in first_row.items()
    }
    edge_cols = {
        name: lax.dynamic_slice_in_dim(listed, row, edge, 0) - (row - edge)
        for name, row in first_row.items()
    }
    low_blocks, high_blocks = blocks[edge : edge + half], blocks[edge + half : tiles - edge]
    low_cols = listed[edge : edge + half]
    high_cols = listed[edge + half : tiles - edge] - half

    def edge_rows(name, halo, now, low, high, prev):
        end = at_end[name]
        pieces = [
            (halo, 0, edge, 2 * edge * end),
            (now, 0, edge, edge),
            (low, 0, edge, 2 * edge + edge * end),
            (high, half - edge, edge, 3 * edge * (1 - end)),
        ]
        return tile_rows(
            edge_cols[name], live - first_row[name], edge_blocks[name], 4 * edge, pieces,
            prev, "edge_" + name,
        )

    def low_rows(even, odd_edge, low, high, prev):
        spare = half + 2 * edge
        pieces = [
            (even, 0, edge, at_end["even"] * spare),
            (odd_edge, 0, edge, at_end["odd"] * spare),
            (low, 0, half, edge),
            (high, 0, edge, edge + half),
        ]
        return tile_rows(
            low_cols, live - edge, low_blocks, spare + edge, pieces, prev, "inner_low"
        )

    def high_rows(even, odd_edge, low, high, prev):
        spare = half + 2 * edge
        last = half + edge
        pieces = [
            (even, 0, edge, spare - edge * at_end["even"]),
            (odd_edge, 0, edge, spare - edge * at_end["odd"]),
            (low, half - edge, edge, 0),
            (high, 0, half, edge),
        ]
        return tile_rows(
            high_cols, live - last, high_blocks, spare + edge, pieces, prev, "inner_high"
        )

    even = masked(first_row["even"], edge)
    even_halo = exchange("even", even)
    odd_edge = masked(first_row["odd"], edge)
    low, high = masked(edge, half), masked(edge + half, half)
    prev = (None,) * 4
    part_arg = part.astype(jnp.int32)[None]
    for step in range(STEPS):
        new_low = low_rows(even, odd_edge, low, high, prev[2])
        even_halo = after(even_halo, new_low)
        odd_halo = exchange("odd", after(odd_edge, even_halo))
        new_even = edge_rows("even", even_halo, even, low, high, prev[0])
        new_high = high_rows(even, odd_edge, low, high, prev[3])
        if step == STEPS - 1:
            flat = [value.reshape(-1, width) for value in (new_even, new_low, new_high)]
            others = [sibling(after(value, even_halo)) for value in flat[1:]]
            share = gram_share(part_arg, flat[1:], others, None)
            others.insert(0, sibling(after(flat[0], share)))
            odd_halo = after(odd_halo, new_even, new_high, share)
        else:
            odd_halo = after(odd_halo, new_even, new_high)
            next_halo = exchange("even", after(new_even, odd_halo))
        new_odd = edge_rows("odd", odd_halo, odd_edge, low, high, prev[1])
        prev = (even, odd_edge, low, high)
        even, odd_edge, low, high = new_even, new_odd, new_low, new_high
        if step < STEPS - 1:
            even_halo = next_halo
    last = odd_edge.reshape(-1, width)
    other_last = sibling(last)
    share = gram_share(part_arg, [flat[0], last], [others[0], other_last], share)
    mine = sum_over_patch(share)
    theirs = sibling(mine)
    place = jnp.stack(
        [
            part, patch % 4, first_row["even"] * tile, edge * tile * jnp.ones_like(patch),
            (edge + half) * tile * jnp.ones_like(patch), first_row["odd"] * tile,
        ]
    ).astype(jnp.int32)
    total_rows = tiles * tile * count
    return rotate(place, mine, theirs, flat + [last], others + [other_last], total_rows)


def solution(mesh):
    in_specs = (P("patch", "cols"), P("patch", None, None, None), P("patch", None), P("patch"))
    return jax.shard_map(
        on_device, mesh=mesh, in_specs=in_specs, out_specs=P("patch", "cols"), check_vma=False
    )
```

```python
import functools

import jax
import jax.numpy as jnp
from jax import lax
from jax.experimental import pallas as pl
from jax.experimental.pallas import tpu as pltpu
from jax.sharding import PartitionSpec as P

HALO_T = 4
STEPS = 3
ITERS = 8
WAYS = 4
GROUP = 4

SMALL = pl.CostEstimate(flops=1000, bytes_accessed=1000, transcendentals=0)
PART, PATCH, LIVE = range(3)
SMALL_VMEM = pltpu.CompilerParams(vmem_limit_bytes=8 * 1024 * 1024)
ANY = pl.BlockSpec(memory_space=pl.ANY)
HBM = pl.BlockSpec(memory_space=pltpu.HBM)
VMEM = pl.BlockSpec(memory_space=pltpu.VMEM)
SMEM = pl.BlockSpec(memory_space=pltpu.SMEM)
F32, BF16 = jnp.float32, jnp.bfloat16


def dot(a, b):
    return jnp.dot(a, b, preferred_element_type=F32)


def tile_row(blocks, listed, field):
    wide = jnp.concatenate([blocks(n) for n in range(len(listed))], axis=1)
    tall = jnp.concatenate([field(tile) for tile in listed], axis=0)
    return dot(wide, tall)


def finish(acc, prev, alive):
    value = acc if prev is None else 2.0 * acc - prev.astype(F32)
    return jnp.where(alive, value, 0.0).astype(BF16)


def at_end(name, info):
    odd = info[PATCH] % 2
    return 1 - odd if name == "even" else odd


def first_edge_kernel(info, whole_ref, out_ref, sem):
    edge, tiles = HALO_T, whole_ref.shape[0]
    first = at_end("even", info) * (tiles - edge)
    copy = pltpu.make_async_copy(whole_ref.at[pl.ds(first, edge)], out_ref, sem)
    copy.start()
    copy.wait()
    clear_dead(out_ref, first, info[LIVE])


def clear_dead(ref, first, live):
    def clear(index, carry):
        ref[index] = jnp.zeros(ref.shape[1:], BF16)
        return carry

    count = ref.shape[0]
    lax.fori_loop(jnp.clip(live - first, 0, count), count, clear, 0)


def prepare_kernel(info, whole_ref, blocks_ref, *refs):
    odd_ref, low_ref, high_ref = refs[:3]
    even_blocks, odd_blocks, low_blocks, high_blocks, sem = refs[3:]
    edge, tiles = HALO_T, whole_ref.shape[0]
    half = tiles // 2 - edge
    even_row = at_end("even", info) * (tiles - edge)
    odd_row = at_end("odd", info) * (tiles - edge)
    moves = [
        (whole_ref, edge, low_ref), (whole_ref, edge + half, high_ref),
        (blocks_ref, edge, low_blocks), (whole_ref, odd_row, odd_ref),
        (blocks_ref, even_row, even_blocks), (blocks_ref, edge + half, high_blocks),
        (blocks_ref, odd_row, odd_blocks),
    ]
    copies = [
        pltpu.make_async_copy(source.at[pl.ds(first, target.shape[0])], target, sem.at[i])
        for i, (source, first, target) in enumerate(moves)
    ]
    for copy in copies:
        copy.start()
    for copy in copies:
        copy.wait()
    live = info[LIVE]
    clear_dead(low_ref, edge, live)
    clear_dead(high_ref, edge + half, live)
    clear_dead(odd_ref, odd_row, live)


def first_edge(info, start):
    _, tile, width = start.shape
    return pl.pallas_call(
        first_edge_kernel,
        in_specs=[SMEM, HBM],
        out_specs=VMEM,
        out_shape=jax.ShapeDtypeStruct((HALO_T, tile, width), BF16),
        scratch_shapes=[pltpu.SemaphoreType.DMA],
        compiler_params=SMALL_VMEM,
        cost_estimate=SMALL,
        name="first_edge",
    )(info, start)


def prepare(info, start, blocks):
    tiles, tile, width = start.shape
    half = tiles // 2 - HALO_T
    counts = (HALO_T, half, half)
    block_counts = (HALO_T, HALO_T, half, half)
    shapes = [jax.ShapeDtypeStruct((count, tile, width), BF16) for count in counts]
    shapes += [
        jax.ShapeDtypeStruct((count,) + blocks.shape[1:], blocks.dtype) for count in block_counts
    ]
    return pl.pallas_call(
        prepare_kernel,
        in_specs=[SMEM, HBM, HBM],
        out_specs=[VMEM] * 7,
        out_shape=shapes,
        scratch_shapes=[pltpu.SemaphoreType.DMA((7,))],
        compiler_params=pltpu.CompilerParams(vmem_limit_bytes=16 * 1024 * 1024),
        cost_estimate=SMALL,
        name="prepare",
    )(info, start, blocks)


def layout(name, info, tiles):
    edge, half = HALO_T, tiles // 2 - HALO_T
    if name in ("even", "odd"):
        end = at_end(name, info)
        first = end * (tiles - edge)
        places = [
            (0, 2 * edge * end), (0, edge), (0, 2 * edge + edge * end),
            (half - edge, 3 * edge * (1 - end)),
        ]
        return first, first - edge, places
    spare = half + 2 * edge
    ends = at_end("even", info), at_end("odd", info)
    if name == "low":
        places = [(0, end * spare) for end in ends] + [(0, edge), (0, edge + half)]
        return edge, 0, places
    places = [(0, spare - edge * end) for end in ends] + [(half - edge, 0), (0, edge)]
    return edge + half, half, places


def rows_kernel(name, counts, tiles, info, cols_ref, *refs):
    sources = refs[:4]
    blocks_ref, out_ref, held = refs[-3:]
    prev_ref = refs[4] if len(refs) == 8 else None
    nnz = blocks_ref.shape[1]
    first, base, places = layout(name, info, tiles)
    for source, count, (begin, slot) in zip(sources, counts, places):
        held[pl.ds(slot, count)] = source[pl.ds(begin, count)]
    live = info[LIVE]
    shift = info[PATCH] * tiles + base

    def group(index, carry):
        for r in range(GROUP):
            row = index * GROUP + r
            listed = [cols_ref[first + row, n] - shift for n in range(nnz)]
            acc = tile_row(lambda n: blocks_ref[row, n], listed, lambda c: held[c])
            prev = None if prev_ref is None else prev_ref[row]
            out_ref[row] = finish(acc, prev, first + row < live)
        return carry

    lax.fori_loop(0, out_ref.shape[0] // GROUP, group, 0)


def tile_rows(name, info, cols, blocks, pieces, prev):
    rows, _, tile, _ = blocks.shape
    tiles = cols.shape[0]
    width = pieces[0].shape[-1]
    edge, half = HALO_T, tiles // 2 - HALO_T
    if name in ("even", "odd"):
        counts, window = (edge,) * 4, 4 * edge
    else:
        counts, window = (edge, edge, half, edge), half + 3 * edge
        if name == "high":
            counts = (edge, edge, edge, half)
    args = list(pieces) + ([] if prev is None else [prev]) + [blocks]
    return pl.pallas_call(
        functools.partial(rows_kernel, name, counts, tiles),
        in_specs=[SMEM, SMEM] + [VMEM] * len(args),
        out_specs=VMEM,
        out_shape=jax.ShapeDtypeStruct((rows, tile, width), BF16),
        scratch_shapes=[pltpu.VMEM((window, tile, width), BF16)],
        compiler_params=SMALL_VMEM,
        cost_estimate=SMALL,
        name="rows_" + name,
    )(info, cols, *args)


def gram_kernel(pairs, chunk, last, info, *refs):
    fields = refs[: 2 * pairs]
    start_ref = refs[2 * pairs] if last else None
    square, cross = refs[-2:]
    half = square.shape[0] // 2
    square[...] = jnp.zeros(square.shape, F32)
    cross[...] = jnp.zeros(cross.shape, F32)
    is_first = info[PART] == 0
    across = (((0,), (0,)), ((), ()))
    for own_ref, other_ref in zip(fields[:pairs], fields[pairs:]):

        def add(index, carry):
            rows = pl.ds(pl.multiple_of(index * chunk, chunk), chunk)
            own, other = own_ref[rows, :], other_ref[rows, :]
            square[...] += lax.dot_general(own, own, across, preferred_element_type=F32)
            left = jnp.where(is_first, own[:, :half], other[:, half:])
            right = jnp.where(is_first, other, own)
            cross[...] += lax.dot_general(left, right, across, preferred_element_type=F32)
            return carry

        lax.fori_loop(0, own_ref.shape[0] // chunk, add, 0)
    blocks = [
        square[:half, :half], square[:half, half:], square[half:, half:],
        cross[:, :half], cross[:, half:],
    ]
    if not last:
        for i, block in enumerate(blocks):
            refs[2 * pairs][pl.ds(i * half, half), :] = block
        return
    outs, share = refs[2 * pairs + 1 : 2 * pairs + 1 + WAYS], refs[-3]
    for i, block in enumerate(blocks):
        at = pl.ds(i * half, half)
        share[at, :] = block + start_ref[at, :]
    piece = outs[0].shape[0]
    quarter = info[PATCH] % WAYS
    for d, out in enumerate(outs):
        out[...] = share[pl.ds(pl.multiple_of((quarter ^ d) * piece, 8), piece), :]


def gram_share(info, owns, others, start):
    width = owns[0].shape[1]
    half = width // 2
    chunk = min(own.shape[0] for own in owns)
    last = start is not None
    args = list(owns) + list(others) + ([start] if last else [])
    shape = jax.ShapeDtypeStruct((5 * half, half), F32)
    piece = jax.ShapeDtypeStruct((5 * half // WAYS, half), F32)
    scratch = [pltpu.VMEM((width, width), F32), pltpu.VMEM((half, width), F32)]
    return pl.pallas_call(
        functools.partial(gram_kernel, len(owns), chunk, last),
        in_specs=[SMEM] + [VMEM] * len(args),
        out_specs=[VMEM] * WAYS if last else VMEM,
        out_shape=[piece] * WAYS if last else shape,
        scratch_shapes=([pltpu.VMEM(shape.shape, F32)] if last else []) + scratch,
        compiler_params=SMALL_VMEM,
        cost_estimate=SMALL,
        name="gram_share",
    )(info, *args)


def add_kernel(a, b, c, d, out):
    out[...] = (a[...] + b[...]) + (c[...] + d[...])


def add_four(values):
    return pl.pallas_call(
        add_kernel,
        in_specs=[VMEM] * WAYS,
        out_specs=VMEM,
        out_shape=jax.ShapeDtypeStruct(values[0].shape, F32),
        compiler_params=SMALL_VMEM,
        cost_estimate=SMALL,
        name="add_four",
    )(*values)


def sum_over_patch(parts):
    count = lax.axis_size("patch")

    def exchange(value, distance):
        return lax.ppermute(value, "patch", [(i, i ^ distance) for i in range(count)])

    total = add_four([parts[0]] + [exchange(parts[d], d) for d in range(1, WAYS)])
    stride = WAYS
    while stride < count:
        total = add_four([total] + [exchange(total, d * stride) for d in range(1, WAYS)])
        stride *= WAYS
    return [total] + [exchange(total, d) for d in range(1, WAYS)]


def split(value):
    high = value.astype(BF16)
    return high, (value - high.astype(F32)).astype(BF16)


def product3(left, right_stack):
    high, low = split(left)
    return dot(jnp.concatenate([high, high, low], axis=1), right_stack)


def finish_kernel(total_rows, chunk, info, *refs):
    mine, theirs = refs[:WAYS], refs[WAYS : 2 * WAYS]
    fields, out_ref = refs[2 * WAYS : 2 * WAYS + 8], refs[2 * WAYS + 8]
    shares, x_ref, z_ref, m_ref, stack, wide, result, sem, out_sem = refs[2 * WAYS + 9 :]
    part, quarter = info[PART], info[PATCH] % WAYS
    size = x_ref.shape[0]
    width = size // 2
    half = width // 2
    edge_size = fields[0].shape[0]
    end = wide.shape[0] - edge_size
    starts = [
        at_end("even", info) * end, edge_size, edge_size + fields[1].shape[0],
        at_end("odd", info) * end,
    ]
    copies = []
    for i, source in enumerate(fields):
        rows = pl.ds(pl.multiple_of(starts[i % 4], edge_size), source.shape[0])
        target = wide.at[rows, pl.ds(i // 4 * width, width)]
        copies.append(pltpu.make_async_copy(source, target, sem.at[i]))
    for copy in copies:
        copy.start()

    piece = mine[0].shape[0]
    for d in range(WAYS):
        rows = pl.ds(pl.multiple_of((quarter ^ d) * piece, 8), piece)
        shares[part, rows, :] = mine[d][...]
        shares[1 - part, rows, :] = theirs[d][...]

    def block(side, index):
        return shares[side, pl.ds(index * half, half), :]

    def place(row, col, value):
        x_ref[pl.ds(row * half, half), pl.ds(col * half, half)] = value
        if row != col:
            x_ref[pl.ds(col * half, half), pl.ds(row * half, half)] = value.T

    for side in range(2):
        place(2 * side, 2 * side, block(side, 0))
        place(2 * side, 2 * side + 1, block(side, 1))
        place(2 * side + 1, 2 * side + 1, block(side, 2))
        place(side, 2, block(side, 3))
        place(side, 3, block(side, 4))

    gram = x_ref[...]
    norm = jnp.sqrt(jnp.sum(gram * gram, keepdims=True))
    x_ref[...] = gram / norm

    def set_middle():
        x = x_ref[...]
        row = lax.broadcasted_iota(jnp.int32, x.shape, 0)
        col = lax.broadcasted_iota(jnp.int32, x.shape, 1)
        middle = jnp.where(row == col, 1.5, 0.0) - 0.5 * x
        high, low = split(middle)
        stack[0:size, :] = high
        stack[size : 2 * size, :] = low
        stack[2 * size :, :] = high
        return middle

    def step_x():
        m_ref[...] = product3(x_ref[...], stack[...])
        x_ref[...] = product3(m_ref[...], stack[...])

    z_ref[...] = set_middle()
    step_x()

    def sweep(index, carry):
        set_middle()
        z_ref[...] = product3(z_ref[...], stack[...])
        step_x()
        return carry

    lax.fori_loop(1, ITERS - 1, sweep, 0)
    set_middle()
    z_ref[...] = product3(z_ref[...], stack[...])

    own = pl.ds(pl.multiple_of(part * width, width), width)
    other = pl.ds(pl.multiple_of((1 - part) * width, width), width)
    rotation = jnp.concatenate([z_ref[own, own], z_ref[other, own]], axis=0).astype(BF16)
    factor = jnp.sqrt(total_rows / norm)
    for copy in copies:
        copy.wait()
    count = wide.shape[0] // chunk
    outs = []
    for i in range(count):
        rows = pl.ds(i * chunk, chunk)
        result[rows, :] = (dot(wide[rows, :], rotation) * factor).astype(BF16)
        outs.append(pltpu.make_async_copy(result.at[rows], out_ref.at[rows], out_sem.at[i]))
        outs[-1].start()
    for out in outs:
        out.wait()


def rotate(info, mine, theirs, owns, others, total_rows):
    width = owns[0].shape[1]
    rows = sum(own.shape[0] for own in owns)
    size = 2 * width
    chunk = min(rows, 512)
    body = functools.partial(finish_kernel, float(total_rows), chunk)
    matrix = pltpu.VMEM((size, size), F32)
    return pl.pallas_call(
        body,
        in_specs=[SMEM] + [VMEM] * (2 * WAYS) + [ANY] * 8,
        out_specs=ANY,
        out_shape=jax.ShapeDtypeStruct((rows, width), BF16),
        scratch_shapes=[
            pltpu.VMEM((2, 5 * width // 2, width // 2), F32),
            matrix, matrix, matrix,
            pltpu.VMEM((3 * size, size), BF16),
            pltpu.VMEM((rows, size), BF16),
            pltpu.VMEM((rows, width), BF16),
            pltpu.SemaphoreType.DMA((8,)),
            pltpu.SemaphoreType.DMA((rows // chunk,)),
        ],
        compiler_params=pltpu.CompilerParams(vmem_limit_bytes=20 * 1024 * 1024),
        cost_estimate=pl.CostEstimate(
            flops=21 * 6 * size**3 + 2 * rows * size * width,
            bytes_accessed=3 * rows * width * 2,
            transcendentals=0,
        ),
        name="rotate",
    )(info, *mine, *theirs, *owns, *others)


def after(value, *others):
    return lax.optimization_barrier((value, others))[0]


def on_device(vectors, blocks, tile_cols, live_tiles):
    tiles, _, tile, _ = blocks.shape
    width = vectors.shape[1]
    count = lax.axis_size("patch")
    pairs = {
        "even": [(i, i ^ 1) for i in range(count)],
        "odd": [(i, ((i + 1) ^ 1) - 1) for i in range(1, count - 1)],
    }

    def exchange(name, value):
        return lax.ppermute(value, "patch", pairs[name])

    def sibling(value):
        return lax.ppermute(value, "cols", [(0, 1), (1, 0)])

    start = vectors.reshape(tiles, tile, width)
    scalars = [lax.axis_index("cols"), lax.axis_index("patch"), live_tiles[0]]
    info = jnp.stack(scalars).astype(jnp.int32)

    even = first_edge(info, start)
    even_halo = exchange("even", even)
    ready = prepare(after(info, even), start, blocks)
    odd, low, high = ready[:3]
    stored = dict(zip(("even", "odd", "low", "high"), ready[3:]))
    prev = dict.fromkeys(stored)

    def rows(name, *pieces):
        return tile_rows(name, info, tile_cols, stored[name], pieces, prev[name])

    for step in range(STEPS):
        new_low = rows("low", even, odd, low, high)
        even_halo = after(even_halo, new_low)
        odd_halo = exchange("odd", after(odd, even_halo))
        new_even = rows("even", even_halo, even, low, high)
        new_high = rows("high", even, odd, low, high)
        if step == STEPS - 1:
            flat = [value.reshape(-1, width) for value in (new_even, new_low, new_high)]
            others = [sibling(after(value, even_halo)) for value in flat[1:]]
            share = gram_share(info, flat[1:], others, None)
            others.insert(0, sibling(after(flat[0], share)))
            odd_halo = after(odd_halo, new_even, new_high, share)
        else:
            odd_halo = after(odd_halo, new_even, new_high)
            even_halo = exchange("even", after(new_even, odd_halo))
        new_odd = rows("odd", odd_halo, odd, low, high)
        prev = {"even": even, "odd": odd, "low": low, "high": high}
        even, odd, low, high = new_even, new_odd, new_low, new_high
    last = odd.reshape(-1, width)
    other_last = sibling(last)
    parts = gram_share(info, [flat[0], last], [others[0], other_last], share)
    mine = sum_over_patch(parts)
    theirs = [sibling(value) for value in mine]
    total_rows = tiles * tile * count
    return rotate(info, mine, theirs, flat + [last], others + [other_last], total_rows)


def solution(mesh):
    in_specs = (P("patch", "cols"), P("patch", None, None, None), P("patch", None), P("patch"))
    return jax.shard_map(
        on_device, mesh=mesh, in_specs=in_specs, out_specs=P("patch", "cols"), check_vma=False
    )
```

```python
import functools

import jax
import jax.numpy as jnp
from jax import lax
from jax.experimental import pallas as pl
from jax.experimental.pallas import tpu as pltpu
from jax.sharding import PartitionSpec as P

HALO_T = 4
STEPS = 3
ITERS = 8
WAYS = 4
GROUP = 4

SMALL = pl.CostEstimate(flops=1000, bytes_accessed=1000, transcendentals=0)
PART, PATCH, LIVE = range(3)
SMALL_VMEM = pltpu.CompilerParams(vmem_limit_bytes=8 * 1024 * 1024)
ANY = pl.BlockSpec(memory_space=pl.ANY)
HBM = pl.BlockSpec(memory_space=pltpu.HBM)
VMEM = pl.BlockSpec(memory_space=pltpu.VMEM)
SMEM = pl.BlockSpec(memory_space=pltpu.SMEM)
F32, BF16 = jnp.float32, jnp.bfloat16


def dot(a, b):
    return jnp.dot(a, b, preferred_element_type=F32)


def tile_row(blocks, listed, field):
    wide = jnp.concatenate([blocks(n) for n in range(len(listed))], axis=1)
    tall = jnp.concatenate([field(tile) for tile in listed], axis=0)
    return dot(wide, tall)


def finish(acc, prev, alive):
    value = acc if prev is None else 2.0 * acc - prev.astype(F32)
    return jnp.where(alive, value, 0.0).astype(BF16)


def at_end(name, info):
    odd = info[PATCH] % 2
    return 1 - odd if name == "even" else odd


def edges_kernel(info, whole_ref, even_ref, odd_ref, sem):
    edge, tiles = HALO_T, whole_ref.shape[0]
    outs = {"even": even_ref, "odd": odd_ref}
    firsts = {name: at_end(name, info) * (tiles - edge) for name in outs}
    copies = [
        pltpu.make_async_copy(whole_ref.at[pl.ds(firsts[name], edge)], outs[name], sem.at[i])
        for i, name in enumerate(outs)
    ]
    for copy in copies:
        copy.start()
    for copy in copies:
        copy.wait()
    for name in outs:
        clear_dead(outs[name], firsts[name], info[LIVE])


def clear_dead(ref, first, live):
    def clear(index, carry):
        ref[index] = jnp.zeros(ref.shape[1:], BF16)
        return carry

    count = ref.shape[0]
    lax.fori_loop(jnp.clip(live - first, 0, count), count, clear, 0)


def prepare_kernel(info, whole_ref, blocks_ref, *refs):
    low_ref, high_ref, even_blocks, odd_blocks, low_blocks, high_blocks, sem = refs
    edge, tiles = HALO_T, whole_ref.shape[0]
    half = tiles // 2 - edge
    moves = [
        (whole_ref, edge, low_ref), (whole_ref, edge + half, high_ref),
        (blocks_ref, edge, low_blocks),
        (blocks_ref, at_end("even", info) * (tiles - edge), even_blocks),
        (blocks_ref, edge + half, high_blocks),
        (blocks_ref, at_end("odd", info) * (tiles - edge), odd_blocks),
    ]
    copies = [
        pltpu.make_async_copy(source.at[pl.ds(first, target.shape[0])], target, sem.at[i])
        for i, (source, first, target) in enumerate(moves)
    ]
    for copy in copies:
        copy.start()
    for copy in copies:
        copy.wait()
    live = info[LIVE]
    clear_dead(low_ref, edge, live)
    clear_dead(high_ref, edge + half, live)


def masked_edges(info, start):
    _, tile, width = start.shape
    return pl.pallas_call(
        edges_kernel,
        in_specs=[SMEM, HBM],
        out_specs=[VMEM] * 2,
        out_shape=[jax.ShapeDtypeStruct((HALO_T, tile, width), BF16)] * 2,
        scratch_shapes=[pltpu.SemaphoreType.DMA((2,))],
        compiler_params=pltpu.CompilerParams(vmem_limit_bytes=4 * 1024 * 1024),
        cost_estimate=SMALL,
        name="masked_edges",
    )(info, start)


def prepare(info, start, blocks):
    tiles, tile, width = start.shape
    half = tiles // 2 - HALO_T
    block_counts = (HALO_T, HALO_T, half, half)
    shapes = [jax.ShapeDtypeStruct((half, tile, width), BF16)] * 2
    shapes += [
        jax.ShapeDtypeStruct((count,) + blocks.shape[1:], blocks.dtype) for count in block_counts
    ]
    return pl.pallas_call(
        prepare_kernel,
        in_specs=[SMEM, HBM, HBM],
        out_specs=[VMEM] * 6,
        out_shape=shapes,
        scratch_shapes=[pltpu.SemaphoreType.DMA((6,))],
        compiler_params=pltpu.CompilerParams(vmem_limit_bytes=16 * 1024 * 1024),
        cost_estimate=SMALL,
        name="prepare",
    )(info, start, blocks)


def layout(name, info, tiles):
    edge, half = HALO_T, tiles // 2 - HALO_T
    if name in ("even", "odd"):
        end = at_end(name, info)
        first = end * (tiles - edge)
        places = [
            (0, 2 * edge * end), (0, edge), (0, 2 * edge + edge * end),
            (half - edge, 3 * edge * (1 - end)),
        ]
        return first, first - edge, places
    spare = half + 2 * edge
    ends = at_end("even", info), at_end("odd", info)
    if name == "low":
        places = [(0, end * spare) for end in ends] + [(0, edge), (0, edge + half)]
        return edge, 0, places
    places = [(0, spare - edge * end) for end in ends] + [(half - edge, 0), (0, edge)]
    return edge + half, half, places


def rows_kernel(name, counts, tiles, info, cols_ref, *refs):
    sources = refs[:4]
    blocks_ref, out_ref, held = refs[-3:]
    prev_ref = refs[4] if len(refs) == 8 else None
    nnz = blocks_ref.shape[1]
    first, base, places = layout(name, info, tiles)
    for source, count, (begin, slot) in zip(sources, counts, places):
        held[pl.ds(slot, count)] = source[pl.ds(begin, count)]
    live = info[LIVE]
    shift = info[PATCH] * tiles + base

    def group(index, carry):
        for r in range(GROUP):
            row = index * GROUP + r
            listed = [cols_ref[(first + row) * nnz + n] - shift for n in range(nnz)]
            acc = tile_row(lambda n: blocks_ref[row, n], listed, lambda c: held[c])
            prev = None if prev_ref is None else prev_ref[row]
            out_ref[row] = finish(acc, prev, first + row < live)
        return carry

    lax.fori_loop(0, out_ref.shape[0] // GROUP, group, 0)


def tile_rows(name, info, cols, blocks, pieces, prev):
    rows, nnz, tile, _ = blocks.shape
    tiles = cols.shape[0] // nnz
    width = pieces[0].shape[-1]
    edge, half = HALO_T, tiles // 2 - HALO_T
    if name in ("even", "odd"):
        counts, window = (edge,) * 4, 4 * edge
    else:
        counts, window = (edge, edge, half, edge), half + 3 * edge
        if name == "high":
            counts = (edge, edge, edge, half)
    args = list(pieces) + ([] if prev is None else [prev]) + [blocks]
    return pl.pallas_call(
        functools.partial(rows_kernel, name, counts, tiles),
        in_specs=[SMEM, SMEM] + [VMEM] * len(args),
        out_specs=VMEM,
        out_shape=jax.ShapeDtypeStruct((rows, tile, width), BF16),
        scratch_shapes=[pltpu.VMEM((window, tile, width), BF16)],
        compiler_params=SMALL_VMEM,
        cost_estimate=SMALL,
        name="rows_" + name,
    )(info, cols, *args)


def gram_kernel(pairs, chunk, last, info, *refs):
    fields = refs[: 2 * pairs]
    start_ref = refs[2 * pairs] if last else None
    square, cross = refs[-2:]
    half = square.shape[0] // 2
    square[...] = jnp.zeros(square.shape, F32)
    cross[...] = jnp.zeros(cross.shape, F32)
    is_first = info[PART] == 0
    across = (((0,), (0,)), ((), ()))
    for own_ref, other_ref in zip(fields[:pairs], fields[pairs:]):

        def add(index, carry):
            rows = pl.ds(pl.multiple_of(index * chunk, chunk), chunk)
            own, other = own_ref[rows, :], other_ref[rows, :]
            square[...] += lax.dot_general(own, own, across, preferred_element_type=F32)
            left = jnp.where(is_first, own[:, :half], other[:, half:])
            right = jnp.where(is_first, other, own)
            cross[...] += lax.dot_general(left, right, across, preferred_element_type=F32)
            return carry

        lax.fori_loop(0, own_ref.shape[0] // chunk, add, 0)
    blocks = [
        square[:half, :half], square[:half, half:], square[half:, half:],
        cross[:, :half], cross[:, half:],
    ]
    if not last:
        for i, block in enumerate(blocks):
            refs[2 * pairs][pl.ds(i * half, half), :] = block
        return
    outs, share = refs[2 * pairs + 1 : 2 * pairs + 1 + WAYS], refs[-3]
    for i, block in enumerate(blocks):
        at = pl.ds(i * half, half)
        share[at, :] = block + start_ref[at, :]
    piece = outs[0].shape[0]
    quarter = info[PATCH] % WAYS
    for d, out in enumerate(outs):
        out[...] = share[pl.ds(pl.multiple_of((quarter ^ d) * piece, 8), piece), :]


def gram_share(info, owns, others, start):
    width = owns[0].shape[1]
    half = width // 2
    chunk = min(own.shape[0] for own in owns)
    last = start is not None
    args = list(owns) + list(others) + ([start] if last else [])
    shape = jax.ShapeDtypeStruct((5 * half, half), F32)
    piece = jax.ShapeDtypeStruct((5 * half // WAYS, half), F32)
    scratch = [pltpu.VMEM((width, width), F32), pltpu.VMEM((half, width), F32)]
    return pl.pallas_call(
        functools.partial(gram_kernel, len(owns), chunk, last),
        in_specs=[SMEM] + [VMEM] * len(args),
        out_specs=[VMEM] * WAYS if last else VMEM,
        out_shape=[piece] * WAYS if last else shape,
        scratch_shapes=([pltpu.VMEM(shape.shape, F32)] if last else []) + scratch,
        compiler_params=SMALL_VMEM,
        cost_estimate=SMALL,
        name="gram_share",
    )(info, *args)


def add_kernel(a, b, c, d, out):
    out[...] = (a[...] + b[...]) + (c[...] + d[...])


def add_four(values):
    return pl.pallas_call(
        add_kernel,
        in_specs=[VMEM] * WAYS,
        out_specs=VMEM,
        out_shape=jax.ShapeDtypeStruct(values[0].shape, F32),
        compiler_params=SMALL_VMEM,
        cost_estimate=SMALL,
        name="add_four",
    )(*values)


def sum_over_patch(parts):
    count = lax.axis_size("patch")

    def exchange(value, distance):
        return lax.ppermute(value, "patch", [(i, i ^ distance) for i in range(count)])

    total = add_four([parts[0]] + [exchange(parts[d], d) for d in range(1, WAYS)])
    stride = WAYS
    while stride < count:
        total = add_four([total] + [exchange(total, d * stride) for d in range(1, WAYS)])
        stride *= WAYS
    return [total] + [exchange(total, d) for d in range(1, WAYS)]


def split(value):
    high = value.astype(BF16)
    return high, (value - high.astype(F32)).astype(BF16)


def put_left(ref, row, col, value):
    size, width = ref.shape[0], value.shape[0]
    high, low = split(value)
    for i, piece in enumerate((high, high, low)):
        ref[pl.ds(row * width, width), pl.ds(i * size + col * width, width)] = piece


def put_right(ref, row, col, value):
    size, width = ref.shape[1], value.shape[0]
    high, low = split(value)
    for i, piece in enumerate((high, low, high)):
        ref[pl.ds(i * size + row * width, width), pl.ds(col * width, width)] = piece


def put_symmetric(put, ref, blocks):
    first, across, second = blocks
    put(ref, 0, 0, first)
    put(ref, 0, 1, across)
    put(ref, 1, 0, across.T)
    put(ref, 1, 1, second)


def product(left_ref, right_ref):
    width = left_ref.shape[0] // 2
    second = dot(left_ref[...], right_ref[:, width:])
    first = dot(left_ref[:width, :], right_ref[:, :width])
    return first, second[:width], second[width:]


def middle(blocks):
    first, across, second = blocks
    row = lax.broadcasted_iota(jnp.int32, first.shape, 0)
    col = lax.broadcasted_iota(jnp.int32, first.shape, 1)
    diagonal = jnp.where(row == col, 1.5, 0.0)
    return diagonal - 0.5 * first, -0.5 * across, diagonal - 0.5 * second


def finish_kernel(total_rows, chunk, info, *refs):
    mine, theirs = refs[:WAYS], refs[WAYS : 2 * WAYS]
    fields, out_ref = refs[2 * WAYS : 2 * WAYS + 8], refs[2 * WAYS + 8]
    shares, x_ref, x_left, w_left, z_left, m_right, wide, result, sem, out_sem = refs[
        2 * WAYS + 9 :
    ]
    part, quarter = info[PART], info[PATCH] % WAYS
    size = x_ref.shape[0]
    width = size // 2
    half = width // 2
    edge_size = fields[0].shape[0]
    end = wide.shape[0] - edge_size
    starts = [
        at_end("even", info) * end, edge_size, edge_size + fields[1].shape[0],
        at_end("odd", info) * end,
    ]
    copies = []
    for i, source in enumerate(fields):
        rows = pl.ds(pl.multiple_of(starts[i % 4], edge_size), source.shape[0])
        side = part if i < 4 else 1 - part
        target = wide.at[rows, pl.ds(pl.multiple_of(side * width, width), width)]
        copies.append(pltpu.make_async_copy(source, target, sem.at[i]))
    for copy in copies:
        copy.start()

    piece = mine[0].shape[0]
    for d in range(WAYS):
        rows = pl.ds(pl.multiple_of((quarter ^ d) * piece, 8), piece)
        shares[part, rows, :] = mine[d][...]
        shares[1 - part, rows, :] = theirs[d][...]

    def block(side, index):
        return shares[side, pl.ds(index * half, half), :]

    def place(row, col, value):
        x_ref[pl.ds(row * half, half), pl.ds(col * half, half)] = value

    for side in range(2):
        across = block(side, 1)
        place(2 * side, 2 * side, block(side, 0))
        place(2 * side, 2 * side + 1, across)
        place(2 * side + 1, 2 * side, across.T)
        place(2 * side + 1, 2 * side + 1, block(side, 2))
        place(side, 2, block(side, 3))
        place(side, 3, block(side, 4))

    gram = x_ref[:width, :width], x_ref[:width, width:], x_ref[width:, width:]
    squares = gram[0] * gram[0] + 2.0 * (gram[1] * gram[1]) + gram[2] * gram[2]
    norm = jnp.sqrt(jnp.sum(squares, keepdims=True))
    x = tuple(value / norm for value in gram)
    put_symmetric(put_left, x_left, x)
    factors = middle(x)
    put_symmetric(put_right, m_right, factors)
    put_symmetric(put_left, z_left, factors)

    def advance(first):
        put_symmetric(put_left, w_left, product(x_left, m_right))
        if not first:
            put_symmetric(put_left, z_left, product(z_left, m_right))
        x = product(w_left, m_right)
        put_symmetric(put_left, x_left, x)
        put_symmetric(put_right, m_right, middle(x))

    advance(True)

    def sweep(index, carry):
        advance(False)
        return carry

    lax.fori_loop(1, ITERS - 1, sweep, 0)
    own = pl.ds(pl.multiple_of(part * width, width), width)
    rotation = dot(z_left[...], m_right[:, own]).astype(BF16)
    factor = jnp.sqrt(total_rows / norm)
    for copy in copies:
        copy.wait()
    count = wide.shape[0] // chunk
    outs = []
    for i in range(count):
        rows = pl.ds(i * chunk, chunk)
        result[rows, :] = (dot(wide[rows, :], rotation) * factor).astype(BF16)
        outs.append(pltpu.make_async_copy(result.at[rows], out_ref.at[rows], out_sem.at[i]))
        outs[-1].start()
    for out in outs:
        out.wait()


def rotate(info, mine, theirs, owns, others, total_rows):
    width = owns[0].shape[1]
    rows = sum(own.shape[0] for own in owns)
    size = 2 * width
    chunk = min(rows, 512)
    body = functools.partial(finish_kernel, float(total_rows), chunk)
    left = pltpu.VMEM((size, 3 * size), BF16)
    return pl.pallas_call(
        body,
        in_specs=[SMEM] + [VMEM] * (2 * WAYS) + [ANY] * 8,
        out_specs=ANY,
        out_shape=jax.ShapeDtypeStruct((rows, width), BF16),
        scratch_shapes=[
            pltpu.VMEM((2, 5 * width // 2, width // 2), F32),
            pltpu.VMEM((size, size), F32),
            left, left, left,
            pltpu.VMEM((3 * size, size), BF16),
            pltpu.VMEM((rows, size), BF16),
            pltpu.VMEM((rows, width), BF16),
            pltpu.SemaphoreType.DMA((8,)),
            pltpu.SemaphoreType.DMA((rows // chunk,)),
        ],
        compiler_params=pltpu.CompilerParams(vmem_limit_bytes=20 * 1024 * 1024),
        cost_estimate=pl.CostEstimate(
            flops=21 * 6 * size**3 + 2 * rows * size * width,
            bytes_accessed=3 * rows * width * 2,
            transcendentals=0,
        ),
        name="rotate",
    )(info, *mine, *theirs, *owns, *others)


def after(value, *others):
    return lax.optimization_barrier((value, others))[0]


def on_device(vectors, blocks, tile_cols, live_tiles):
    tiles, _, tile, _ = blocks.shape
    width = vectors.shape[1]
    count = lax.axis_size("patch")
    pairs = {
        "even": [(i, i ^ 1) for i in range(count)],
        "odd": [(i, ((i + 1) ^ 1) - 1) for i in range(1, count - 1)],
    }

    def exchange(name, value):
        return lax.ppermute(value, "patch", pairs[name])

    def sibling(value):
        return lax.ppermute(value, "cols", [(0, 1), (1, 0)])

    start = vectors.reshape(tiles, tile, width)
    scalars = [lax.axis_index("cols"), lax.axis_index("patch"), live_tiles[0]]
    info = jnp.stack(scalars).astype(jnp.int32)

    cols = tile_cols.reshape(-1)

    even, odd = masked_edges(after(info, cols), start)
    even_halo, odd_halo = exchange("even", even), exchange("odd", odd)
    ready = prepare(after(info, even), start, blocks)
    low, high = ready[:2]
    stored = dict(zip(("even", "odd", "low", "high"), ready[2:]))
    prev = dict.fromkeys(stored)

    def rows(name, *pieces):
        return tile_rows(name, info, cols, stored[name], pieces, prev[name])

    for step in range(STEPS):
        final = step == STEPS - 1
        new_low = rows("low", even, odd, low, high)
        even_halo = after(even_halo, new_low)
        new_even = rows("even", even_halo, even, low, high)
        if not final:
            even_halo = exchange("even", new_even)
        new_high = rows("high", even, odd, low, high)
        if final:
            flat = [value.reshape(-1, width) for value in (new_even, new_low, new_high)]
            others = [sibling(after(value, new_even)) for value in flat]
            share = gram_share(info, flat, others, None)
            odd_halo = after(odd_halo, share)
        else:
            odd_halo = after(odd_halo, new_even, new_high)
        new_odd = rows("odd", odd_halo, odd, low, high)
        if not final:
            odd_halo = exchange("odd", new_odd)
        prev = {"even": even, "odd": odd, "low": low, "high": high}
        even, odd, low, high = new_even, new_odd, new_low, new_high
    last = odd.reshape(-1, width)
    other_last = sibling(last)
    parts = gram_share(info, [last], [other_last], share)
    mine = sum_over_patch(parts)
    theirs = [sibling(value) for value in mine]
    total_rows = tiles * tile * count
    return rotate(info, mine, theirs, flat + [last], others + [other_last], total_rows)


def solution(mesh):
    in_specs = (P("patch", "cols"), P("patch", None, None, None), P("patch", None), P("patch"))
    return jax.shard_map(
        on_device, mesh=mesh, in_specs=in_specs, out_specs=P("patch", "cols"), check_vma=False
    )
```

```python
import functools

import jax
import jax.numpy as jnp
from jax import lax
from jax.experimental import pallas as pl
from jax.experimental.pallas import tpu as pltpu
from jax.sharding import PartitionSpec as P

HALO_T = 4
STEPS = 3
ITERS = 8
WAYS = 4
GROUP = 4

SMALL = pl.CostEstimate(flops=1000, bytes_accessed=1000, transcendentals=0)
LARGE = pl.CostEstimate(flops=10**11, bytes_accessed=1000, transcendentals=0)
PART, PATCH, LIVE = range(3)
SMALL_VMEM = pltpu.CompilerParams(vmem_limit_bytes=8 * 1024 * 1024)
ANY = pl.BlockSpec(memory_space=pl.ANY)
HBM = pl.BlockSpec(memory_space=pltpu.HBM)
VMEM = pl.BlockSpec(memory_space=pltpu.VMEM)
SMEM = pl.BlockSpec(memory_space=pltpu.SMEM)
F32, BF16 = jnp.float32, jnp.bfloat16


def dot(a, b):
    return jnp.dot(a, b, preferred_element_type=F32)


def tile_row(blocks, listed, field):
    wide = jnp.concatenate([blocks(n) for n in range(len(listed))], axis=1)
    tall = jnp.concatenate([field(tile) for tile in listed], axis=0)
    return dot(wide, tall)


def finish(acc, prev, alive):
    value = acc if prev is None else 2.0 * acc - prev.astype(F32)
    return jnp.where(alive, value, 0.0).astype(BF16)


def at_end(name, info):
    odd = info[PATCH] % 2
    return 1 - odd if name == "even" else odd


def edges_kernel(info, whole_ref, even_ref, odd_ref, sem):
    edge, tiles = HALO_T, whole_ref.shape[0]
    outs = {"even": even_ref, "odd": odd_ref}
    firsts = {name: at_end(name, info) * (tiles - edge) for name in outs}
    copies = [
        pltpu.make_async_copy(whole_ref.at[pl.ds(firsts[name], edge)], outs[name], sem.at[i])
        for i, name in enumerate(outs)
    ]
    for copy in copies:
        copy.start()
    for copy in copies:
        copy.wait()
    for name in outs:
        clear_dead(outs[name], firsts[name], info[LIVE])


def clear_dead(ref, first, live):
    def clear(index, carry):
        ref[index] = jnp.zeros(ref.shape[1:], BF16)
        return carry

    count = ref.shape[0]
    lax.fori_loop(jnp.clip(live - first, 0, count), count, clear, 0)


def prepare_kernel(info, whole_ref, blocks_ref, *refs):
    low_ref, high_ref, even_blocks, odd_blocks, low_blocks, high_blocks, sem = refs
    edge, tiles = HALO_T, whole_ref.shape[0]
    half = tiles // 2 - edge
    moves = [
        (whole_ref, edge, low_ref), (whole_ref, edge + half, high_ref),
        (blocks_ref, edge, low_blocks),
        (blocks_ref, at_end("even", info) * (tiles - edge), even_blocks),
        (blocks_ref, edge + half, high_blocks),
        (blocks_ref, at_end("odd", info) * (tiles - edge), odd_blocks),
    ]
    copies = [
        pltpu.make_async_copy(source.at[pl.ds(first, target.shape[0])], target, sem.at[i])
        for i, (source, first, target) in enumerate(moves)
    ]
    for copy in copies:
        copy.start()
    for copy in copies:
        copy.wait()
    live = info[LIVE]
    clear_dead(low_ref, edge, live)
    clear_dead(high_ref, edge + half, live)


def masked_edges(info, start):
    _, tile, width = start.shape
    return pl.pallas_call(
        edges_kernel,
        in_specs=[SMEM, HBM],
        out_specs=[VMEM] * 2,
        out_shape=[jax.ShapeDtypeStruct((HALO_T, tile, width), BF16)] * 2,
        scratch_shapes=[pltpu.SemaphoreType.DMA((2,))],
        compiler_params=pltpu.CompilerParams(vmem_limit_bytes=4 * 1024 * 1024),
        cost_estimate=SMALL,
        name="masked_edges",
    )(info, start)


def prepare(info, start, blocks):
    tiles, tile, width = start.shape
    half = tiles // 2 - HALO_T
    block_counts = (HALO_T, HALO_T, half, half)
    shapes = [jax.ShapeDtypeStruct((half, tile, width), BF16)] * 2
    shapes += [
        jax.ShapeDtypeStruct((count,) + blocks.shape[1:], blocks.dtype) for count in block_counts
    ]
    return pl.pallas_call(
        prepare_kernel,
        in_specs=[SMEM, HBM, HBM],
        out_specs=[VMEM] * 6,
        out_shape=shapes,
        scratch_shapes=[pltpu.SemaphoreType.DMA((6,))],
        compiler_params=pltpu.CompilerParams(vmem_limit_bytes=16 * 1024 * 1024),
        cost_estimate=SMALL,
        name="prepare",
    )(info, start, blocks)


def layout(name, info, tiles):
    edge, half = HALO_T, tiles // 2 - HALO_T
    if name in ("even", "odd"):
        end = at_end(name, info)
        first = end * (tiles - edge)
        places = [
            (0, 2 * edge * end), (0, edge), (0, 2 * edge + edge * end),
            (half - edge, 3 * edge * (1 - end)),
        ]
        return first, first - edge, places
    spare = half + 2 * edge
    ends = at_end("even", info), at_end("odd", info)
    if name == "low":
        places = [(0, end * spare) for end in ends] + [(0, edge), (0, edge + half)]
        return edge, 0, places
    places = [(0, spare - edge * end) for end in ends] + [(half - edge, 0), (0, edge)]
    return edge + half, half, places


def rows_kernel(name, counts, tiles, info, cols_ref, *refs):
    sources = refs[:4]
    blocks_ref, out_ref, held = refs[-3:]
    prev_ref = refs[4] if len(refs) == 8 else None
    nnz = blocks_ref.shape[1]
    first, base, places = layout(name, info, tiles)
    for source, count, (begin, slot) in zip(sources, counts, places):
        held[pl.ds(slot, count)] = source[pl.ds(begin, count)]
    live = info[LIVE]
    shift = info[PATCH] * tiles + base

    def group(index, carry):
        for r in range(GROUP):
            row = index * GROUP + r
            listed = [cols_ref[(first + row) * nnz + n] - shift for n in range(nnz)]
            acc = tile_row(lambda n: blocks_ref[row, n], listed, lambda c: held[c])
            prev = None if prev_ref is None else prev_ref[row]
            out_ref[row] = finish(acc, prev, first + row < live)
        return carry

    lax.fori_loop(0, out_ref.shape[0] // GROUP, group, 0)


def tile_rows(name, info, cols, blocks, pieces, prev, cost):
    rows, nnz, tile, _ = blocks.shape
    tiles = cols.shape[0] // nnz
    width = pieces[0].shape[-1]
    edge, half = HALO_T, tiles // 2 - HALO_T
    if name in ("even", "odd"):
        counts, window = (edge,) * 4, 4 * edge
    else:
        counts, window = (edge, edge, half, edge), half + 3 * edge
        if name == "high":
            counts = (edge, edge, edge, half)
    args = list(pieces) + ([] if prev is None else [prev]) + [blocks]
    return pl.pallas_call(
        functools.partial(rows_kernel, name, counts, tiles),
        in_specs=[SMEM, SMEM] + [VMEM] * len(args),
        out_specs=VMEM,
        out_shape=jax.ShapeDtypeStruct((rows, tile, width), BF16),
        scratch_shapes=[pltpu.VMEM((window, tile, width), BF16)],
        compiler_params=SMALL_VMEM,
        cost_estimate=cost,
        name="rows_" + name,
    )(info, cols, *args)


def gram_kernel(pairs, chunk, last, info, *refs):
    fields = refs[: 2 * pairs]
    start_ref = refs[2 * pairs] if last else None
    square, cross = refs[-2:]
    half = square.shape[0] // 2
    square[...] = jnp.zeros(square.shape, F32)
    cross[...] = jnp.zeros(cross.shape, F32)
    is_first = info[PART] == 0
    across = (((0,), (0,)), ((), ()))
    for own_ref, other_ref in zip(fields[:pairs], fields[pairs:]):

        def add(index, carry):
            rows = pl.ds(pl.multiple_of(index * chunk, chunk), chunk)
            own, other = own_ref[rows, :], other_ref[rows, :]
            square[...] += lax.dot_general(own, own, across, preferred_element_type=F32)
            left = jnp.where(is_first, own[:, :half], other[:, half:])
            right = jnp.where(is_first, other, own)
            cross[...] += lax.dot_general(left, right, across, preferred_element_type=F32)
            return carry

        lax.fori_loop(0, own_ref.shape[0] // chunk, add, 0)
    blocks = [
        square[:half, :half], square[:half, half:], square[half:, half:],
        cross[:, :half], cross[:, half:],
    ]
    if not last:
        for i, block in enumerate(blocks):
            refs[2 * pairs][pl.ds(i * half, half), :] = block
        return
    outs, share = refs[2 * pairs + 1 : 2 * pairs + 1 + WAYS], refs[-3]
    for i, block in enumerate(blocks):
        at = pl.ds(i * half, half)
        share[at, :] = block + start_ref[at, :]
    piece = outs[0].shape[0]
    quarter = info[PATCH] % WAYS
    for d, out in enumerate(outs):
        out[...] = share[pl.ds(pl.multiple_of((quarter ^ d) * piece, 8), piece), :]


def gram_share(info, owns, others, start):
    width = owns[0].shape[1]
    half = width // 2
    chunk = min(own.shape[0] for own in owns)
    last = start is not None
    args = list(owns) + list(others) + ([start] if last else [])
    shape = jax.ShapeDtypeStruct((5 * half, half), F32)
    piece = jax.ShapeDtypeStruct((5 * half // WAYS, half), F32)
    scratch = [pltpu.VMEM((width, width), F32), pltpu.VMEM((half, width), F32)]
    return pl.pallas_call(
        functools.partial(gram_kernel, len(owns), chunk, last),
        in_specs=[SMEM] + [VMEM] * len(args),
        out_specs=[VMEM] * WAYS if last else VMEM,
        out_shape=[piece] * WAYS if last else shape,
        scratch_shapes=([pltpu.VMEM(shape.shape, F32)] if last else []) + scratch,
        compiler_params=SMALL_VMEM,
        cost_estimate=SMALL,
        name="gram_share",
    )(info, *args)


def add_kernel(a, b, c, d, out):
    out[...] = (a[...] + b[...]) + (c[...] + d[...])


def add_four(values):
    return pl.pallas_call(
        add_kernel,
        in_specs=[VMEM] * WAYS,
        out_specs=VMEM,
        out_shape=jax.ShapeDtypeStruct(values[0].shape, F32),
        compiler_params=SMALL_VMEM,
        cost_estimate=SMALL,
        name="add_four",
    )(*values)


def sum_over_patch(parts):
    count = lax.axis_size("patch")

    def exchange(value, distance):
        return lax.ppermute(value, "patch", [(i, i ^ distance) for i in range(count)])

    total = add_four([parts[0]] + [exchange(parts[d], d) for d in range(1, WAYS)])
    stride = WAYS
    while stride < count:
        total = add_four([total] + [exchange(total, d * stride) for d in range(1, WAYS)])
        stride *= WAYS
    return [total] + [exchange(total, d) for d in range(1, WAYS)]


def split(value):
    high = value.astype(BF16)
    return high, (value - high.astype(F32)).astype(BF16)


def put_row(ref, size, col, value):
    width = value.shape[0]
    high, low = split(value)
    for i, piece in enumerate((high, high, low)):
        ref[:, pl.ds(i * size + col * width, width)] = piece


def put_col(ref, size, row, col, value):
    width = value.shape[0]
    high, low = split(value)
    for i, piece in enumerate((high, low, high)):
        ref[pl.ds(i * size + row * width, width), pl.ds(col * width, width)] = piece


def put_left(refs, blocks):
    row_ref, col_ref = refs
    size = 2 * blocks[0].shape[0]
    put_row(row_ref, size, 0, blocks[0])
    put_row(row_ref, size, 1, blocks[1])
    put_col(col_ref, size, 0, 0, blocks[1])
    put_col(col_ref, size, 1, 0, blocks[2])


def put_right(refs, blocks):
    last_ref, all_ref = refs
    size = 2 * blocks[0].shape[0]
    across = blocks[1].T
    put_col(all_ref, size, 0, 0, blocks[0])
    put_col(all_ref, size, 0, 1, blocks[1])
    put_col(all_ref, size, 1, 0, across)
    put_col(all_ref, size, 1, 1, blocks[2])
    put_row(last_ref, size, 0, across)
    put_row(last_ref, size, 1, blocks[2])


def times_middle(blocks, left, right):
    width = blocks[0].shape[0]
    first = dot(left[0][...], right[1][...])
    second = dot(right[0][...], left[1][...])
    parts = first[:, :width], first[:, width:], second
    return tuple(1.5 * block - 0.5 * part for block, part in zip(blocks, parts))


def middle(blocks):
    first, across, second = blocks
    row = lax.broadcasted_iota(jnp.int32, first.shape, 0)
    col = lax.broadcasted_iota(jnp.int32, first.shape, 1)
    diagonal = jnp.where(row == col, 1.5, 0.0)
    return diagonal - 0.5 * first, -0.5 * across, diagonal - 0.5 * second


def finish_kernel(total_rows, chunk, info, *refs):
    mine, theirs = refs[:WAYS], refs[WAYS : 2 * WAYS]
    fields, out_ref = refs[2 * WAYS : 2 * WAYS + 8], refs[2 * WAYS + 8]
    shares, x_ref, x_held, w_held, z_held, *rest = refs[2 * WAYS + 9 :]
    x_left, w_left, z_left, x_right = rest[0:2], rest[2:4], rest[4:6], (rest[6:8], rest[8:10])
    wide, result, sem, out_sem = rest[10:]
    part, quarter = info[PART], info[PATCH] % WAYS
    size = x_ref.shape[0]
    width = size // 2
    half = width // 2
    edge_size = fields[0].shape[0]
    end = wide.shape[0] - edge_size
    starts = [
        at_end("even", info) * end, edge_size, edge_size + fields[1].shape[0],
        at_end("odd", info) * end,
    ]
    copies = []
    for i, source in enumerate(fields):
        rows = pl.ds(pl.multiple_of(starts[i % 4], edge_size), source.shape[0])
        side = part if i < 4 else 1 - part
        target = wide.at[rows, pl.ds(pl.multiple_of(side * width, width), width)]
        copies.append(pltpu.make_async_copy(source, target, sem.at[i]))
    for copy in copies:
        copy.start()

    piece = mine[0].shape[0]
    for d in range(WAYS):
        rows = pl.ds(pl.multiple_of((quarter ^ d) * piece, 8), piece)
        shares[part, rows, :] = mine[d][...]
        shares[1 - part, rows, :] = theirs[d][...]

    def block(side, index):
        return shares[side, pl.ds(index * half, half), :]

    def place(row, col, value):
        x_ref[pl.ds(row * half, half), pl.ds(col * half, half)] = value

    for side in range(2):
        across = block(side, 1)
        place(2 * side, 2 * side, block(side, 0))
        place(2 * side, 2 * side + 1, across)
        place(2 * side + 1, 2 * side, across.T)
        place(2 * side + 1, 2 * side + 1, block(side, 2))
        place(side, 2, block(side, 3))
        place(side, 3, block(side, 4))

    gram = x_ref[:width, :width], x_ref[:width, width:], x_ref[width:, width:]
    squares = gram[0] * gram[0] + 2.0 * (gram[1] * gram[1]) + gram[2] * gram[2]
    norm = jnp.sqrt(jnp.sum(squares, keepdims=True))
    def hold(ref, blocks):
        for i, value in enumerate(blocks):
            ref[i] = value

    def held(ref):
        return tuple(ref[i] for i in range(3))

    def set_x(x, right):
        hold(x_held, x)
        put_left(x_left, x)
        put_right(right, x)

    def advance(now, then):
        w = times_middle(held(x_held), x_left, now)
        hold(w_held, w)
        put_left(w_left, w)
        z = times_middle(held(z_held), z_left, now)
        x = times_middle(w, w_left, now)
        hold(z_held, z)
        put_left(z_left, z)
        set_x(x, then)

    x = tuple(value / norm for value in gram)
    set_x(x, x_right[0])
    z = middle(x)
    hold(z_held, z)
    put_left(z_left, z)
    w = times_middle(x, x_left, x_right[0])
    put_left(w_left, w)
    set_x(times_middle(w, w_left, x_right[0]), x_right[1])

    def sweeps(index, carry):
        advance(x_right[1], x_right[0])
        advance(x_right[0], x_right[1])
        return carry

    lax.fori_loop(0, (ITERS - 2) // 2, sweeps, 0)
    first, across, second = times_middle(held(z_held), z_left, x_right[1])
    z_ref = x_ref
    z_ref[:width, :width] = first
    z_ref[:width, width:] = across
    z_ref[width:, :width] = across.T
    z_ref[width:, width:] = second
    own = pl.ds(pl.multiple_of(part * width, width), width)
    rotation = z_ref[:, own].astype(BF16)
    factor = jnp.sqrt(total_rows / norm)
    for copy in copies:
        copy.wait()
    count = wide.shape[0] // chunk
    outs = []
    for i in range(count):
        rows = pl.ds(i * chunk, chunk)
        result[rows, :] = (dot(wide[rows, :], rotation) * factor).astype(BF16)
        outs.append(pltpu.make_async_copy(result.at[rows], out_ref.at[rows], out_sem.at[i]))
        outs[-1].start()
    for out in outs:
        out.wait()


def rotate(info, mine, theirs, owns, others, total_rows):
    width = owns[0].shape[1]
    rows = sum(own.shape[0] for own in owns)
    size = 2 * width
    chunk = min(rows, 512)
    body = functools.partial(finish_kernel, float(total_rows), chunk)
    blocks = pltpu.VMEM((3, width, width), F32)
    row_form = pltpu.VMEM((width, 3 * size), BF16)
    col_form = pltpu.VMEM((3 * size, width), BF16)
    all_form = pltpu.VMEM((3 * size, size), BF16)
    return pl.pallas_call(
        body,
        in_specs=[SMEM] + [VMEM] * (2 * WAYS) + [ANY] * 8,
        out_specs=ANY,
        out_shape=jax.ShapeDtypeStruct((rows, width), BF16),
        scratch_shapes=[
            pltpu.VMEM((2, 5 * width // 2, width // 2), F32),
            pltpu.VMEM((size, size), F32),
            blocks, blocks, blocks,
            row_form, col_form, row_form, col_form, row_form, col_form,
            row_form, all_form, row_form, all_form,
            pltpu.VMEM((rows, size), BF16),
            pltpu.VMEM((rows, width), BF16),
            pltpu.SemaphoreType.DMA((8,)),
            pltpu.SemaphoreType.DMA((rows // chunk,)),
        ],
        compiler_params=pltpu.CompilerParams(vmem_limit_bytes=28 * 1024 * 1024),
        cost_estimate=pl.CostEstimate(
            flops=21 * 6 * size**3 + 2 * rows * size * width,
            bytes_accessed=3 * rows * width * 2,
            transcendentals=0,
        ),
        name="rotate",
    )(info, *mine, *theirs, *owns, *others)


def after(value, *others):
    return lax.optimization_barrier((value, others))[0]


def on_device(vectors, blocks, tile_cols, live_tiles):
    tiles, _, tile, _ = blocks.shape
    width = vectors.shape[1]
    count = lax.axis_size("patch")
    pairs = {
        "even": [(i, i ^ 1) for i in range(count)],
        "odd": [(i, ((i + 1) ^ 1) - 1) for i in range(1, count - 1)],
    }

    def exchange(name, value):
        return lax.ppermute(value, "patch", pairs[name])

    def sibling(value):
        return lax.ppermute(value, "cols", [(0, 1), (1, 0)])

    start = vectors.reshape(tiles, tile, width)
    scalars = [lax.axis_index("cols"), lax.axis_index("patch"), live_tiles[0]]
    info = jnp.stack(scalars).astype(jnp.int32)

    cols = tile_cols.reshape(-1)

    even, odd = masked_edges(after(info, cols), start)
    even_halo = exchange("even", even)
    ready = prepare(after(info, even), start, blocks)
    low, high = ready[:2]
    stored = dict(zip(("even", "odd", "low", "high"), ready[2:]))
    odd_halo = exchange("odd", after(odd, low))
    prev = dict.fromkeys(stored)

    def rows(name, *pieces, cost=SMALL):
        return tile_rows(name, info, cols, stored[name], pieces, prev[name], cost)

    for step in range(STEPS):
        first, final = step == 0, step == STEPS - 1
        if not first:
            new_low = rows("low", even, odd, low, high)
            even_halo = after(even_halo, new_low)
        new_even = rows("even", even_halo, even, low, high)
        if not final:
            even_halo = exchange("even", new_even)
        if first:
            new_low = rows("low", after(even, new_even), odd, low, high)
        new_high = rows("high", even, odd, low, high)
        if final:
            flat = [value.reshape(-1, width) for value in (new_even, new_low, new_high)]
            others = [sibling(after(value, new_even)) for value in flat]
        odd_halo = after(odd_halo, new_even, new_low, new_high)
        new_odd = rows("odd", odd_halo, odd, low, high, cost=LARGE if final else SMALL)
        if not final:
            odd_halo = exchange("odd", new_odd)
        prev = {"even": even, "odd": odd, "low": low, "high": high}
        even, odd, low, high = new_even, new_odd, new_low, new_high
    last = odd.reshape(-1, width)
    other_last = sibling(last)
    others = [after(other, last) for other in others]
    share = gram_share(info, flat, others, None)
    parts = gram_share(info, [last], [other_last], share)
    mine = sum_over_patch(parts)
    theirs = [sibling(value) for value in mine]
    total_rows = tiles * tile * count
    return rotate(info, mine, theirs, flat + [last], others + [other_last], total_rows)


def solution(mesh):
    in_specs = (P("patch", "cols"), P("patch", None, None, None), P("patch", None), P("patch"))
    return jax.shard_map(
        on_device, mesh=mesh, in_specs=in_specs, out_specs=P("patch", "cols"), check_vma=False
    )
```

```python
import functools

import jax
import jax.numpy as jnp
from jax import lax
from jax.experimental import pallas as pl
from jax.experimental.pallas import tpu as pltpu
from jax.sharding import PartitionSpec as P

HALO_T = 4
STEPS = 3
ITERS = 8
GROUP = 4

SMALL = pl.CostEstimate(flops=1000, bytes_accessed=1000, transcendentals=0)
LARGE = pl.CostEstimate(flops=10**11, bytes_accessed=1000, transcendentals=0)
PART, PATCH, LIVE = range(3)
SMALL_VMEM = pltpu.CompilerParams(vmem_limit_bytes=8 * 1024 * 1024)
ANY = pl.BlockSpec(memory_space=pl.ANY)
HBM = pl.BlockSpec(memory_space=pltpu.HBM)
VMEM = pl.BlockSpec(memory_space=pltpu.VMEM)
SMEM = pl.BlockSpec(memory_space=pltpu.SMEM)
F32, BF16 = jnp.float32, jnp.bfloat16


def dot(a, b):
    return jnp.dot(a, b, preferred_element_type=F32)


def tile_row(blocks, listed, field):
    wide = jnp.concatenate([blocks(n) for n in range(len(listed))], axis=1)
    tall = jnp.concatenate([field(tile) for tile in listed], axis=0)
    return dot(wide, tall)


def finish(acc, prev, alive):
    value = acc if prev is None else 2.0 * acc - prev.astype(F32)
    return jnp.where(alive, value, 0.0).astype(BF16)


def at_end(name, info):
    odd = info[PATCH] % 2
    return 1 - odd if name == "even" else odd


def edges_kernel(info, whole_ref, even_ref, odd_ref, sem):
    edge, tiles = HALO_T, whole_ref.shape[0]
    outs = {"even": even_ref, "odd": odd_ref}
    firsts = {name: at_end(name, info) * (tiles - edge) for name in outs}
    copies = [
        pltpu.make_async_copy(whole_ref.at[pl.ds(firsts[name], edge)], outs[name], sem.at[i])
        for i, name in enumerate(outs)
    ]
    for copy in copies:
        copy.start()
    for copy in copies:
        copy.wait()
    for name in outs:
        clear_dead(outs[name], firsts[name], info[LIVE])


def clear_dead(ref, first, live):
    def clear(index, carry):
        ref[index] = jnp.zeros(ref.shape[1:], BF16)
        return carry

    count = ref.shape[0]
    lax.fori_loop(jnp.clip(live - first, 0, count), count, clear, 0)


def prepare_kernel(info, whole_ref, blocks_ref, *refs):
    low_ref, high_ref, even_blocks, odd_blocks, low_blocks, high_blocks, sem = refs
    edge, tiles = HALO_T, whole_ref.shape[0]
    half = tiles // 2 - edge
    moves = [
        (whole_ref, edge, low_ref), (whole_ref, edge + half, high_ref),
        (blocks_ref, edge, low_blocks),
        (blocks_ref, at_end("even", info) * (tiles - edge), even_blocks),
        (blocks_ref, edge + half, high_blocks),
        (blocks_ref, at_end("odd", info) * (tiles - edge), odd_blocks),
    ]
    copies = [
        pltpu.make_async_copy(source.at[pl.ds(first, target.shape[0])], target, sem.at[i])
        for i, (source, first, target) in enumerate(moves)
    ]
    for copy in copies:
        copy.start()
    for copy in copies:
        copy.wait()
    live = info[LIVE]
    clear_dead(low_ref, edge, live)
    clear_dead(high_ref, edge + half, live)


def masked_edges(info, start):
    _, tile, width = start.shape
    return pl.pallas_call(
        edges_kernel,
        in_specs=[SMEM, HBM],
        out_specs=[VMEM] * 2,
        out_shape=[jax.ShapeDtypeStruct((HALO_T, tile, width), BF16)] * 2,
        scratch_shapes=[pltpu.SemaphoreType.DMA((2,))],
        compiler_params=pltpu.CompilerParams(vmem_limit_bytes=4 * 1024 * 1024),
        cost_estimate=SMALL,
        name="masked_edges",
    )(info, start)


def prepare(info, start, blocks):
    tiles, tile, width = start.shape
    half = tiles // 2 - HALO_T
    block_counts = (HALO_T, HALO_T, half, half)
    shapes = [jax.ShapeDtypeStruct((half, tile, width), BF16)] * 2
    shapes += [
        jax.ShapeDtypeStruct((count,) + blocks.shape[1:], blocks.dtype) for count in block_counts
    ]
    return pl.pallas_call(
        prepare_kernel,
        in_specs=[SMEM, HBM, HBM],
        out_specs=[VMEM] * 6,
        out_shape=shapes,
        scratch_shapes=[pltpu.SemaphoreType.DMA((6,))],
        compiler_params=pltpu.CompilerParams(vmem_limit_bytes=16 * 1024 * 1024),
        cost_estimate=SMALL,
        name="prepare",
    )(info, start, blocks)


def layout(name, info, tiles):
    edge, half = HALO_T, tiles // 2 - HALO_T
    if name in ("even", "odd"):
        end = at_end(name, info)
        first = end * (tiles - edge)
        places = [
            (0, 2 * edge * end), (0, edge), (0, 2 * edge + edge * end),
            (half - edge, 3 * edge * (1 - end)),
        ]
        return first, first - edge, places
    spare = half + 2 * edge
    ends = at_end("even", info), at_end("odd", info)
    if name == "low":
        places = [(0, end * spare) for end in ends] + [(0, edge), (0, edge + half)]
        return edge, 0, places
    places = [(0, spare - edge * end) for end in ends] + [(half - edge, 0), (0, edge)]
    return edge + half, half, places


def rows_kernel(name, counts, tiles, info, cols_ref, *refs):
    sources = refs[:4]
    blocks_ref, out_ref, held = refs[-3:]
    prev_ref = refs[4] if len(refs) == 8 else None
    nnz = blocks_ref.shape[1]
    first, base, places = layout(name, info, tiles)
    for source, count, (begin, slot) in zip(sources, counts, places):
        held[pl.ds(slot, count)] = source[pl.ds(begin, count)]
    live = info[LIVE]
    shift = info[PATCH] * tiles + base

    def group(index, carry):
        for r in range(GROUP):
            row = index * GROUP + r
            listed = [cols_ref[(first + row) * nnz + n] - shift for n in range(nnz)]
            acc = tile_row(lambda n: blocks_ref[row, n], listed, lambda c: held[c])
            prev = None if prev_ref is None else prev_ref[row]
            out_ref[row] = finish(acc, prev, first + row < live)
        return carry

    lax.fori_loop(0, out_ref.shape[0] // GROUP, group, 0)


def tile_rows(name, info, cols, blocks, pieces, prev, cost):
    rows, nnz, tile, _ = blocks.shape
    tiles = cols.shape[0] // nnz
    width = pieces[0].shape[-1]
    edge, half = HALO_T, tiles // 2 - HALO_T
    if name in ("even", "odd"):
        counts, window = (edge,) * 4, 4 * edge
    else:
        counts, window = (edge, edge, half, edge), half + 3 * edge
        if name == "high":
            counts = (edge, edge, edge, half)
    args = list(pieces) + ([] if prev is None else [prev]) + [blocks]
    return pl.pallas_call(
        functools.partial(rows_kernel, name, counts, tiles),
        in_specs=[SMEM, SMEM] + [VMEM] * len(args),
        out_specs=VMEM,
        out_shape=jax.ShapeDtypeStruct((rows, tile, width), BF16),
        scratch_shapes=[pltpu.VMEM((window, tile, width), BF16)],
        compiler_params=SMALL_VMEM,
        cost_estimate=cost,
        name="rows_" + name,
    )(info, cols, *args)


ACROSS = (((0,), (0,)), ((), ()))


def add_square(chunk, own_ref, square):
    def add(index, carry):
        own = own_ref[pl.ds(pl.multiple_of(index * chunk, chunk), chunk), :]
        square[...] += lax.dot_general(own, own, ACROSS, preferred_element_type=F32)
        return carry

    lax.fori_loop(0, own_ref.shape[0] // chunk, add, 0)


def add_cross(chunk, info, own_ref, other_ref, cross):
    half = cross.shape[0]
    is_first = info[PART] == 0

    def add(index, carry):
        rows = pl.ds(pl.multiple_of(index * chunk, chunk), chunk)
        own, other = own_ref[rows, :], other_ref[rows, :]
        left = jnp.where(is_first, own[:, :half], other[:, half:])
        right = jnp.where(is_first, other, own)
        cross[...] += lax.dot_general(left, right, ACROSS, preferred_element_type=F32)
        return carry

    lax.fori_loop(0, own_ref.shape[0] // chunk, add, 0)


def square_kernel(chunk, *refs):
    refs[-1][...] = jnp.zeros(refs[-1].shape, F32)
    for own_ref in refs[:-1]:
        add_square(chunk, own_ref, refs[-1])


def cross_kernel(chunk, info, *refs):
    count = len(refs) // 2
    refs[-1][...] = jnp.zeros(refs[-1].shape, F32)
    for own_ref, other_ref in zip(refs[:count], refs[count:-1]):
        add_cross(chunk, info, own_ref, other_ref, refs[-1])


def share_kernel(chunk, info, own_ref, other_ref, square_ref, cross_ref, out_ref, square, cross):
    square[...] = square_ref[...]
    cross[...] = cross_ref[...]
    add_square(chunk, own_ref, square)
    add_cross(chunk, info, own_ref, other_ref, cross)
    half = cross.shape[0]
    blocks = [
        square[:half, :half], square[:half, half:], square[half:, half:],
        cross[:, :half], cross[:, half:],
    ]
    for i, block in enumerate(blocks):
        out_ref[pl.ds(i * half, half), :] = block
    used = len(blocks) * half
    if used < out_ref.shape[0]:
        out_ref[used:, :] = jnp.zeros((out_ref.shape[0] - used, half), F32)


def gram_call(body, name, args, shape, scratch=(), scalars=()):
    return pl.pallas_call(
        body,
        in_specs=[SMEM] * len(scalars) + [VMEM] * len(args),
        out_specs=VMEM,
        out_shape=jax.ShapeDtypeStruct(shape, F32),
        scratch_shapes=scratch,
        compiler_params=SMALL_VMEM,
        cost_estimate=SMALL,
        name=name,
    )(*scalars, *args)


def gram_square(owns):
    chunk, width = min(own.shape[0] for own in owns), owns[0].shape[1]
    body = functools.partial(square_kernel, chunk)
    return gram_call(body, "gram_square", owns, (width, width))


def gram_cross(info, owns, others):
    chunk, width = min(own.shape[0] for own in owns), owns[0].shape[1]
    body = functools.partial(cross_kernel, chunk)
    shape = (width // 2, width)
    return gram_call(body, "gram_cross", owns + others, shape, scalars=[info])


def gram_share(info, own, other, square, cross, count):
    width = own.shape[1]
    half = width // 2
    rows = -(-5 * half // (8 * count)) * 8 * count
    body = functools.partial(share_kernel, own.shape[0])
    scratch = [pltpu.VMEM((width, width), F32), pltpu.VMEM((half, width), F32)]
    args = [own, other, square, cross]
    return gram_call(body, "gram_share", args, (rows, half), scratch, [info])


def sum_kernel(parts_ref, out_ref):
    count = parts_ref.shape[0]
    values = [parts_ref[i] for i in range(count)]
    while len(values) > 1:
        pairs = zip(values[::2], values[1::2])
        values = [one + two for one, two in pairs] + values[len(values) // 2 * 2 :]
    for i in range(count):
        out_ref[i] = values[0]


def sum_over_patch(share):
    count = lax.axis_size("patch")
    parts = share.reshape(count, -1, share.shape[1])
    parts = lax.all_to_all(parts, "patch", 0, 0, tiled=True)
    totals = gram_call(sum_kernel, "sum_parts", [parts], parts.shape)
    return lax.all_to_all(totals, "patch", 0, 0, tiled=True).reshape(share.shape)


def split(value):
    high = value.astype(BF16)
    return high, (value - high.astype(F32)).astype(BF16)


def put(pair, blocks, right=False):
    width = blocks[0].shape[0]
    places = [(0, 0), (0, 1), (1, 1)]
    if right:
        blocks, places = tuple(blocks) + (blocks[1].T,), places + [(1, 0)]
    for (row, col), block in zip(places, blocks):
        for i, piece in enumerate(split(block)):
            pair[i, pl.ds(row * width, width), pl.ds(col * width, width)] = piece


def product3(left, right):
    rows = left[0].shape[0]
    both = dot(jnp.concatenate(left, axis=0), right[0])
    return both[:rows] + both[rows:] + dot(left[0], right[1])


def product(left, right):
    width = left.shape[1] // 2
    first = product3(
        (left[0, :width, :], left[1, :width, :]), (right[0], right[1])
    )
    second = product3(
        (right[0, width:, :], right[1, width:, :]), (left[0, :, width:], left[1, :, width:])
    )
    return first[:, :width], first[:, width:], second


def combine(*terms, unit=0.0):
    width = terms[0][1][0].shape[0]
    row = lax.broadcasted_iota(jnp.int32, (width, width), 0)
    col = lax.broadcasted_iota(jnp.int32, (width, width), 1)
    diagonal = jnp.where(row == col, unit, 0.0)
    out = []
    for i in range(3):
        value = functools.reduce(jnp.add, [factor * matrix[i] for factor, matrix in terms])
        out.append(value if i == 1 else value + diagonal)
    return tuple(out)


def finish_kernel(total_rows, chunk, info, mine, theirs, *refs):
    fields, out_ref = refs[:8], refs[8]
    x_ref, x_held, x_pair, q_pair, u_pair, n_pair, v_pair, z_pair = refs[9:17]
    wide, result, sem, out_sem = refs[17:]
    part = info[PART]
    size = x_ref.shape[0]
    width = size // 2
    half = width // 2
    edge_size = fields[0].shape[0]
    end = wide.shape[0] - edge_size
    starts = [
        at_end("even", info) * end, edge_size, edge_size + fields[1].shape[0],
        at_end("odd", info) * end,
    ]
    copies = []
    for i, source in enumerate(fields):
        rows = pl.ds(pl.multiple_of(starts[i % 4], edge_size), source.shape[0])
        side = part if i < 4 else 1 - part
        target = wide.at[rows, pl.ds(pl.multiple_of(side * width, width), width)]
        copies.append(pltpu.make_async_copy(source, target, sem.at[i]))
    for copy in copies:
        copy.start()

    def block(side, index):
        rows = pl.ds(index * half, half)
        return jnp.where(part == side, mine[rows, :], theirs[rows, :])

    def place(row, col, value):
        x_ref[pl.ds(row * half, half), pl.ds(col * half, half)] = value

    for side in range(2):
        across = block(side, 1)
        place(2 * side, 2 * side, block(side, 0))
        place(2 * side, 2 * side + 1, across)
        place(2 * side + 1, 2 * side, across.T)
        place(2 * side + 1, 2 * side + 1, block(side, 2))
        place(side, 2, block(side, 3))
        place(side, 3, block(side, 4))

    gram = x_ref[:width, :width], x_ref[:width, width:], x_ref[width:, width:]
    squares = gram[0] * gram[0] + 2.0 * (gram[1] * gram[1]) + gram[2] * gram[2]
    norm = jnp.sqrt(jnp.sum(squares, keepdims=True))

    def set_x(x):
        put(x_pair, x, right=True)
        for i, value in enumerate(x):
            x_held[i] = value

    def two_sweeps(first=False, last=False):
        x = tuple(x_held[i] for i in range(3))
        q = product(x_pair, x_pair)
        put(q_pair, q)
        put(u_pair, combine((0.0625, q), (-0.5625, x), unit=1.6875), right=True)
        qu = product(q_pair, u_pair)
        x = tuple(x_held[i] for i in range(3))
        n = combine((1.0, qu), (-2.4375, x), unit=2.25)
        put(n_pair, n, right=True)
        if not last:
            put(v_pair, product(x_pair, n_pair))
        z = n if first else product(z_pair, n_pair)
        if last:
            return z
        put(z_pair, z)
        set_x(product(v_pair, n_pair))

    set_x(tuple(value / norm for value in gram))
    two_sweeps(first=True)

    def body(index, carry):
        two_sweeps()
        return carry

    lax.fori_loop(0, ITERS // 2 - 2, body, 0)
    first, across, second = two_sweeps(last=True)
    z_ref = x_ref
    z_ref[:width, :width] = first
    z_ref[:width, width:] = across
    z_ref[width:, :width] = across.T
    z_ref[width:, width:] = second
    own = pl.ds(pl.multiple_of(part * width, width), width)
    rotation = z_ref[:, own].astype(BF16)
    factor = jnp.sqrt(total_rows / norm)
    for copy in copies:
        copy.wait()
    count = wide.shape[0] // chunk
    outs = []
    for i in range(count):
        rows = pl.ds(i * chunk, chunk)
        result[rows, :] = (dot(wide[rows, :], rotation) * factor).astype(BF16)
        outs.append(pltpu.make_async_copy(result.at[rows], out_ref.at[rows], out_sem.at[i]))
        outs[-1].start()
    for out in outs:
        out.wait()


def rotate(info, mine, theirs, owns, others, total_rows):
    width = owns[0].shape[1]
    rows = sum(own.shape[0] for own in owns)
    size = 2 * width
    chunk = min(rows, 512)
    body = functools.partial(finish_kernel, float(total_rows), chunk)
    pair = pltpu.VMEM((2, size, size), BF16)
    return pl.pallas_call(
        body,
        in_specs=[SMEM, VMEM, VMEM] + [ANY] * 8,
        out_specs=ANY,
        out_shape=jax.ShapeDtypeStruct((rows, width), BF16),
        scratch_shapes=[
            pltpu.VMEM((size, size), F32),
            pltpu.VMEM((3, width, width), F32),
            pair, pair, pair, pair, pair, pair,
            pltpu.VMEM((rows, size), BF16),
            pltpu.VMEM((rows, width), BF16),
            pltpu.SemaphoreType.DMA((8,)),
            pltpu.SemaphoreType.DMA((rows // chunk,)),
        ],
        compiler_params=pltpu.CompilerParams(vmem_limit_bytes=28 * 1024 * 1024),
        cost_estimate=pl.CostEstimate(
            flops=21 * 6 * size**3 + 2 * rows * size * width,
            bytes_accessed=3 * rows * width * 2,
            transcendentals=0,
        ),
        name="rotate",
    )(info, mine, theirs, *owns, *others)


def after(value, *others):
    return lax.optimization_barrier((value, others))[0]


def on_device(vectors, blocks, tile_cols, live_tiles):
    tiles, _, tile, _ = blocks.shape
    width = vectors.shape[1]
    count = lax.axis_size("patch")
    pairs = {
        "even": [(i, i ^ 1) for i in range(count)],
        "odd": [(i, ((i + 1) ^ 1) - 1) for i in range(1, count - 1)],
    }

    def exchange(name, value):
        return lax.ppermute(value, "patch", pairs[name])

    def sibling(value):
        return lax.ppermute(value, "cols", [(0, 1), (1, 0)])

    start = vectors.reshape(tiles, tile, width)
    scalars = [lax.axis_index("cols"), lax.axis_index("patch"), live_tiles[0]]
    info = jnp.stack(scalars).astype(jnp.int32)

    cols = tile_cols.reshape(-1)

    even, odd = masked_edges(after(info, cols), start)
    even_halo = exchange("even", even)
    ready = prepare(after(info, even), start, blocks)
    low, high = ready[:2]
    stored = dict(zip(("even", "odd", "low", "high"), ready[2:]))
    odd_halo = exchange("odd", after(odd, low))
    prev = dict.fromkeys(stored)

    def rows(name, *pieces, cost=SMALL):
        return tile_rows(name, info, cols, stored[name], pieces, prev[name], cost)

    for step in range(STEPS):
        first, final = step == 0, step == STEPS - 1
        if not first:
            new_low = rows("low", even, odd, low, high)
            even_halo = after(even_halo, new_low)
        new_even = rows("even", even_halo, even, low, high)
        if not final:
            even_halo = exchange("even", new_even)
        if first:
            new_low = rows("low", after(even, new_even), odd, low, high)
        new_high = rows("high", even, odd, low, high)
        odd_halo = after(odd_halo, new_even, new_low, new_high)
        if final:
            flat = [value.reshape(-1, width) for value in (new_even, new_low, new_high)]
            others = [sibling(after(value, new_even)) for value in flat]
            square = gram_square(flat)
            odd_halo = after(odd_halo, square)
        new_odd = rows("odd", odd_halo, odd, low, high, cost=LARGE if final else SMALL)
        if not final:
            odd_halo = exchange("odd", new_odd)
        prev = {"even": even, "odd": odd, "low": low, "high": high}
        even, odd, low, high = new_even, new_odd, new_low, new_high
    last = odd.reshape(-1, width)
    other_last = sibling(last)
    others = [after(other, last) for other in others]
    cross = gram_cross(info, flat, others)
    share = gram_share(info, last, other_last, square, cross, count)
    mine = sum_over_patch(share)
    theirs = sibling(mine)
    total_rows = tiles * tile * count
    return rotate(info, mine, theirs, flat + [last], others + [other_last], total_rows)


def solution(mesh):
    in_specs = (P("patch", "cols"), P("patch", None, None, None), P("patch", None), P("patch"))
    return jax.shard_map(
        on_device, mesh=mesh, in_specs=in_specs, out_specs=P("patch", "cols"), check_vma=False
    )
```

```python
import functools

import jax
import jax.numpy as jnp
from jax import lax
from jax.experimental import pallas as pl
from jax.experimental.pallas import tpu as pltpu
from jax.sharding import PartitionSpec as P

HALO_T = 4
STEPS = 3
ITERS = 8
WAYS = 4
GROUP = 4

SMALL = pl.CostEstimate(flops=1000, bytes_accessed=1000, transcendentals=0)
LARGE = pl.CostEstimate(flops=10**11, bytes_accessed=1000, transcendentals=0)
PART, PATCH, LIVE = range(3)
SMALL_VMEM = pltpu.CompilerParams(vmem_limit_bytes=8 * 1024 * 1024)
ANY = pl.BlockSpec(memory_space=pl.ANY)
HBM = pl.BlockSpec(memory_space=pltpu.HBM)
VMEM = pl.BlockSpec(memory_space=pltpu.VMEM)
EDGES_MB, FIELDS_MB, BLOCKS_MB = 53, 50, 44
SMEM = pl.BlockSpec(memory_space=pltpu.SMEM)
F32, BF16 = jnp.float32, jnp.bfloat16


def dot(a, b):
    return jnp.dot(a, b, preferred_element_type=F32)


def tile_row(blocks, listed, field):
    wide = jnp.concatenate([blocks(n) for n in range(len(listed))], axis=1)
    tall = jnp.concatenate([field(tile) for tile in listed], axis=0)
    return dot(wide, tall)


def finish(acc, prev, alive):
    value = acc if prev is None else 2.0 * acc - prev.astype(F32)
    return jnp.where(alive, value, 0.0).astype(BF16)


def at_end(name, info):
    odd = info[PATCH] % 2
    return 1 - odd if name == "even" else odd


def edges_kernel(info, whole_ref, even_ref, odd_ref, sem):
    edge, tiles = HALO_T, whole_ref.shape[0]
    outs = {"even": even_ref, "odd": odd_ref}
    firsts = {name: at_end(name, info) * (tiles - edge) for name in outs}
    copies = [
        pltpu.make_async_copy(whole_ref.at[pl.ds(firsts[name], edge)], outs[name], sem.at[i])
        for i, name in enumerate(outs)
    ]
    for copy in copies:
        copy.start()
    for copy in copies:
        copy.wait()
    for name in outs:
        clear_dead(outs[name], firsts[name], info[LIVE])


def clear_dead(ref, first, live):
    def clear(index, carry):
        ref[index] = jnp.zeros(ref.shape[1:], BF16)
        return carry

    count = ref.shape[0]
    lax.fori_loop(jnp.clip(live - first, 0, count), count, clear, 0)


def load(moves, sem):
    copies = [
        pltpu.make_async_copy(source.at[pl.ds(first, target.shape[0])], target, sem.at[i])
        for i, (source, first, target) in enumerate(moves)
    ]
    for copy in copies:
        copy.start()
    for copy in copies:
        copy.wait()


def fields_kernel(info, whole_ref, blocks_ref, low_ref, high_ref, even_blocks, odd_blocks, sem):
    edge, tiles = HALO_T, whole_ref.shape[0]
    half = tiles // 2 - edge
    moves = [
        (blocks_ref, at_end("even", info) * (tiles - edge), even_blocks),
        (blocks_ref, at_end("odd", info) * (tiles - edge), odd_blocks),
        (whole_ref, edge, low_ref), (whole_ref, edge + half, high_ref),
    ]
    load(moves, sem)
    live = info[LIVE]
    clear_dead(low_ref, edge, live)
    clear_dead(high_ref, edge + half, live)


def blocks_kernel(info, blocks_ref, low_blocks, high_blocks, sem):
    half = low_blocks.shape[0]
    load([(blocks_ref, HALO_T, low_blocks), (blocks_ref, HALO_T + half, high_blocks)], sem)


def masked_edges(info, start):
    _, tile, width = start.shape
    return pl.pallas_call(
        edges_kernel,
        in_specs=[SMEM, HBM],
        out_specs=[VMEM] * 2,
        out_shape=[jax.ShapeDtypeStruct((HALO_T, tile, width), BF16)] * 2,
        scratch_shapes=[pltpu.SemaphoreType.DMA((2,))],
        compiler_params=pltpu.CompilerParams(vmem_limit_bytes=EDGES_MB * 1024 * 1024),
        cost_estimate=SMALL,
        name="masked_edges",
    )(info, start)


def load_call(body, name, info, args, shapes, megabytes):
    return pl.pallas_call(
        body,
        in_specs=[SMEM] + [HBM] * len(args),
        out_specs=[VMEM] * len(shapes),
        out_shape=shapes,
        scratch_shapes=[pltpu.SemaphoreType.DMA((len(shapes),))],
        compiler_params=pltpu.CompilerParams(vmem_limit_bytes=megabytes * 1024 * 1024),
        cost_estimate=SMALL,
        name=name,
    )(info, *args)


def load_fields(info, start, blocks):
    tiles, tile, width = start.shape
    shapes = [jax.ShapeDtypeStruct((tiles // 2 - HALO_T, tile, width), BF16)] * 2
    shapes += [jax.ShapeDtypeStruct((HALO_T,) + blocks.shape[1:], blocks.dtype)] * 2
    return load_call(fields_kernel, "load_fields", info, [start, blocks], shapes, FIELDS_MB)


def load_blocks(info, blocks):
    half = blocks.shape[0] // 2 - HALO_T
    shapes = [jax.ShapeDtypeStruct((half,) + blocks.shape[1:], blocks.dtype)] * 2
    return load_call(blocks_kernel, "load_blocks", info, [blocks], shapes, BLOCKS_MB)


def layout(name, info, tiles):
    edge, half = HALO_T, tiles // 2 - HALO_T
    if name in ("even", "odd"):
        end = at_end(name, info)
        first = end * (tiles - edge)
        places = [
            (0, 2 * edge * end), (0, edge), (0, 2 * edge + edge * end),
            (half - edge, 3 * edge * (1 - end)),
        ]
        return first, first - edge, places
    spare = half + 2 * edge
    ends = at_end("even", info), at_end("odd", info)
    if name == "low":
        places = [(0, end * spare) for end in ends] + [(0, edge), (0, edge + half)]
        return edge, 0, places
    places = [(0, spare - edge * end) for end in ends] + [(half - edge, 0), (0, edge)]
    return edge + half, half, places


def rows_kernel(name, counts, tiles, info, cols_ref, *refs):
    sources = refs[:4]
    blocks_ref, out_ref, held = refs[-3:]
    prev_ref = refs[4] if len(refs) == 8 else None
    nnz = blocks_ref.shape[1]
    first, base, places = layout(name, info, tiles)
    for source, count, (begin, slot) in zip(sources, counts, places):
        held[pl.ds(slot, count)] = source[pl.ds(begin, count)]
    live = info[LIVE]
    shift = info[PATCH] * tiles + base

    def group(index, carry):
        for r in range(GROUP):
            row = index * GROUP + r
            listed = [cols_ref[(first + row) * nnz + n] - shift for n in range(nnz)]
            acc = tile_row(lambda n: blocks_ref[row, n], listed, lambda c: held[c])
            prev = None if prev_ref is None else prev_ref[row]
            out_ref[row] = finish(acc, prev, first + row < live)
        return carry

    lax.fori_loop(0, out_ref.shape[0] // GROUP, group, 0)


def tile_rows(name, info, cols, blocks, pieces, prev, cost):
    rows, nnz, tile, _ = blocks.shape
    tiles = cols.shape[0] // nnz
    width = pieces[0].shape[-1]
    edge, half = HALO_T, tiles // 2 - HALO_T
    if name in ("even", "odd"):
        counts, window = (edge,) * 4, 4 * edge
    else:
        counts, window = (edge, edge, half, edge), half + 3 * edge
        if name == "high":
            counts = (edge, edge, edge, half)
    args = list(pieces) + ([] if prev is None else [prev]) + [blocks]
    return pl.pallas_call(
        functools.partial(rows_kernel, name, counts, tiles),
        in_specs=[SMEM, SMEM] + [VMEM] * len(args),
        out_specs=VMEM,
        out_shape=jax.ShapeDtypeStruct((rows, tile, width), BF16),
        scratch_shapes=[pltpu.VMEM((window, tile, width), BF16)],
        compiler_params=SMALL_VMEM,
        cost_estimate=cost,
        name="rows_" + name,
    )(info, cols, *args)


ACROSS = (((0,), (0,)), ((), ()))


def add_square(chunk, own_ref, square):
    def add(index, carry):
        own = own_ref[pl.ds(pl.multiple_of(index * chunk, chunk), chunk), :]
        square[...] += lax.dot_general(own, own, ACROSS, preferred_element_type=F32)
        return carry

    lax.fori_loop(0, own_ref.shape[0] // chunk, add, 0)


def add_cross(chunk, info, own_ref, other_ref, cross):
    half = cross.shape[0]
    is_first = info[PART] == 0

    def add(index, carry):
        rows = pl.ds(pl.multiple_of(index * chunk, chunk), chunk)
        own, other = own_ref[rows, :], other_ref[rows, :]
        left = jnp.where(is_first, own[:, :half], other[:, half:])
        right = jnp.where(is_first, other, own)
        cross[...] += lax.dot_general(left, right, ACROSS, preferred_element_type=F32)
        return carry

    lax.fori_loop(0, own_ref.shape[0] // chunk, add, 0)


def square_kernel(chunk, *refs):
    refs[-1][...] = jnp.zeros(refs[-1].shape, F32)
    for own_ref in refs[:-1]:
        add_square(chunk, own_ref, refs[-1])


def cross_kernel(chunk, info, *refs):
    count = len(refs) // 2
    refs[-1][...] = jnp.zeros(refs[-1].shape, F32)
    for own_ref, other_ref in zip(refs[:count], refs[count:-1]):
        add_cross(chunk, info, own_ref, other_ref, refs[-1])


def share_kernel(chunk, info, own_ref, other_ref, square_ref, cross_ref, *refs):
    outs, (square, cross, share) = refs[:WAYS], refs[WAYS:]
    square[...] = square_ref[...]
    cross[...] = cross_ref[...]
    add_square(chunk, own_ref, square)
    add_cross(chunk, info, own_ref, other_ref, cross)
    half = cross.shape[0]
    blocks = [
        square[:half, :half], square[:half, half:], square[half:, half:],
        cross[:, :half], cross[:, half:],
    ]
    for i, block in enumerate(blocks):
        share[pl.ds(i * half, half), :] = block
    quarter = info[PATCH] % WAYS
    for d, out in enumerate(outs):
        rows = out.shape[0]
        out[...] = share[pl.ds(pl.multiple_of((quarter ^ d) * rows, 8), rows), :]


def gram_call(body, name, args, shape, scratch=(), scalars=(), outs=0):
    out_shape = jax.ShapeDtypeStruct(shape, F32)
    return pl.pallas_call(
        body,
        in_specs=[SMEM] * len(scalars) + [VMEM] * len(args),
        out_specs=[VMEM] * outs if outs else VMEM,
        out_shape=[out_shape] * outs if outs else out_shape,
        scratch_shapes=scratch,
        compiler_params=SMALL_VMEM,
        cost_estimate=SMALL,
        name=name,
    )(*scalars, *args)


def gram_square(owns):
    chunk, width = min(own.shape[0] for own in owns), owns[0].shape[1]
    body = functools.partial(square_kernel, chunk)
    return gram_call(body, "gram_square", owns, (width, width))


def gram_cross(info, owns, others):
    chunk, width = min(own.shape[0] for own in owns), owns[0].shape[1]
    body = functools.partial(cross_kernel, chunk)
    shape = (width // 2, width)
    return gram_call(body, "gram_cross", owns + others, shape, scalars=[info])


def gram_share(info, own, other, square, cross):
    width = own.shape[1]
    half = width // 2
    body = functools.partial(share_kernel, own.shape[0])
    scratch = [
        pltpu.VMEM((width, width), F32), pltpu.VMEM((half, width), F32),
        pltpu.VMEM((5 * half, half), F32),
    ]
    args = [own, other, square, cross]
    shape = (5 * half // WAYS, half)
    return gram_call(body, "gram_share", args, shape, scratch, [info], outs=WAYS)


def add_kernel(a, b, c, d, out):
    out[...] = (a[...] + b[...]) + (c[...] + d[...])


def join_kernel(info, *refs):
    parts, out = refs[:-1], refs[-1]
    rows = parts[0].shape[0]
    quarter = info[PATCH] % WAYS
    for d, part in enumerate(parts):
        out[pl.ds(pl.multiple_of((quarter ^ d) * rows, 8), rows), :] = part[...]


def sum_over_patch(info, parts):
    count = lax.axis_size("patch")
    rows, columns = parts[0].shape

    def add_four(values):
        return gram_call(add_kernel, "add_four", values, (rows, columns))

    def from_others(values, stride=1):
        return [
            lax.ppermute(values[d], "patch", [(i, i ^ (d * stride)) for i in range(count)])
            for d in range(1, WAYS)
        ]

    total = add_four([parts[0]] + from_others(parts))
    stride = WAYS
    while stride < count:
        total = add_four([total] + from_others([total] * WAYS, stride))
        stride *= WAYS
    quarters = [total] + from_others([total] * WAYS)
    return gram_call(join_kernel, "join", quarters, (WAYS * rows, columns), scalars=[info])


def split(value):
    high = value.astype(BF16)
    return high, (value - high.astype(F32)).astype(BF16)


def put(pair, blocks, right=False):
    width = blocks[0].shape[0]
    places = [(0, 0), (0, 1), (1, 1)]
    if right:
        blocks, places = tuple(blocks) + (blocks[1].T,), places + [(1, 0)]
    for (row, col), block in zip(places, blocks):
        for i, piece in enumerate(split(block)):
            pair[i, pl.ds(row * width, width), pl.ds(col * width, width)] = piece


def product3(left, right):
    rows = left[0].shape[0]
    both = dot(jnp.concatenate(left, axis=0), right[0])
    return both[:rows] + both[rows:] + dot(left[0], right[1])


def product(left, right):
    width = left.shape[1] // 2
    first = product3(
        (left[0, :width, :], left[1, :width, :]), (right[0], right[1])
    )
    second = product3(
        (right[0, width:, :], right[1, width:, :]), (left[0, :, width:], left[1, :, width:])
    )
    return first[:, :width], first[:, width:], second


def combine(*terms, unit=0.0):
    width = terms[0][1][0].shape[0]
    row = lax.broadcasted_iota(jnp.int32, (width, width), 0)
    col = lax.broadcasted_iota(jnp.int32, (width, width), 1)
    diagonal = jnp.where(row == col, unit, 0.0)
    out = []
    for i in range(3):
        value = functools.reduce(jnp.add, [factor * matrix[i] for factor, matrix in terms])
        out.append(value if i == 1 else value + diagonal)
    return tuple(out)


def finish_kernel(total_rows, chunk, info, mine, theirs, *refs):
    fields, out_ref = refs[:8], refs[8]
    x_ref, x_held, x_pair, q_pair, u_pair, n_pair, v_pair, z_pair = refs[9:17]
    wide, result, sem, out_sem = refs[17:]
    part = info[PART]
    size = x_ref.shape[0]
    width = size // 2
    half = width // 2
    edge_size = fields[0].shape[0]
    end = wide.shape[0] - edge_size
    starts = [
        at_end("even", info) * end, edge_size, edge_size + fields[1].shape[0],
        at_end("odd", info) * end,
    ]
    copies = []
    for i, source in enumerate(fields):
        rows = pl.ds(pl.multiple_of(starts[i % 4], edge_size), source.shape[0])
        side = part if i < 4 else 1 - part
        target = wide.at[rows, pl.ds(pl.multiple_of(side * width, width), width)]
        copies.append(pltpu.make_async_copy(source, target, sem.at[i]))
    for copy in copies:
        copy.start()

    def block(side, index):
        rows = pl.ds(index * half, half)
        return jnp.where(part == side, mine[rows, :], theirs[rows, :])

    def place(row, col, value):
        x_ref[pl.ds(row * half, half), pl.ds(col * half, half)] = value

    for side in range(2):
        across = block(side, 1)
        place(2 * side, 2 * side, block(side, 0))
        place(2 * side, 2 * side + 1, across)
        place(2 * side + 1, 2 * side, across.T)
        place(2 * side + 1, 2 * side + 1, block(side, 2))
        place(side, 2, block(side, 3))
        place(side, 3, block(side, 4))

    gram = x_ref[:width, :width], x_ref[:width, width:], x_ref[width:, width:]
    squares = gram[0] * gram[0] + 2.0 * (gram[1] * gram[1]) + gram[2] * gram[2]
    norm = jnp.sqrt(jnp.sum(squares, keepdims=True))

    def set_x(x):
        put(x_pair, x, right=True)
        for i, value in enumerate(x):
            x_held[i] = value

    def two_sweeps(first=False, last=False):
        x = tuple(x_held[i] for i in range(3))
        q = product(x_pair, x_pair)
        put(q_pair, q)
        put(u_pair, combine((0.0625, q), (-0.5625, x), unit=1.6875), right=True)
        qu = product(q_pair, u_pair)
        x = tuple(x_held[i] for i in range(3))
        n = combine((1.0, qu), (-2.4375, x), unit=2.25)
        put(n_pair, n, right=True)
        if not last:
            put(v_pair, product(x_pair, n_pair))
        z = n if first else product(z_pair, n_pair)
        if last:
            return z
        put(z_pair, z)
        set_x(product(v_pair, n_pair))

    set_x(tuple(value / norm for value in gram))
    two_sweeps(first=True)

    def body(index, carry):
        two_sweeps()
        return carry

    lax.fori_loop(0, ITERS // 2 - 2, body, 0)
    first, across, second = two_sweeps(last=True)
    z_ref = x_ref
    z_ref[:width, :width] = first
    z_ref[:width, width:] = across
    z_ref[width:, :width] = across.T
    z_ref[width:, width:] = second
    own = pl.ds(pl.multiple_of(part * width, width), width)
    rotation = z_ref[:, own].astype(BF16)
    factor = jnp.sqrt(total_rows / norm)
    for copy in copies:
        copy.wait()
    count = wide.shape[0] // chunk
    outs = []
    for i in range(count):
        rows = pl.ds(i * chunk, chunk)
        result[rows, :] = (dot(wide[rows, :], rotation) * factor).astype(BF16)
        outs.append(pltpu.make_async_copy(result.at[rows], out_ref.at[rows], out_sem.at[i]))
        outs[-1].start()
    for out in outs:
        out.wait()


def rotate(info, mine, theirs, owns, others, total_rows):
    width = owns[0].shape[1]
    rows = sum(own.shape[0] for own in owns)
    size = 2 * width
    chunk = min(rows, 512)
    body = functools.partial(finish_kernel, float(total_rows), chunk)
    pair = pltpu.VMEM((2, size, size), BF16)
    return pl.pallas_call(
        body,
        in_specs=[SMEM, VMEM, VMEM] + [ANY] * 8,
        out_specs=ANY,
        out_shape=jax.ShapeDtypeStruct((rows, width), BF16),
        scratch_shapes=[
            pltpu.VMEM((size, size), F32),
            pltpu.VMEM((3, width, width), F32),
            pair, pair, pair, pair, pair, pair,
            pltpu.VMEM((rows, size), BF16),
            pltpu.VMEM((rows, width), BF16),
            pltpu.SemaphoreType.DMA((8,)),
            pltpu.SemaphoreType.DMA((rows // chunk,)),
        ],
        compiler_params=pltpu.CompilerParams(vmem_limit_bytes=28 * 1024 * 1024),
        cost_estimate=pl.CostEstimate(
            flops=21 * 6 * size**3 + 2 * rows * size * width,
            bytes_accessed=3 * rows * width * 2,
            transcendentals=0,
        ),
        name="rotate",
    )(info, mine, theirs, *owns, *others)


def after(value, *others):
    return lax.optimization_barrier((value, others))[0]


def on_device(vectors, blocks, tile_cols, live_tiles):
    tiles, _, tile, _ = blocks.shape
    width = vectors.shape[1]
    count = lax.axis_size("patch")
    pairs = {
        "even": [(i, i ^ 1) for i in range(count)],
        "odd": [(i, ((i + 1) ^ 1) - 1) for i in range(1, count - 1)],
    }

    def exchange(name, value):
        return lax.ppermute(value, "patch", pairs[name])

    def sibling(value):
        return lax.ppermute(value, "cols", [(0, 1), (1, 0)])

    start = vectors.reshape(tiles, tile, width)
    scalars = [lax.axis_index("cols"), lax.axis_index("patch"), live_tiles[0]]
    info = jnp.stack(scalars).astype(jnp.int32)

    cols = tile_cols.reshape(-1)

    even, odd = masked_edges(after(info, cols), start)
    even_halo = exchange("even", even)
    low, high, even_blocks, odd_blocks = load_fields(after(info, even), start, blocks)
    odd_halo = exchange("odd", after(odd, low))
    low_blocks, high_blocks = load_blocks(after(info, low), blocks)
    stored = {"even": even_blocks, "odd": odd_blocks, "low": low_blocks, "high": high_blocks}
    prev = dict.fromkeys(stored)

    def rows(name, *pieces, cost=SMALL):
        return tile_rows(name, info, cols, stored[name], pieces, prev[name], cost)

    for step in range(STEPS):
        final = step == STEPS - 1
        new_even = rows("even", after(even_halo, low_blocks), even, low, high)
        if not final:
            even_halo = exchange("even", new_even)
        held = after(even, new_even)
        new_low, new_high = rows("low", held, odd, low, high), rows("high", held, odd, low, high)
        odd_halo = after(odd_halo, new_low, new_high)
        if final:
            flat = [value.reshape(-1, width) for value in (new_even, new_low, new_high)]
            others = [sibling(value) for value in flat]
            square = gram_square(flat)
            odd_halo = after(odd_halo, square)
        new_odd = rows("odd", odd_halo, odd, low, high, cost=LARGE if final else SMALL)
        if not final:
            odd_halo = exchange("odd", new_odd)
        prev = {"even": even, "odd": odd, "low": low, "high": high}
        even, odd, low, high = new_even, new_odd, new_low, new_high
    last = odd.reshape(-1, width)
    other_last = sibling(last)
    others = [after(other, last) for other in others]
    cross = gram_cross(info, flat, others)
    mine = sum_over_patch(info, gram_share(info, last, other_last, square, cross))
    theirs = sibling(mine)
    total_rows = tiles * tile * count
    return rotate(info, mine, theirs, flat + [last], others + [other_last], total_rows)


def solution(mesh):
    in_specs = (P("patch", "cols"), P("patch", None, None, None), P("patch", None), P("patch"))
    return jax.shard_map(
        on_device, mesh=mesh, in_specs=in_specs, out_specs=P("patch", "cols"), check_vma=False
    )
```

```python
import functools

import jax
import jax.numpy as jnp
from jax import lax
from jax.experimental import pallas as pl
from jax.experimental.pallas import tpu as pltpu
from jax.sharding import PartitionSpec as P

HALO_T = 4
STEPS = 3
ITERS = 8
WAYS = 4
LOAD_CUTS = 4
GROUP = 4

SMALL = pl.CostEstimate(flops=1000, bytes_accessed=1000, transcendentals=0)
LARGE = pl.CostEstimate(flops=10**11, bytes_accessed=1000, transcendentals=0)
PART, PATCH, LIVE = range(3)
SMALL_VMEM = pltpu.CompilerParams(vmem_limit_bytes=8 * 1024 * 1024)
ANY = pl.BlockSpec(memory_space=pl.ANY)
HBM = pl.BlockSpec(memory_space=pltpu.HBM)
VMEM = pl.BlockSpec(memory_space=pltpu.VMEM)
EDGES_MB, FIELDS_MB, BLOCKS_MB = 53, 50, 44
SMEM = pl.BlockSpec(memory_space=pltpu.SMEM)
F32, BF16 = jnp.float32, jnp.bfloat16


def dot(a, b):
    return jnp.dot(a, b, preferred_element_type=F32)


def tile_row(blocks, listed, field):
    wide = jnp.concatenate([blocks(n) for n in range(len(listed))], axis=1)
    tall = jnp.concatenate([field(tile) for tile in listed], axis=0)
    return dot(wide, tall)


def finish(acc, prev, alive):
    value = acc if prev is None else 2.0 * acc - prev.astype(F32)
    return jnp.where(alive, value, 0.0).astype(BF16)


def at_end(name, info):
    odd = info[PATCH] % 2
    return 1 - odd if name == "even" else odd


def edges_kernel(info, whole_ref, even_ref, odd_ref, sem):
    edge, tiles = HALO_T, whole_ref.shape[0]
    outs = {"even": even_ref, "odd": odd_ref}
    firsts = {name: at_end(name, info) * (tiles - edge) for name in outs}
    copies = [
        pltpu.make_async_copy(whole_ref.at[pl.ds(firsts[name], edge)], outs[name], sem.at[i])
        for i, name in enumerate(outs)
    ]
    for copy in copies:
        copy.start()
    for copy in copies:
        copy.wait()
    for name in outs:
        clear_dead(outs[name], firsts[name], info[LIVE])


def clear_dead(ref, first, live):
    def clear(index, carry):
        ref[index] = jnp.zeros(ref.shape[1:], BF16)
        return carry

    count = ref.shape[0]
    lax.fori_loop(jnp.clip(live - first, 0, count), count, clear, 0)


def load(moves, sem):
    copies = []
    for source, first, target in moves:
        count = target.shape[0] // LOAD_CUTS
        for cut in range(LOAD_CUTS):
            copies.append(
                pltpu.make_async_copy(
                    source.at[pl.ds(first + cut * count, count)],
                    target.at[pl.ds(cut * count, count)],
                    sem.at[len(copies)],
                )
            )
    for copy in copies:
        copy.start()
    for copy in copies:
        copy.wait()


def fields_kernel(info, whole_ref, blocks_ref, low_ref, high_ref, even_blocks, odd_blocks, sem):
    edge, tiles = HALO_T, whole_ref.shape[0]
    half = tiles // 2 - edge
    moves = [
        (blocks_ref, at_end("even", info) * (tiles - edge), even_blocks),
        (blocks_ref, at_end("odd", info) * (tiles - edge), odd_blocks),
        (whole_ref, edge, low_ref), (whole_ref, edge + half, high_ref),
    ]
    load(moves, sem)
    live = info[LIVE]
    clear_dead(low_ref, edge, live)
    clear_dead(high_ref, edge + half, live)


def blocks_kernel(info, blocks_ref, low_blocks, high_blocks, sem):
    half = low_blocks.shape[0]
    load([(blocks_ref, HALO_T, low_blocks), (blocks_ref, HALO_T + half, high_blocks)], sem)


def masked_edges(info, start):
    _, tile, width = start.shape
    return pl.pallas_call(
        edges_kernel,
        in_specs=[SMEM, HBM],
        out_specs=[VMEM] * 2,
        out_shape=[jax.ShapeDtypeStruct((HALO_T, tile, width), BF16)] * 2,
        scratch_shapes=[pltpu.SemaphoreType.DMA((2,))],
        compiler_params=pltpu.CompilerParams(vmem_limit_bytes=EDGES_MB * 1024 * 1024),
        cost_estimate=SMALL,
        name="masked_edges",
    )(info, start)


def load_call(body, name, info, args, shapes, megabytes):
    return pl.pallas_call(
        body,
        in_specs=[SMEM] + [HBM] * len(args),
        out_specs=[VMEM] * len(shapes),
        out_shape=shapes,
        scratch_shapes=[pltpu.SemaphoreType.DMA((len(shapes) * LOAD_CUTS,))],
        compiler_params=pltpu.CompilerParams(vmem_limit_bytes=megabytes * 1024 * 1024),
        cost_estimate=SMALL,
        name=name,
    )(info, *args)


def load_fields(info, start, blocks):
    tiles, tile, width = start.shape
    shapes = [jax.ShapeDtypeStruct((tiles // 2 - HALO_T, tile, width), BF16)] * 2
    shapes += [jax.ShapeDtypeStruct((HALO_T,) + blocks.shape[1:], blocks.dtype)] * 2
    return load_call(fields_kernel, "load_fields", info, [start, blocks], shapes, FIELDS_MB)


def load_blocks(info, blocks):
    half = blocks.shape[0] // 2 - HALO_T
    shapes = [jax.ShapeDtypeStruct((half,) + blocks.shape[1:], blocks.dtype)] * 2
    return load_call(blocks_kernel, "load_blocks", info, [blocks], shapes, BLOCKS_MB)


def layout(name, info, tiles):
    edge, half = HALO_T, tiles // 2 - HALO_T
    if name in ("even", "odd"):
        end = at_end(name, info)
        first = end * (tiles - edge)
        places = [
            (0, 2 * edge * end), (0, edge), (0, 2 * edge + edge * end),
            (half - edge, 3 * edge * (1 - end)),
        ]
        return first, first - edge, places
    spare = half + 2 * edge
    ends = at_end("even", info), at_end("odd", info)
    if name == "low":
        places = [(0, end * spare) for end in ends] + [(0, edge), (0, edge + half)]
        return edge, 0, places
    places = [(0, spare - edge * end) for end in ends] + [(half - edge, 0), (0, edge)]
    return edge + half, half, places


def rows_kernel(name, counts, tiles, info, cols_ref, *refs):
    sources = refs[:4]
    blocks_ref, out_ref, held = refs[-3:]
    prev_ref = refs[4] if len(refs) == 8 else None
    nnz = blocks_ref.shape[1]
    first, base, places = layout(name, info, tiles)
    for source, count, (begin, slot) in zip(sources, counts, places):
        held[pl.ds(slot, count)] = source[pl.ds(begin, count)]
    live = info[LIVE]
    shift = info[PATCH] * tiles + base

    def group(index, carry):
        for r in range(GROUP):
            row = index * GROUP + r
            listed = [cols_ref[n, first + row] - shift for n in range(nnz)]
            acc = tile_row(lambda n: blocks_ref[row, n], listed, lambda c: held[c])
            prev = None if prev_ref is None else prev_ref[row]
            out_ref[row] = finish(acc, prev, first + row < live)
        return carry

    lax.fori_loop(0, out_ref.shape[0] // GROUP, group, 0)


def tile_rows(name, info, cols, blocks, pieces, prev, cost):
    rows, _, tile, _ = blocks.shape
    tiles = cols.shape[1]
    width = pieces[0].shape[-1]
    edge, half = HALO_T, tiles // 2 - HALO_T
    if name in ("even", "odd"):
        counts, window = (edge,) * 4, 4 * edge
    else:
        counts, window = (edge, edge, half, edge), half + 3 * edge
        if name == "high":
            counts = (edge, edge, edge, half)
    args = list(pieces) + ([] if prev is None else [prev]) + [blocks]
    return pl.pallas_call(
        functools.partial(rows_kernel, name, counts, tiles),
        in_specs=[SMEM, SMEM] + [VMEM] * len(args),
        out_specs=VMEM,
        out_shape=jax.ShapeDtypeStruct((rows, tile, width), BF16),
        scratch_shapes=[pltpu.VMEM((window, tile, width), BF16)],
        compiler_params=SMALL_VMEM,
        cost_estimate=cost,
        name="rows_" + name,
    )(info, cols, *args)


ACROSS = (((0,), (0,)), ((), ()))


def add_gram(chunk, own_ref, other_ref, total):
    def add(index, carry):
        rows = pl.ds(pl.multiple_of(index * chunk, chunk), chunk)
        own = own_ref[rows, :]
        both = jnp.concatenate([own, other_ref[rows, :]], axis=1)
        total[...] += lax.dot_general(own, both, ACROSS, preferred_element_type=F32)
        return carry

    lax.fori_loop(0, own_ref.shape[0] // chunk, add, 0)


def gram_kernel(chunk, *refs):
    count = len(refs) // 2
    refs[-1][...] = jnp.zeros(refs[-1].shape, F32)
    for own_ref, other_ref in zip(refs[:count], refs[count:-1]):
        add_gram(chunk, own_ref, other_ref, refs[-1])


def share_kernel(chunk, info, own_ref, other_ref, start_ref, *refs):
    outs, (total, share) = refs[:WAYS], refs[WAYS:]
    total[...] = start_ref[...]
    add_gram(chunk, own_ref, other_ref, total)
    width = total.shape[0]
    half = width // 2
    own, other = total[:, :width], total[:, width:]
    second = jnp.where(info[PART] == 0, other[:half, :half], other[:half, half:])
    third = jnp.where(info[PART] == 0, other[:half, half:], other[half:, half:])
    blocks = [own[:half, :half], own[:half, half:], own[half:, half:], second, third]
    for i, block in enumerate(blocks):
        share[pl.ds(i * half, half), :] = block
    quarter = info[PATCH] % WAYS
    for d, out in enumerate(outs):
        rows = out.shape[0]
        out[...] = share[pl.ds(pl.multiple_of((quarter ^ d) * rows, 8), rows), :]


def gram_call(body, name, args, shape, scratch=(), scalars=(), outs=0):
    out_shape = jax.ShapeDtypeStruct(shape, F32)
    return pl.pallas_call(
        body,
        in_specs=[SMEM] * len(scalars) + [VMEM] * len(args),
        out_specs=[VMEM] * outs if outs else VMEM,
        out_shape=[out_shape] * outs if outs else out_shape,
        scratch_shapes=scratch,
        compiler_params=SMALL_VMEM,
        cost_estimate=SMALL,
        name=name,
    )(*scalars, *args)


def gram(owns, others):
    chunk, width = min(own.shape[0] for own in owns), owns[0].shape[1]
    body = functools.partial(gram_kernel, chunk)
    return gram_call(body, "gram", owns + others, (width, 2 * width))


def gram_share(info, own, other, start):
    rows, width = own.shape
    half = width // 2
    body = functools.partial(share_kernel, rows)
    scratch = [pltpu.VMEM((width, 2 * width), F32), pltpu.VMEM((5 * half, half), F32)]
    shape = (5 * half // WAYS, half)
    args = [own, other, start]
    return gram_call(body, "gram_share", args, shape, scratch, [info], outs=WAYS)


def add_kernel(a, b, c, d, out):
    out[...] = (a[...] + b[...]) + (c[...] + d[...])


def join_kernel(info, *refs):
    parts, out = refs[:-1], refs[-1]
    rows = parts[0].shape[0]
    quarter = info[PATCH] % WAYS
    for d, part in enumerate(parts):
        out[pl.ds(pl.multiple_of((quarter ^ d) * rows, 8), rows), :] = part[...]


def sum_over_patch(info, parts):
    count = lax.axis_size("patch")
    rows, columns = parts[0].shape

    def add_four(values):
        return gram_call(add_kernel, "add_four", values, (rows, columns))

    def from_others(values, stride=1):
        return [
            lax.ppermute(values[d], "patch", [(i, i ^ (d * stride)) for i in range(count)])
            for d in range(1, WAYS)
        ]

    total = add_four([parts[0]] + from_others(parts))
    stride = WAYS
    while stride < count:
        total = add_four([total] + from_others([total] * WAYS, stride))
        stride *= WAYS
    quarters = [total] + from_others([total] * WAYS)
    return gram_call(join_kernel, "join", quarters, (WAYS * rows, columns), scalars=[info])


def split(value):
    high = value.astype(BF16)
    return high, (value - high.astype(F32)).astype(BF16)


def put(pair, blocks, right=False):
    width = blocks[0].shape[0]
    places = [(0, 0), (0, 1), (1, 1)]
    if right:
        blocks, places = tuple(blocks) + (blocks[1].T,), places + [(1, 0)]
    for (row, col), block in zip(places, blocks):
        for i, piece in enumerate(split(block)):
            pair[i, pl.ds(row * width, width), pl.ds(col * width, width)] = piece


def product3(left, right):
    rows = left[0].shape[0]
    both = dot(jnp.concatenate(left, axis=0), right[0])
    return both[:rows] + both[rows:] + dot(left[0], right[1])


def product(left, right):
    width = left.shape[1] // 2
    first = product3(
        (left[0, :width, :], left[1, :width, :]), (right[0], right[1])
    )
    second = product3(
        (right[0, width:, :], right[1, width:, :]), (left[0, :, width:], left[1, :, width:])
    )
    return first[:, :width], first[:, width:], second


def combine(*terms, unit=0.0):
    width = terms[0][1][0].shape[0]
    row = lax.broadcasted_iota(jnp.int32, (width, width), 0)
    col = lax.broadcasted_iota(jnp.int32, (width, width), 1)
    diagonal = jnp.where(row == col, unit, 0.0)
    out = []
    for i in range(3):
        value = functools.reduce(jnp.add, [factor * matrix[i] for factor, matrix in terms])
        out.append(value if i == 1 else value + diagonal)
    return tuple(out)


def finish_kernel(total_rows, chunk, info, mine, theirs, *refs):
    fields, out_ref = refs[:8], refs[8]
    x_ref, x_held, x_pair, q_pair, u_pair, n_pair, v_pair, z_pair = refs[9:17]
    wide, result, sem, out_sem = refs[17:]
    part = info[PART]
    size = x_ref.shape[0]
    width = size // 2
    half = width // 2
    edge_size = fields[0].shape[0]
    end = wide.shape[0] - edge_size
    starts = [
        at_end("even", info) * end, edge_size, edge_size + fields[1].shape[0],
        at_end("odd", info) * end,
    ]
    copies = []
    for i, source in enumerate(fields):
        rows = pl.ds(pl.multiple_of(starts[i % 4], edge_size), source.shape[0])
        side = part if i < 4 else 1 - part
        target = wide.at[rows, pl.ds(pl.multiple_of(side * width, width), width)]
        copies.append(pltpu.make_async_copy(source, target, sem.at[i]))
    for copy in copies:
        copy.start()

    def block(side, index):
        rows = pl.ds(index * half, half)
        return jnp.where(part == side, mine[rows, :], theirs[rows, :])

    def place(row, col, value):
        x_ref[pl.ds(row * half, half), pl.ds(col * half, half)] = value

    for side in range(2):
        across = block(side, 1)
        place(2 * side, 2 * side, block(side, 0))
        place(2 * side, 2 * side + 1, across)
        place(2 * side + 1, 2 * side, across.T)
        place(2 * side + 1, 2 * side + 1, block(side, 2))
        for col in (0, 1):
            part_of = block(side, 3 + col)
            place(side, 2 + col, part_of if side == 0 else part_of.T)

    gram = x_ref[:width, :width], x_ref[:width, width:], x_ref[width:, width:]
    squares = gram[0] * gram[0] + 2.0 * (gram[1] * gram[1]) + gram[2] * gram[2]
    norm = jnp.sqrt(jnp.sum(squares, keepdims=True))

    def set_x(x):
        put(x_pair, x, right=True)
        for i, value in enumerate(x):
            x_held[i] = value

    def two_sweeps(first=False, last=False):
        x = tuple(x_held[i] for i in range(3))
        q = product(x_pair, x_pair)
        put(q_pair, q)
        put(u_pair, combine((0.0625, q), (-0.5625, x), unit=1.6875), right=True)
        qu = product(q_pair, u_pair)
        x = tuple(x_held[i] for i in range(3))
        n = combine((1.0, qu), (-2.4375, x), unit=2.25)
        put(n_pair, n, right=True)
        if not last:
            put(v_pair, product(x_pair, n_pair))
        z = n if first else product(z_pair, n_pair)
        if last:
            return z
        put(z_pair, z)
        set_x(product(v_pair, n_pair))

    set_x(tuple(value / norm for value in gram))
    two_sweeps(first=True)

    def body(index, carry):
        two_sweeps()
        return carry

    lax.fori_loop(0, ITERS // 2 - 2, body, 0)
    first, across, second = two_sweeps(last=True)
    z_ref = x_ref
    z_ref[:width, :width] = first
    z_ref[:width, width:] = across
    z_ref[width:, :width] = across.T
    z_ref[width:, width:] = second
    own = pl.ds(pl.multiple_of(part * width, width), width)
    rotation = z_ref[:, own].astype(BF16)
    factor = jnp.sqrt(total_rows / norm)
    for copy in copies:
        copy.wait()
    count = wide.shape[0] // chunk
    outs = []
    for i in range(count):
        rows = pl.ds(i * chunk, chunk)
        result[rows, :] = (dot(wide[rows, :], rotation) * factor).astype(BF16)
        outs.append(pltpu.make_async_copy(result.at[rows], out_ref.at[rows], out_sem.at[i]))
        outs[-1].start()
    for out in outs:
        out.wait()


def rotate(info, mine, theirs, owns, others, total_rows):
    width = owns[0].shape[1]
    rows = sum(own.shape[0] for own in owns)
    size = 2 * width
    chunk = min(rows, 512)
    body = functools.partial(finish_kernel, float(total_rows), chunk)
    pair = pltpu.VMEM((2, size, size), BF16)
    return pl.pallas_call(
        body,
        in_specs=[SMEM, VMEM, VMEM] + [ANY] * 8,
        out_specs=ANY,
        out_shape=jax.ShapeDtypeStruct((rows, width), BF16),
        scratch_shapes=[
            pltpu.VMEM((size, size), F32),
            pltpu.VMEM((3, width, width), F32),
            pair, pair, pair, pair, pair, pair,
            pltpu.VMEM((rows, size), BF16),
            pltpu.VMEM((rows, width), BF16),
            pltpu.SemaphoreType.DMA((8,)),
            pltpu.SemaphoreType.DMA((rows // chunk,)),
        ],
        compiler_params=pltpu.CompilerParams(vmem_limit_bytes=28 * 1024 * 1024),
        cost_estimate=pl.CostEstimate(
            flops=21 * 6 * size**3 + 2 * rows * size * width,
            bytes_accessed=3 * rows * width * 2,
            transcendentals=0,
        ),
        name="rotate",
    )(info, mine, theirs, *owns, *others)


def after(value, *others):
    return lax.optimization_barrier((value, others))[0]


def on_device(vectors, blocks, tile_cols, live_tiles):
    tiles, _, tile, _ = blocks.shape
    width = vectors.shape[1]
    count = lax.axis_size("patch")
    pairs = {
        "even": [(i, i ^ 1) for i in range(count)],
        "odd": [(i, ((i + 1) ^ 1) - 1) for i in range(1, count - 1)],
    }

    def exchange(name, value):
        return lax.ppermute(value, "patch", pairs[name])

    def sibling(value):
        return lax.ppermute(value, "cols", [(0, 1), (1, 0)])

    start = vectors.reshape(tiles, tile, width)
    scalars = [lax.axis_index("cols"), lax.axis_index("patch"), live_tiles[0]]
    info = jnp.stack(scalars).astype(jnp.int32)

    cols = tile_cols.T

    even, odd = masked_edges(after(info, cols), start)
    even_halo = exchange("even", even)
    low, high, even_blocks, odd_blocks = load_fields(after(info, even), start, blocks)
    odd_halo = exchange("odd", after(odd, low))
    stored = {"even": even_blocks, "odd": odd_blocks}
    prev = dict.fromkeys(("even", "odd", "low", "high"))

    def rows(name, *pieces, cost=SMALL):
        return tile_rows(name, info, cols, stored[name], pieces, prev[name], cost)

    for step in range(STEPS):
        first, final = step == 0, step == STEPS - 1
        if final:
            new_low = rows("low", even, odd, low, high)
            new_high = rows("high", even, odd, low, high)
            even_halo = after(even_halo, new_low, new_high)
        new_even = rows("even", even_halo, even, low, high)
        if final:
            flat = [value.reshape(-1, width) for value in (new_even, new_low, new_high)]
            others = [sibling(value) for value in flat]
        else:
            even_halo = exchange("even", new_even)
        odd_halo = after(odd_halo, new_even)
        new_odd = rows("odd", odd_halo, odd, low, high, cost=LARGE if final else SMALL)
        if first:
            stored["low"], stored["high"] = load_blocks(after(info, new_odd), blocks)
            odd_halo = exchange("odd", after(new_odd, stored["low"]))
        if not final:
            held = after(even, new_odd)
            new_low = rows("low", held, odd, low, high)
            new_high = rows("high", held, odd, low, high)
            if not first:
                odd_halo = exchange("odd", after(new_odd, new_low, new_high))
        prev = {"even": even, "odd": odd, "low": low, "high": high}
        even, odd, low, high = new_even, new_odd, new_low, new_high
    last = odd.reshape(-1, width)
    other_last = sibling(last)
    others = [after(other, last) for other in others]
    share = gram_share(info, last, other_last, gram(flat, others))
    mine = sum_over_patch(info, share)
    theirs = sibling(mine)
    total_rows = tiles * tile * count
    return rotate(info, mine, theirs, flat + [last], others + [other_last], total_rows)


def solution(mesh):
    in_specs = (P("patch", "cols"), P("patch", None, None, None), P("patch", None), P("patch"))
    return jax.shard_map(
        on_device, mesh=mesh, in_specs=in_specs, out_specs=P("patch", "cols"), check_vma=False
    )
```

```python
import functools

import jax
import jax.numpy as jnp
from jax import lax
from jax.experimental import pallas as pl
from jax.experimental.pallas import tpu as pltpu
from jax.sharding import PartitionSpec as P

HALO_T = 4
STEPS = 3
ITERS = 8
WAYS = 4
LOAD_CUTS = 4
GROUP = 8

SMALL = pl.CostEstimate(flops=1000, bytes_accessed=1000, transcendentals=0)
LARGE = pl.CostEstimate(flops=10**11, bytes_accessed=1000, transcendentals=0)
SMALL_VMEM = pltpu.CompilerParams(vmem_limit_bytes=8 * 1024 * 1024)
ANY = pl.BlockSpec(memory_space=pl.ANY)
HBM = pl.BlockSpec(memory_space=pltpu.HBM)
VMEM = pl.BlockSpec(memory_space=pltpu.VMEM)
EDGES_MB, FIELDS_MB, BLOCKS_MB = 53, 50, 44
SMEM = pl.BlockSpec(memory_space=pltpu.SMEM)
F32, BF16 = jnp.float32, jnp.bfloat16


def dot(a, b):
    return jnp.dot(a, b, preferred_element_type=F32)


def tile_row(blocks, listed, field):
    wide = jnp.concatenate([blocks(n) for n in range(len(listed))], axis=1)
    tall = jnp.concatenate([field(tile) for tile in listed], axis=0)
    return dot(wide, tall)


def finish(acc, prev, alive):
    value = acc if prev is None else 2.0 * acc - prev.astype(F32)
    return jnp.where(alive, value, 0.0).astype(BF16)


def at_end(name):
    odd = lax.axis_index("patch") % 2
    return 1 - odd if name == "even" else odd


def live_count(table):
    return table[table.shape[0] - 1, 0]


def edges_kernel(table, whole_ref, even_ref, odd_ref, sem):
    edge, tiles = HALO_T, whole_ref.shape[0]
    outs = {"even": even_ref, "odd": odd_ref}
    firsts = {name: at_end(name) * (tiles - edge) for name in outs}
    load([(whole_ref, firsts[name], outs[name]) for name in outs], sem)
    for name in outs:
        clear_dead(outs[name], firsts[name], live_count(table))


def clear_dead(ref, first, live):
    def clear(index, carry):
        ref[index] = jnp.zeros(ref.shape[1:], BF16)
        return carry

    count = ref.shape[0]
    lax.fori_loop(jnp.clip(live - first, 0, count), count, clear, 0)


def load(moves, sem):
    copies = []
    for source, first, target in moves:
        count = target.shape[0] // LOAD_CUTS
        for cut in range(LOAD_CUTS):
            copies.append(
                pltpu.make_async_copy(
                    source.at[pl.ds(first + cut * count, count)],
                    target.at[pl.ds(cut * count, count)],
                    sem.at[len(copies)],
                )
            )
    for copy in copies:
        copy.start()
    for copy in copies:
        copy.wait()


def fields_kernel(table, whole_ref, blocks_ref, inner_ref, even_blocks, odd_blocks, sem):
    last = whole_ref.shape[0] - HALO_T
    moves = [
        (blocks_ref, at_end("even") * last, even_blocks),
        (blocks_ref, at_end("odd") * last, odd_blocks),
        (whole_ref, HALO_T, inner_ref),
    ]
    load(moves, sem)
    clear_dead(inner_ref, HALO_T, live_count(table))


def blocks_kernel(blocks_ref, inner_blocks, sem):
    load([(blocks_ref, HALO_T, inner_blocks)], sem)


def load_call(body, name, args, shapes, megabytes, table=()):
    return pl.pallas_call(
        body,
        in_specs=[SMEM] * len(table) + [HBM] * len(args),
        out_specs=[VMEM] * len(shapes),
        out_shape=shapes,
        scratch_shapes=[pltpu.SemaphoreType.DMA((len(shapes) * LOAD_CUTS,))],
        compiler_params=pltpu.CompilerParams(vmem_limit_bytes=megabytes * 1024 * 1024),
        cost_estimate=SMALL,
        name=name,
    )(*table, *args)


def masked_edges(table, start):
    shapes = [jax.ShapeDtypeStruct((HALO_T,) + start.shape[1:], BF16)] * 2
    return load_call(edges_kernel, "masked_edges", [start], shapes, EDGES_MB, [table])


def load_fields(table, start, blocks):
    inner = start.shape[0] - 2 * HALO_T
    shapes = [jax.ShapeDtypeStruct((inner,) + start.shape[1:], BF16)]
    shapes += [jax.ShapeDtypeStruct((HALO_T,) + blocks.shape[1:], blocks.dtype)] * 2
    return load_call(fields_kernel, "load_fields", [start, blocks], shapes, FIELDS_MB, [table])


def load_blocks(blocks):
    inner = blocks.shape[0] - 2 * HALO_T
    shapes = [jax.ShapeDtypeStruct((inner,) + blocks.shape[1:], blocks.dtype)]
    return load_call(blocks_kernel, "load_blocks", [blocks], shapes, BLOCKS_MB)[0]


def layout(name, tiles):
    edge, last = HALO_T, tiles - HALO_T
    if name == "inner":
        ends = [at_end(which) for which in ("even", "odd")]
        pieces = [(i, 0, edge, end * last) for i, end in enumerate(ends)]
        return edge, 0, pieces + [(2, 0, tiles - 2 * edge, edge)]
    end = at_end(name)
    pieces = [
        (0, 0, edge, 2 * edge * end), (1, 0, edge, edge), (2, 0, edge, (2 + end) * edge),
        (2, tiles - 3 * edge, edge, 3 * edge * (1 - end)),
    ]
    return end * last, end * last - edge, pieces


def rows_kernel(name, table_ref, *refs):
    sources, (out_ref, held, table, sem) = refs[:3], refs[-4:]
    blocks_ref = refs[-5]
    prev_ref = refs[3] if len(refs) == 9 else None
    fetch = pltpu.make_async_copy(table_ref, table, sem)
    fetch.start()
    nnz, tiles = blocks_ref.shape[1], table.shape[1]
    first, base, pieces = layout(name, tiles)
    for i, begin, count, slot in pieces:
        held[pl.ds(slot, count)] = sources[i][pl.ds(begin, count)]
    fetch.wait()
    live = live_count(table)
    shift = lax.axis_index("patch") * tiles + base
    rows = out_ref.shape[0]
    together = min(GROUP, rows)

    def group(index, carry):
        for r in range(together):
            row = index * together + r
            listed = [table[n, first + row] - shift for n in range(nnz)]
            acc = tile_row(lambda n: blocks_ref[row, n], listed, lambda c: held[c])
            prev = None if prev_ref is None else prev_ref[row]
            out_ref[row] = finish(acc, prev, first + row < live)
        return carry

    lax.fori_loop(0, rows // together, group, 0)


def tile_rows(name, table, blocks, sources, prev, cost):
    rows, _, tile, _ = blocks.shape
    width = sources[0].shape[-1]
    window = table.shape[1] if name == "inner" else 4 * HALO_T
    args = [table] + list(sources) + ([] if prev is None else [prev]) + [blocks]
    return pl.pallas_call(
        functools.partial(rows_kernel, name),
        in_specs=[VMEM] * len(args),
        out_specs=VMEM,
        out_shape=jax.ShapeDtypeStruct((rows, tile, width), BF16),
        scratch_shapes=[
            pltpu.VMEM((window, tile, width), BF16),
            pltpu.SMEM(table.shape, jnp.int32),
            pltpu.SemaphoreType.DMA,
        ],
        compiler_params=SMALL_VMEM,
        cost_estimate=cost,
        name="rows_" + name,
    )(*args)


ACROSS = (((0,), (0,)), ((), ()))


def add_gram(chunk, own_ref, other_ref, total):
    def add(index, carry):
        rows = pl.ds(pl.multiple_of(index * chunk, chunk), chunk)
        own = own_ref[rows, :]
        both = jnp.concatenate([own, other_ref[rows, :]], axis=1)
        total[...] += lax.dot_general(own, both, ACROSS, preferred_element_type=F32)
        return carry

    lax.fori_loop(0, own_ref.shape[0] // chunk, add, 0)


def gram_kernel(chunk, *refs):
    count = len(refs) // 2
    refs[-1][...] = jnp.zeros(refs[-1].shape, F32)
    for own_ref, other_ref in zip(refs[:count], refs[count:-1]):
        add_gram(chunk, own_ref, other_ref, refs[-1])


def share_kernel(chunk, own_ref, other_ref, start_ref, *refs):
    outs, (total, share) = refs[:WAYS], refs[WAYS:]
    total[...] = start_ref[...]
    add_gram(chunk, own_ref, other_ref, total)
    width = total.shape[0]
    half = width // 2
    own, other = total[:, :width], total[:, width:]
    first_core = lax.axis_index("cols") == 0
    second = jnp.where(first_core, other[:half, :half], other[:half, half:])
    third = jnp.where(first_core, other[:half, half:], other[half:, half:])
    blocks = [own[:half, :half], own[:half, half:], own[half:, half:], second, third]
    for i, block in enumerate(blocks):
        share[pl.ds(i * half, half), :] = block
    quarter = lax.axis_index("patch") % WAYS
    for d, out in enumerate(outs):
        rows = out.shape[0]
        out[...] = share[pl.ds(pl.multiple_of((quarter ^ d) * rows, 8), rows), :]


def gram_call(body, name, args, shape, scratch=(), outs=0):
    out_shape = jax.ShapeDtypeStruct(shape, F32)
    return pl.pallas_call(
        body,
        in_specs=[VMEM] * len(args),
        out_specs=[VMEM] * outs if outs else VMEM,
        out_shape=[out_shape] * outs if outs else out_shape,
        scratch_shapes=scratch,
        compiler_params=SMALL_VMEM,
        cost_estimate=SMALL,
        name=name,
    )(*args)


def gram(owns, others):
    chunk, width = min(own.shape[0] for own in owns), owns[0].shape[1]
    body = functools.partial(gram_kernel, chunk)
    return gram_call(body, "gram", owns + others, (width, 2 * width))


def gram_share(own, other, start):
    rows, width = own.shape
    half = width // 2
    body = functools.partial(share_kernel, rows)
    scratch = [pltpu.VMEM((width, 2 * width), F32), pltpu.VMEM((5 * half, half), F32)]
    shape = (5 * half // WAYS, half)
    args = [own, other, start]
    return gram_call(body, "gram_share", args, shape, scratch, outs=WAYS)


def add_kernel(a, b, c, d, out):
    out[...] = (a[...] + b[...]) + (c[...] + d[...])


def join_kernel(*refs):
    parts, out = refs[:-1], refs[-1]
    rows = parts[0].shape[0]
    quarter = lax.axis_index("patch") % WAYS
    for d, part in enumerate(parts):
        out[pl.ds(pl.multiple_of((quarter ^ d) * rows, 8), rows), :] = part[...]


def sum_over_patch(parts):
    count = lax.axis_size("patch")
    rows, columns = parts[0].shape

    def add_four(values):
        return gram_call(add_kernel, "add_four", values, (rows, columns))

    def from_others(values, stride=1):
        return [
            lax.ppermute(values[d], "patch", [(i, i ^ (d * stride)) for i in range(count)])
            for d in range(1, WAYS)
        ]

    total = add_four([parts[0]] + from_others(parts))
    stride = WAYS
    while stride < count:
        total = add_four([total] + from_others([total] * WAYS, stride))
        stride *= WAYS
    quarters = [total] + from_others([total] * WAYS)
    return gram_call(join_kernel, "join", quarters, (WAYS * rows, columns))


def split(value):
    high = value.astype(BF16)
    return high, (value - high.astype(F32)).astype(BF16)


def put(pair, blocks, right=False):
    width = blocks[0].shape[0]
    places = [(0, 0), (0, 1), (1, 1)]
    if right:
        blocks, places = tuple(blocks) + (blocks[1].T,), places + [(1, 0)]
    for (row, col), block in zip(places, blocks):
        for i, piece in enumerate(split(block)):
            pair[i, pl.ds(row * width, width), pl.ds(col * width, width)] = piece


def product3(left, right):
    rows = left[0].shape[0]
    both = dot(jnp.concatenate(left, axis=0), right[0])
    return both[:rows] + both[rows:] + dot(left[0], right[1])


def product(left, right):
    width = left.shape[1] // 2
    first = product3(
        (left[0, :width, :], left[1, :width, :]), (right[0], right[1])
    )
    second = product3(
        (right[0, width:, :], right[1, width:, :]), (left[0, :, width:], left[1, :, width:])
    )
    return first[:, :width], first[:, width:], second


def combine(*terms, unit=0.0):
    width = terms[0][1][0].shape[0]
    row = lax.broadcasted_iota(jnp.int32, (width, width), 0)
    col = lax.broadcasted_iota(jnp.int32, (width, width), 1)
    diagonal = jnp.where(row == col, unit, 0.0)
    out = []
    for i in range(3):
        value = functools.reduce(jnp.add, [factor * matrix[i] for factor, matrix in terms])
        out.append(value if i == 1 else value + diagonal)
    return tuple(out)


def finish_kernel(total_rows, chunk, mine, theirs, *refs):
    fields, out_ref = refs[:6], refs[6]
    x_ref, x_held, x_pair, q_pair, u_pair, n_pair, v_pair, z_pair = refs[7:15]
    wide, result, sem, out_sem = refs[15:]
    part = lax.axis_index("cols")
    size = x_ref.shape[0]
    width = size // 2
    half = width // 2
    edge_size = fields[0].shape[0]
    end = wide.shape[0] - edge_size
    starts = [at_end("even") * end, edge_size, at_end("odd") * end]
    copies = []
    for i, source in enumerate(fields):
        rows = pl.ds(pl.multiple_of(starts[i % 3], edge_size), source.shape[0])
        side = part if i < 3 else 1 - part
        target = wide.at[rows, pl.ds(pl.multiple_of(side * width, width), width)]
        copies.append(pltpu.make_async_copy(source, target, sem.at[i]))
    for copy in copies:
        copy.start()

    def block(side, index):
        rows = pl.ds(index * half, half)
        return jnp.where(part == side, mine[rows, :], theirs[rows, :])

    def place(row, col, value):
        x_ref[pl.ds(row * half, half), pl.ds(col * half, half)] = value

    for side in range(2):
        across = block(side, 1)
        place(2 * side, 2 * side, block(side, 0))
        place(2 * side, 2 * side + 1, across)
        place(2 * side + 1, 2 * side, across.T)
        place(2 * side + 1, 2 * side + 1, block(side, 2))
        for col in (0, 1):
            part_of = block(side, 3 + col)
            place(side, 2 + col, part_of if side == 0 else part_of.T)

    gram = x_ref[:width, :width], x_ref[:width, width:], x_ref[width:, width:]
    squares = gram[0] * gram[0] + 2.0 * (gram[1] * gram[1]) + gram[2] * gram[2]
    norm = jnp.sqrt(jnp.sum(squares, keepdims=True))

    def set_x(x):
        put(x_pair, x, right=True)
        for i, value in enumerate(x):
            x_held[i] = value

    def two_sweeps(first=False, last=False):
        x = tuple(x_held[i] for i in range(3))
        q = product(x_pair, x_pair)
        put(q_pair, q)
        put(u_pair, combine((0.0625, q), (-0.5625, x), unit=1.6875), right=True)
        qu = product(q_pair, u_pair)
        x = tuple(x_held[i] for i in range(3))
        n = combine((1.0, qu), (-2.4375, x), unit=2.25)
        put(n_pair, n, right=True)
        if not last:
            put(v_pair, product(x_pair, n_pair))
        z = n if first else product(z_pair, n_pair)
        if last:
            return z
        put(z_pair, z)
        set_x(product(v_pair, n_pair))

    set_x(tuple(value / norm for value in gram))
    two_sweeps(first=True)

    def body(index, carry):
        two_sweeps()
        return carry

    lax.fori_loop(0, ITERS // 2 - 2, body, 0)
    first, across, second = two_sweeps(last=True)
    z_ref = x_ref
    z_ref[:width, :width] = first
    z_ref[:width, width:] = across
    z_ref[width:, :width] = across.T
    z_ref[width:, width:] = second
    own = pl.ds(pl.multiple_of(part * width, width), width)
    rotation = z_ref[:, own].astype(BF16)
    factor = jnp.sqrt(total_rows / norm)
    for copy in copies:
        copy.wait()
    count = wide.shape[0] // chunk
    outs = []
    for i in range(count):
        rows = pl.ds(i * chunk, chunk)
        result[rows, :] = (dot(wide[rows, :], rotation) * factor).astype(BF16)
        outs.append(pltpu.make_async_copy(result.at[rows], out_ref.at[rows], out_sem.at[i]))
        outs[-1].start()
    for out in outs:
        out.wait()


def rotate(mine, theirs, owns, others, total_rows):
    width = owns[0].shape[1]
    rows = sum(own.shape[0] for own in owns)
    size = 2 * width
    chunk = min(rows, 512)
    body = functools.partial(finish_kernel, float(total_rows), chunk)
    pair = pltpu.VMEM((2, size, size), BF16)
    return pl.pallas_call(
        body,
        in_specs=[VMEM, VMEM] + [ANY] * 6,
        out_specs=ANY,
        out_shape=jax.ShapeDtypeStruct((rows, width), BF16),
        scratch_shapes=[
            pltpu.VMEM((size, size), F32),
            pltpu.VMEM((3, width, width), F32),
            pair, pair, pair, pair, pair, pair,
            pltpu.VMEM((rows, size), BF16),
            pltpu.VMEM((rows, width), BF16),
            pltpu.SemaphoreType.DMA((6,)),
            pltpu.SemaphoreType.DMA((rows // chunk,)),
        ],
        compiler_params=pltpu.CompilerParams(vmem_limit_bytes=28 * 1024 * 1024),
        cost_estimate=pl.CostEstimate(
            flops=21 * 6 * size**3 + 2 * rows * size * width,
            bytes_accessed=3 * rows * width * 2,
            transcendentals=0,
        ),
        name="rotate",
    )(mine, theirs, *owns, *others)


def after(value, *others):
    return lax.optimization_barrier((value, others))[0]


def on_device(vectors, blocks, tile_cols, live_tiles):
    tiles, _, tile, _ = blocks.shape
    width = vectors.shape[1]
    count = lax.axis_size("patch")
    pairs = {
        "even": [(i, i ^ 1) for i in range(count)],
        "odd": [(i, ((i + 1) ^ 1) - 1) for i in range(1, count - 1)],
    }

    def exchange(name, value):
        return lax.ppermute(value, "patch", pairs[name])

    def sibling(value):
        return lax.ppermute(value, "cols", [(0, 1), (1, 0)])

    start = vectors.reshape(tiles, tile, width)
    table = jnp.concatenate([tile_cols.T, jnp.broadcast_to(live_tiles[None], (1, tiles))])

    even, odd = masked_edges(table, start)
    even_halo = exchange("even", even)
    inner, even_blocks, odd_blocks = load_fields(after(table, even), start, blocks)
    odd_halo = exchange("odd", after(odd, inner))
    stored = {"even": even_blocks, "odd": odd_blocks}
    prev = dict.fromkeys(("even", "odd", "inner"))

    def rows(name, *sources, cost=SMALL):
        return tile_rows(name, table, stored[name], sources, prev[name], cost)

    for step in range(STEPS):
        first, final = step == 0, step == STEPS - 1
        if final:
            new_inner = rows("inner", even, odd, inner)
            even_halo = after(even_halo, new_inner)
        new_even = rows("even", even_halo, even, inner)
        if final:
            flat = [value.reshape(-1, width) for value in (new_even, new_inner)]
            others = [sibling(value) for value in flat]
        else:
            even_halo = exchange("even", new_even)
        if first:
            stored["inner"] = load_blocks(after(blocks, new_even))
            odd_halo = after(odd_halo, stored["inner"])
        odd_halo = after(odd_halo, new_even)
        new_odd = rows("odd", odd_halo, odd, inner, cost=LARGE if final else SMALL)
        if not final:
            odd_halo = exchange("odd", new_odd)
            new_inner = rows("inner", after(even, new_odd), odd, inner)
            even_halo = after(even_halo, new_inner)
        prev = {"even": even, "odd": odd, "inner": inner}
        even, odd, inner = new_even, new_odd, new_inner
    last = odd.reshape(-1, width)
    other_last = sibling(last)
    others = [after(other, last) for other in others]
    mine = sum_over_patch(gram_share(last, other_last, gram(flat, others)))
    theirs = sibling(mine)
    total_rows = tiles * tile * count
    return rotate(mine, theirs, flat + [last], others + [other_last], total_rows)


def solution(mesh):
    in_specs = (P("patch", "cols"), P("patch", None, None, None), P("patch", None), P("patch"))
    return jax.shard_map(
        on_device, mesh=mesh, in_specs=in_specs, out_specs=P("patch", "cols"), check_vma=False
    )
```

```python
import functools

import jax
import jax.numpy as jnp
from jax import lax
from jax.experimental import pallas as pl
from jax.experimental.pallas import tpu as pltpu
from jax.sharding import PartitionSpec as P

HALO_T = 4
STEPS = 3
ITERS = 8
WAYS = 4
LOAD_CUTS = 4
GRAM_ROWS = 1024
GROUP = 8

SMALL = pl.CostEstimate(flops=1000, bytes_accessed=1000, transcendentals=0)
LARGE = pl.CostEstimate(flops=10**11, bytes_accessed=1000, transcendentals=0)
SMALL_VMEM = pltpu.CompilerParams(vmem_limit_bytes=8 * 1024 * 1024)
ANY = pl.BlockSpec(memory_space=pl.ANY)
HBM = pl.BlockSpec(memory_space=pltpu.HBM)
VMEM = pl.BlockSpec(memory_space=pltpu.VMEM)
EDGES_MB, FIELDS_MB, BLOCKS_MB = 53, 50, 44
SMEM = pl.BlockSpec(memory_space=pltpu.SMEM)
F32, BF16 = jnp.float32, jnp.bfloat16


def dot(a, b):
    return jnp.dot(a, b, preferred_element_type=F32)


def tile_row(blocks, listed, field):
    wide = jnp.concatenate([blocks(n) for n in range(len(listed))], axis=1)
    tall = jnp.concatenate([field(tile) for tile in listed], axis=0)
    return dot(wide, tall)


def finish(acc, prev, alive):
    value = acc if prev is None else 2.0 * acc - prev.astype(F32)
    return jnp.where(alive, value, 0.0).astype(BF16)


def at_end(name):
    odd = lax.axis_index("patch") % 2
    return 1 - odd if name == "even" else odd


def live_count(table):
    return table[table.shape[0] - 1, 0]


def edges_kernel(table, whole_ref, even_ref, odd_ref, sem):
    edge, tiles = HALO_T, whole_ref.shape[0]
    outs = {"even": even_ref, "odd": odd_ref}
    firsts = {name: at_end(name) * (tiles - edge) for name in outs}
    load([(whole_ref, firsts[name], outs[name]) for name in outs], sem)
    for name in outs:
        clear_dead(outs[name], firsts[name], live_count(table))


def clear_dead(ref, first, live):
    def clear(index, carry):
        ref[index] = jnp.zeros(ref.shape[1:], BF16)
        return carry

    count = ref.shape[0]
    lax.fori_loop(jnp.clip(live - first, 0, count), count, clear, 0)


def load(moves, sem):
    copies = []
    for source, first, target in moves:
        count = target.shape[0] // LOAD_CUTS
        for cut in range(LOAD_CUTS):
            copies.append(
                pltpu.make_async_copy(
                    source.at[pl.ds(first + cut * count, count)],
                    target.at[pl.ds(cut * count, count)],
                    sem.at[len(copies)],
                )
            )
    for copy in copies:
        copy.start()
    for copy in copies:
        copy.wait()


def fields_kernel(table, whole_ref, blocks_ref, inner_ref, even_blocks, odd_blocks, sem):
    last = whole_ref.shape[0] - HALO_T
    moves = [
        (blocks_ref, at_end("even") * last, even_blocks),
        (blocks_ref, at_end("odd") * last, odd_blocks),
        (whole_ref, HALO_T, inner_ref),
    ]
    load(moves, sem)
    clear_dead(inner_ref, HALO_T, live_count(table))


def blocks_kernel(blocks_ref, inner_blocks, sem):
    load([(blocks_ref, HALO_T, inner_blocks)], sem)


def load_call(body, name, args, shapes, megabytes, table=()):
    return pl.pallas_call(
        body,
        in_specs=[SMEM] * len(table) + [HBM] * len(args),
        out_specs=[VMEM] * len(shapes),
        out_shape=shapes,
        scratch_shapes=[pltpu.SemaphoreType.DMA((len(shapes) * LOAD_CUTS,))],
        compiler_params=pltpu.CompilerParams(vmem_limit_bytes=megabytes * 1024 * 1024),
        cost_estimate=SMALL,
        name=name,
    )(*table, *args)


def masked_edges(table, start):
    shapes = [jax.ShapeDtypeStruct((HALO_T,) + start.shape[1:], BF16)] * 2
    return load_call(edges_kernel, "masked_edges", [start], shapes, EDGES_MB, [table])


def load_fields(table, start, blocks):
    inner = start.shape[0] - 2 * HALO_T
    shapes = [jax.ShapeDtypeStruct((inner,) + start.shape[1:], BF16)]
    shapes += [jax.ShapeDtypeStruct((HALO_T,) + blocks.shape[1:], blocks.dtype)] * 2
    return load_call(fields_kernel, "load_fields", [start, blocks], shapes, FIELDS_MB, [table])


def load_blocks(blocks):
    inner = blocks.shape[0] - 2 * HALO_T
    shapes = [jax.ShapeDtypeStruct((inner,) + blocks.shape[1:], blocks.dtype)]
    return load_call(blocks_kernel, "load_blocks", [blocks], shapes, BLOCKS_MB)[0]


def layout(name, tiles):
    edge, last = HALO_T, tiles - HALO_T
    if name == "inner":
        ends = [at_end(which) for which in ("even", "odd")]
        pieces = [(i, 0, edge, end * last) for i, end in enumerate(ends)]
        return edge, 0, pieces + [(2, 0, tiles - 2 * edge, edge)]
    end = at_end(name)
    pieces = [
        (0, 0, edge, 2 * edge * end), (1, 0, edge, edge), (2, 0, edge, (2 + end) * edge),
        (2, tiles - 3 * edge, edge, 3 * edge * (1 - end)),
    ]
    return end * last, end * last - edge, pieces


def rows_kernel(name, table_ref, *refs):
    sources, (out_ref, held, table, sem) = refs[:3], refs[-4:]
    blocks_ref = refs[-5]
    prev_ref = refs[3] if len(refs) == 9 else None
    fetch = pltpu.make_async_copy(table_ref, table, sem)
    fetch.start()
    nnz, tiles = blocks_ref.shape[1], table.shape[1]
    first, base, pieces = layout(name, tiles)
    for i, begin, count, slot in pieces:
        held[pl.ds(slot, count)] = sources[i][pl.ds(begin, count)]
    fetch.wait()
    live = live_count(table)
    shift = lax.axis_index("patch") * tiles + base
    rows = out_ref.shape[0]
    together = min(GROUP, rows)

    def group(index, carry):
        for r in range(together):
            row = index * together + r
            listed = [table[n, first + row] - shift for n in range(nnz)]
            acc = tile_row(lambda n: blocks_ref[row, n], listed, lambda c: held[c])
            prev = None if prev_ref is None else prev_ref[row]
            out_ref[row] = finish(acc, prev, first + row < live)
        return carry

    lax.fori_loop(0, rows // together, group, 0)


def tile_rows(name, table, blocks, sources, prev, cost):
    rows, _, tile, _ = blocks.shape
    width = sources[0].shape[-1]
    window = table.shape[1] if name == "inner" else 4 * HALO_T
    args = [table] + list(sources) + ([] if prev is None else [prev]) + [blocks]
    return pl.pallas_call(
        functools.partial(rows_kernel, name),
        in_specs=[VMEM] * len(args),
        out_specs=VMEM,
        out_shape=jax.ShapeDtypeStruct((rows, tile, width), BF16),
        scratch_shapes=[
            pltpu.VMEM((window, tile, width), BF16),
            pltpu.SMEM(table.shape, jnp.int32),
            pltpu.SemaphoreType.DMA,
        ],
        compiler_params=SMALL_VMEM,
        cost_estimate=cost,
        name="rows_" + name,
    )(*args)


ACROSS = (((0,), (0,)), ((), ()))


def add_gram(chunk, own_ref, other_ref, total):
    chunk = min(chunk, own_ref.shape[0])

    def add(index, carry):
        rows = pl.ds(pl.multiple_of(index * chunk, chunk), chunk)
        own = own_ref[rows, :]
        both = jnp.concatenate([own, other_ref[rows, :]], axis=1)
        total[...] += lax.dot_general(own, both, ACROSS, preferred_element_type=F32)
        return carry

    lax.fori_loop(0, own_ref.shape[0] // chunk, add, 0)


def gram_kernel(chunk, *refs):
    count = len(refs) // 2
    refs[-1][...] = jnp.zeros(refs[-1].shape, F32)
    for own_ref, other_ref in zip(refs[:count], refs[count:-1]):
        add_gram(chunk, own_ref, other_ref, refs[-1])


def share_kernel(chunk, own_ref, other_ref, start_ref, *refs):
    share, total = refs
    total[...] = start_ref[...]
    add_gram(chunk, own_ref, other_ref, total)
    width = total.shape[0]
    half = width // 2
    own, other = total[:, :width], total[:, width:]
    first_core = lax.axis_index("cols") == 0
    second = jnp.where(first_core, other[:half, :half], other[:half, half:])
    third = jnp.where(first_core, other[:half, half:], other[half:, half:])
    blocks = [own[:half, :half], own[:half, half:], own[half:, half:], second, third]
    for i, block in enumerate(blocks):
        share[pl.ds(i * half, half), :] = block


def gram_call(body, name, args, shape, scratch=(), outs=0):
    out_shape = jax.ShapeDtypeStruct(shape, F32)
    return pl.pallas_call(
        body,
        in_specs=[VMEM] * len(args),
        out_specs=[VMEM] * outs if outs else VMEM,
        out_shape=[out_shape] * outs if outs else out_shape,
        scratch_shapes=scratch,
        compiler_params=SMALL_VMEM,
        cost_estimate=SMALL,
        name=name,
    )(*args)


def gram(owns, others):
    width = owns[0].shape[1]
    body = functools.partial(gram_kernel, GRAM_ROWS)
    return gram_call(body, "gram", owns + others, (width, 2 * width))


def gram_share(own, other, start):
    rows, width = own.shape
    half = width // 2
    body = functools.partial(share_kernel, rows)
    scratch = [pltpu.VMEM((width, 2 * width), F32)]
    return gram_call(body, "gram_share", [own, other, start], (5 * half, half), scratch)


def add_kernel(*refs):
    parts = [ref[...] for ref in refs[:-1]]
    if len(parts) == 1:
        parts = [parts[0][i] for i in range(WAYS)]
    refs[-1][...] = (parts[0] + parts[1]) + (parts[2] + parts[3])


def join_kernel(*refs):
    parts, out = refs[:-1], refs[-1]
    rows = parts[0].shape[0]
    quarter = lax.axis_index("patch") % WAYS
    for d, part in enumerate(parts):
        out[pl.ds(pl.multiple_of((quarter ^ d) * rows, 8), rows), :] = part[...]


def sum_over_patch(share):
    count = lax.axis_size("patch")
    columns = share.shape[1]
    parts = share.reshape(WAYS, -1, columns)
    rows = parts.shape[1]

    def add_four(values):
        return gram_call(add_kernel, "add_four", values, (rows, columns))

    def from_others(value, stride=1):
        return [
            lax.ppermute(value, "patch", [(i, i ^ (d * stride)) for i in range(count)])
            for d in range(1, WAYS)
        ]

    groups = [list(range(i, i + WAYS)) for i in range(0, count, WAYS)]
    total = add_four(
        [lax.all_to_all(parts, "patch", 0, 0, axis_index_groups=groups, tiled=True)]
    )
    stride = WAYS
    while stride < count:
        total = add_four([total] + from_others(total, stride))
        stride *= WAYS
    quarters = [total] + from_others(total)
    return gram_call(join_kernel, "join", quarters, (WAYS * rows, columns))


def split(value):
    high = value.astype(BF16)
    return high, (value - high.astype(F32)).astype(BF16)


def put(pair, blocks, right=False):
    width = blocks[0].shape[0]
    places = [(0, 0), (0, 1), (1, 1)]
    if right:
        blocks, places = tuple(blocks) + (blocks[1].T,), places + [(1, 0)]
    for (row, col), block in zip(places, blocks):
        for i, piece in enumerate(split(block)):
            pair[i, pl.ds(row * width, width), pl.ds(col * width, width)] = piece


def product3(left, right):
    return dot(
        jnp.concatenate([left[0], left[0], left[1]], axis=1),
        jnp.concatenate([right[0], right[1], right[0]], axis=0),
    )


def product(left, right):
    width = left.shape[1] // 2
    first = product3(
        (left[0, :width, :], left[1, :width, :]), (right[0], right[1])
    )
    second = product3(
        (right[0, width:, :], right[1, width:, :]), (left[0, :, width:], left[1, :, width:])
    )
    return first[:, :width], first[:, width:], second


def combine(*terms, unit=0.0):
    width = terms[0][1][0].shape[0]
    row = lax.broadcasted_iota(jnp.int32, (width, width), 0)
    col = lax.broadcasted_iota(jnp.int32, (width, width), 1)
    diagonal = jnp.where(row == col, unit, 0.0)
    out = []
    for i in range(3):
        value = functools.reduce(jnp.add, [factor * matrix[i] for factor, matrix in terms])
        out.append(value if i == 1 else value + diagonal)
    return tuple(out)


def finish_kernel(total_rows, chunk, mine, theirs, *refs):
    fields, out_ref = refs[:6], refs[6]
    x_ref, x_held, x_pair, q_pair, u_pair, n_pair, v_pair, z_pair = refs[7:15]
    wide, result, sem, out_sem = refs[15:]
    part = lax.axis_index("cols")
    size = x_ref.shape[0]
    width = size // 2
    half = width // 2
    edge_size = fields[0].shape[0]
    end = wide.shape[0] - edge_size
    starts = [at_end("even") * end, edge_size, at_end("odd") * end]
    copies = []
    for i, source in enumerate(fields):
        rows = pl.ds(pl.multiple_of(starts[i % 3], edge_size), source.shape[0])
        side = part if i < 3 else 1 - part
        target = wide.at[rows, pl.ds(pl.multiple_of(side * width, width), width)]
        copies.append(pltpu.make_async_copy(source, target, sem.at[i]))
    for copy in copies:
        copy.start()

    def block(side, index):
        rows = pl.ds(index * half, half)
        return jnp.where(part == side, mine[rows, :], theirs[rows, :])

    def place(row, col, value):
        x_ref[pl.ds(row * half, half), pl.ds(col * half, half)] = value

    for side in range(2):
        across = block(side, 1)
        place(2 * side, 2 * side, block(side, 0))
        place(2 * side, 2 * side + 1, across)
        place(2 * side + 1, 2 * side, across.T)
        place(2 * side + 1, 2 * side + 1, block(side, 2))
        for col in (0, 1):
            part_of = block(side, 3 + col)
            place(side, 2 + col, part_of if side == 0 else part_of.T)

    gram = x_ref[:width, :width], x_ref[:width, width:], x_ref[width:, width:]
    squares = gram[0] * gram[0] + 2.0 * (gram[1] * gram[1]) + gram[2] * gram[2]
    norm = jnp.sqrt(jnp.sum(squares, keepdims=True))

    def set_x(x):
        put(x_pair, x, right=True)
        for i, value in enumerate(x):
            x_held[i] = value

    def two_sweeps(first=False, last=False):
        x = tuple(x_held[i] for i in range(3))
        q = product(x_pair, x_pair)
        put(q_pair, q)
        put(u_pair, combine((0.0625, q), (-0.5625, x), unit=1.6875), right=True)
        qu = product(q_pair, u_pair)
        x = tuple(x_held[i] for i in range(3))
        n = combine((1.0, qu), (-2.4375, x), unit=2.25)
        put(n_pair, n, right=True)
        if not last:
            put(v_pair, product(x_pair, n_pair))
        z = n if first else product(z_pair, n_pair)
        if last:
            return z
        put(z_pair, z)
        set_x(product(v_pair, n_pair))

    set_x(tuple(value / norm for value in gram))
    two_sweeps(first=True)

    def body(index, carry):
        two_sweeps()
        return carry

    lax.fori_loop(0, ITERS // 2 - 2, body, 0)
    first, across, second = two_sweeps(last=True)
    z_ref = x_ref
    z_ref[:width, :width] = first
    z_ref[:width, width:] = across
    z_ref[width:, :width] = across.T
    z_ref[width:, width:] = second
    own = pl.ds(pl.multiple_of(part * width, width), width)
    rotation = z_ref[:, own].astype(BF16)
    factor = jnp.sqrt(total_rows / norm)
    for copy in copies:
        copy.wait()
    count = wide.shape[0] // chunk
    outs = []
    for i in range(count):
        rows = pl.ds(i * chunk, chunk)
        result[rows, :] = (dot(wide[rows, :], rotation) * factor).astype(BF16)
        outs.append(pltpu.make_async_copy(result.at[rows], out_ref.at[rows], out_sem.at[i]))
        outs[-1].start()
    for out in outs:
        out.wait()


def rotate(mine, theirs, owns, others, total_rows):
    width = owns[0].shape[1]
    rows = sum(own.shape[0] for own in owns)
    size = 2 * width
    chunk = min(rows, 512)
    body = functools.partial(finish_kernel, float(total_rows), chunk)
    pair = pltpu.VMEM((2, size, size), BF16)
    return pl.pallas_call(
        body,
        in_specs=[VMEM, VMEM] + [ANY] * 6,
        out_specs=ANY,
        out_shape=jax.ShapeDtypeStruct((rows, width), BF16),
        scratch_shapes=[
            pltpu.VMEM((size, size), F32),
            pltpu.VMEM((3, width, width), F32),
            pair, pair, pair, pair, pair, pair,
            pltpu.VMEM((rows, size), BF16),
            pltpu.VMEM((rows, width), BF16),
            pltpu.SemaphoreType.DMA((6,)),
            pltpu.SemaphoreType.DMA((rows // chunk,)),
        ],
        compiler_params=pltpu.CompilerParams(vmem_limit_bytes=28 * 1024 * 1024),
        cost_estimate=pl.CostEstimate(
            flops=21 * 6 * size**3 + 2 * rows * size * width,
            bytes_accessed=3 * rows * width * 2,
            transcendentals=0,
        ),
        name="rotate",
    )(mine, theirs, *owns, *others)


def after(value, *others):
    return lax.optimization_barrier((value, others))[0]


def on_device(vectors, blocks, tile_cols, live_tiles):
    tiles, _, tile, _ = blocks.shape
    width = vectors.shape[1]
    count = lax.axis_size("patch")
    pairs = {
        "even": [(i, i ^ 1) for i in range(count)],
        "odd": [(i, ((i + 1) ^ 1) - 1) for i in range(1, count - 1)],
    }

    def exchange(name, value):
        return lax.ppermute(value, "patch", pairs[name])

    def sibling(value):
        return lax.ppermute(value, "cols", [(0, 1), (1, 0)])

    start = vectors.reshape(tiles, tile, width)
    table = jnp.concatenate([tile_cols.T, jnp.broadcast_to(live_tiles[None], (1, tiles))])

    even, odd = masked_edges(table, start)
    even_halo = exchange("even", even)
    inner, even_blocks, odd_blocks = load_fields(after(table, even), start, blocks)
    odd_halo = exchange("odd", after(odd, inner))
    stored = {"even": even_blocks, "odd": odd_blocks}
    prev = dict.fromkeys(("even", "odd", "inner"))

    def rows(name, *sources, cost=SMALL):
        return tile_rows(name, table, stored[name], sources, prev[name], cost)

    for step in range(STEPS):
        final = step == STEPS - 1
        if final:
            new_inner = rows("inner", even, odd, inner)
            even_halo = after(even_halo, new_inner)
        new_even = rows("even", even_halo, even, inner)
        if final:
            flat = [value.reshape(-1, width) for value in (new_even, new_inner)]
            others = [sibling(value) for value in flat]
            odd_halo = after(odd_halo, new_even)
        else:
            even_halo = exchange("even", new_even)
            if step == 0:
                stored["inner"] = load_blocks(after(blocks, new_even))
            new_inner = rows("inner", after(even, new_even), odd, inner)
            odd_halo = after(odd_halo, new_inner)
        new_odd = rows("odd", odd_halo, odd, inner, cost=LARGE if final else SMALL)
        if not final:
            odd_halo = exchange("odd", new_odd)
            even_halo = after(even_halo, new_odd)
        prev = {"even": even, "odd": odd, "inner": inner}
        even, odd, inner = new_even, new_odd, new_inner
    last = odd.reshape(-1, width)
    other_last = sibling(last)
    others = [after(other, last) for other in others]
    mine = sum_over_patch(gram_share(last, other_last, gram(flat, others)))
    theirs = sibling(mine)
    total_rows = tiles * tile * count
    return rotate(mine, theirs, flat + [last], others + [other_last], total_rows)


def solution(mesh):
    in_specs = (P("patch", "cols"), P("patch", None, None, None), P("patch", None), P("patch"))
    return jax.shard_map(
        on_device, mesh=mesh, in_specs=in_specs, out_specs=P("patch", "cols"), check_vma=False
    )
```

```python
import functools

import jax
import jax.numpy as jnp
from jax import lax
from jax.experimental import pallas as pl
from jax.experimental.pallas import tpu as pltpu
from jax.sharding import PartitionSpec as P

HALO_T = 4
STEPS = 3
ITERS = 8
WAYS = 4
LOAD_CUTS = 4
GRAM_ROWS = 1024
GROUP = 8

SMALL = pl.CostEstimate(flops=1000, bytes_accessed=1000, transcendentals=0)
LARGE = pl.CostEstimate(flops=10**11, bytes_accessed=1000, transcendentals=0)
SMALL_VMEM = pltpu.CompilerParams(vmem_limit_bytes=8 * 1024 * 1024)
ANY = pl.BlockSpec(memory_space=pl.ANY)
HBM = pl.BlockSpec(memory_space=pltpu.HBM)
VMEM = pl.BlockSpec(memory_space=pltpu.VMEM)
EDGES_MB, FIELDS_MB, BLOCKS_MB = 53, 50, 44
SMEM = pl.BlockSpec(memory_space=pltpu.SMEM)
F32, BF16 = jnp.float32, jnp.bfloat16


def dot(a, b):
    return jnp.dot(a, b, preferred_element_type=F32)


def tile_row(blocks, listed, field):
    wide = jnp.concatenate([blocks(n) for n in range(len(listed))], axis=1)
    tall = jnp.concatenate([field(tile) for tile in listed], axis=0)
    return dot(wide, tall)


def finish(acc, prev, alive):
    value = acc if prev is None else 2.0 * acc - prev.astype(F32)
    return jnp.where(alive, value, 0.0).astype(BF16)


def at_end(name):
    odd = lax.axis_index("patch") % 2
    return 1 - odd if name == "even" else odd


def live_count(table):
    return table[table.shape[0] - 1, 0]


def edges_kernel(table, whole_ref, even_ref, odd_ref, sem):
    edge, tiles = HALO_T, whole_ref.shape[0]
    outs = {"even": even_ref, "odd": odd_ref}
    firsts = {name: at_end(name) * (tiles - edge) for name in outs}
    load([(whole_ref, firsts[name], outs[name]) for name in outs], sem)
    for name in outs:
        clear_dead(outs[name], firsts[name], live_count(table))


def clear_dead(ref, first, live):
    def clear(index, carry):
        ref[index] = jnp.zeros(ref.shape[1:], BF16)
        return carry

    count = ref.shape[0]
    lax.fori_loop(jnp.clip(live - first, 0, count), count, clear, 0)


def load(moves, sem):
    copies = []
    for source, first, target in moves:
        count = target.shape[0] // LOAD_CUTS
        for cut in range(LOAD_CUTS):
            copies.append(
                pltpu.make_async_copy(
                    source.at[pl.ds(first + cut * count, count)],
                    target.at[pl.ds(cut * count, count)],
                    sem.at[len(copies)],
                )
            )
    for copy in copies:
        copy.start()
    for copy in copies:
        copy.wait()


def fields_kernel(table, whole_ref, blocks_ref, inner_ref, even_blocks, odd_blocks, sem):
    last = whole_ref.shape[0] - HALO_T
    moves = [
        (blocks_ref, at_end("even") * last, even_blocks),
        (blocks_ref, at_end("odd") * last, odd_blocks),
        (whole_ref, HALO_T, inner_ref),
    ]
    load(moves, sem)
    clear_dead(inner_ref, HALO_T, live_count(table))


def blocks_kernel(blocks_ref, inner_blocks, sem):
    load([(blocks_ref, HALO_T, inner_blocks)], sem)


def load_call(body, name, args, shapes, megabytes, table=()):
    return pl.pallas_call(
        body,
        in_specs=[SMEM] * len(table) + [HBM] * len(args),
        out_specs=[VMEM] * len(shapes),
        out_shape=shapes,
        scratch_shapes=[pltpu.SemaphoreType.DMA((len(shapes) * LOAD_CUTS,))],
        compiler_params=pltpu.CompilerParams(vmem_limit_bytes=megabytes * 1024 * 1024),
        cost_estimate=SMALL,
        name=name,
    )(*table, *args)


def masked_edges(table, start):
    shapes = [jax.ShapeDtypeStruct((HALO_T,) + start.shape[1:], BF16)] * 2
    return load_call(edges_kernel, "masked_edges", [start], shapes, EDGES_MB, [table])


def load_fields(table, start, blocks):
    inner = start.shape[0] - 2 * HALO_T
    shapes = [jax.ShapeDtypeStruct((inner,) + start.shape[1:], BF16)]
    shapes += [jax.ShapeDtypeStruct((HALO_T,) + blocks.shape[1:], blocks.dtype)] * 2
    return load_call(fields_kernel, "load_fields", [start, blocks], shapes, FIELDS_MB, [table])


def load_blocks(blocks):
    inner = blocks.shape[0] - 2 * HALO_T
    shapes = [jax.ShapeDtypeStruct((inner,) + blocks.shape[1:], blocks.dtype)]
    return load_call(blocks_kernel, "load_blocks", [blocks], shapes, BLOCKS_MB)[0]


def layout(name, tiles):
    edge, last = HALO_T, tiles - HALO_T
    if name == "inner":
        ends = [at_end(which) for which in ("even", "odd")]
        pieces = [(i, 0, edge, end * last) for i, end in enumerate(ends)]
        return edge, 0, pieces + [(2, 0, tiles - 2 * edge, edge)]
    end = at_end(name)
    pieces = [
        (0, 0, edge, 2 * edge * end), (1, 0, edge, edge), (2, 0, edge, (2 + end) * edge),
        (2, tiles - 3 * edge, edge, 3 * edge * (1 - end)),
    ]
    return end * last, end * last - edge, pieces


def rows_kernel(name, table_ref, *refs):
    sources, (out_ref, held, table, sem) = refs[:3], refs[-4:]
    blocks_ref = refs[-5]
    prev_ref = refs[3] if len(refs) == 9 else None
    fetch = pltpu.make_async_copy(table_ref, table, sem)
    fetch.start()
    nnz, tiles = blocks_ref.shape[1], table.shape[1]
    first, base, pieces = layout(name, tiles)
    for i, begin, count, slot in pieces:
        held[pl.ds(slot, count)] = sources[i][pl.ds(begin, count)]
    fetch.wait()
    live = live_count(table)
    shift = lax.axis_index("patch") * tiles + base
    rows = out_ref.shape[0]
    together = min(GROUP, rows)

    def group(index, carry):
        for r in range(together):
            row = index * together + r
            listed = [table[n, first + row] - shift for n in range(nnz)]
            acc = tile_row(lambda n: blocks_ref[row, n], listed, lambda c: held[c])
            prev = None if prev_ref is None else prev_ref[row]
            out_ref[row] = finish(acc, prev, first + row < live)
        return carry

    lax.fori_loop(0, rows // together, group, 0)


def tile_rows(name, table, blocks, sources, prev, cost):
    rows, _, tile, _ = blocks.shape
    width = sources[0].shape[-1]
    window = table.shape[1] if name == "inner" else 4 * HALO_T
    args = [table] + list(sources) + ([] if prev is None else [prev]) + [blocks]
    return pl.pallas_call(
        functools.partial(rows_kernel, name),
        in_specs=[VMEM] * len(args),
        out_specs=VMEM,
        out_shape=jax.ShapeDtypeStruct((rows, tile, width), BF16),
        scratch_shapes=[
            pltpu.VMEM((window, tile, width), BF16),
            pltpu.SMEM(table.shape, jnp.int32),
            pltpu.SemaphoreType.DMA,
        ],
        compiler_params=SMALL_VMEM,
        cost_estimate=cost,
        name="rows_" + name,
    )(*args)


ACROSS = (((0,), (0,)), ((), ()))


def add_gram(chunk, own_ref, other_ref, total):
    chunk = min(chunk, own_ref.shape[0])

    def add(index, carry):
        rows = pl.ds(pl.multiple_of(index * chunk, chunk), chunk)
        own = own_ref[rows, :]
        both = jnp.concatenate([own, other_ref[rows, :]], axis=1)
        total[...] += lax.dot_general(own, both, ACROSS, preferred_element_type=F32)
        return carry

    lax.fori_loop(0, own_ref.shape[0] // chunk, add, 0)


def gram_kernel(chunk, *refs):
    count = len(refs) // 2
    refs[-1][...] = jnp.zeros(refs[-1].shape, F32)
    for own_ref, other_ref in zip(refs[:count], refs[count:-1]):
        add_gram(chunk, own_ref, other_ref, refs[-1])


def share_kernel(chunk, own_ref, other_ref, start_ref, *refs):
    outs, (total, share) = refs[:WAYS], refs[WAYS:]
    total[...] = start_ref[...]
    add_gram(chunk, own_ref, other_ref, total)
    width = total.shape[0]
    half = width // 2
    own, other = total[:, :width], total[:, width:]
    first_core = lax.axis_index("cols") == 0
    second = jnp.where(first_core, other[:half, :half], other[:half, half:])
    third = jnp.where(first_core, other[:half, half:], other[half:, half:])
    blocks = [own[:half, :half], own[:half, half:], own[half:, half:], second, third]
    for i, block in enumerate(blocks):
        share[pl.ds(i * half, half), :] = block
    quarter = lax.axis_index("patch") % WAYS
    for d, out in enumerate(outs):
        rows = out.shape[0]
        out[...] = share[pl.ds(pl.multiple_of((quarter ^ d) * rows, 8), rows), :]


def gram_call(body, name, args, shape, scratch=(), outs=0):
    out_shape = jax.ShapeDtypeStruct(shape, F32)
    return pl.pallas_call(
        body,
        in_specs=[VMEM] * len(args),
        out_specs=[VMEM] * outs if outs else VMEM,
        out_shape=[out_shape] * outs if outs else out_shape,
        scratch_shapes=scratch,
        compiler_params=SMALL_VMEM,
        cost_estimate=SMALL,
        name=name,
    )(*args)


def gram(owns, others):
    width = owns[0].shape[1]
    body = functools.partial(gram_kernel, GRAM_ROWS)
    return gram_call(body, "gram", owns + others, (width, 2 * width))


def gram_share(own, other, start):
    rows, width = own.shape
    half = width // 2
    body = functools.partial(share_kernel, rows)
    scratch = [pltpu.VMEM((width, 2 * width), F32), pltpu.VMEM((5 * half, half), F32)]
    shape = (5 * half // WAYS, half)
    return gram_call(body, "gram_share", [own, other, start], shape, scratch, outs=WAYS)


def add_kernel(a, b, c, d, out):
    out[...] = (a[...] + b[...]) + (c[...] + d[...])


def join_kernel(*refs):
    parts, out = refs[:-1], refs[-1]
    rows = parts[0].shape[0]
    quarter = lax.axis_index("patch") % WAYS
    for d, part in enumerate(parts):
        out[pl.ds(pl.multiple_of((quarter ^ d) * rows, 8), rows), :] = part[...]


def sum_over_patch(parts):
    count = lax.axis_size("patch")
    rows, columns = parts[0].shape

    def add_four(values):
        return gram_call(add_kernel, "add_four", values, (rows, columns))

    def from_others(values, stride=1):
        return [
            lax.ppermute(values[d], "patch", [(i, i ^ (d * stride)) for i in range(count)])
            for d in range(1, WAYS)
        ]

    total = add_four([parts[0]] + from_others(parts))
    stride = WAYS
    while stride < count:
        total = add_four([total] + from_others([total] * WAYS, stride))
        stride *= WAYS
    quarters = [total] + from_others([total] * WAYS)
    return gram_call(join_kernel, "join", quarters, (WAYS * rows, columns))


def split(value):
    high = value.astype(BF16)
    return high, (value - high.astype(F32)).astype(BF16)


def put(pair, blocks, right=False):
    width = blocks[0].shape[0]
    places = [(0, 0), (0, 1), (1, 1)]
    if right:
        blocks, places = tuple(blocks) + (blocks[1].T,), places + [(1, 0)]
    for (row, col), block in zip(places, blocks):
        for i, piece in enumerate(split(block)):
            pair[i, pl.ds(row * width, width), pl.ds(col * width, width)] = piece


def product3(left, right):
    return dot(
        jnp.concatenate([left[0], left[0], left[1]], axis=1),
        jnp.concatenate([right[0], right[1], right[0]], axis=0),
    )


def product(lefts, right):
    width = right.shape[1] // 2
    rows = [jnp.concatenate([left[i, :width, :] for left in lefts], axis=0) for i in range(2)]
    cols = [jnp.concatenate([left[i, :, width:] for left in lefts], axis=1) for i in range(2)]
    first = product3(rows, (right[0], right[1]))
    second = product3((right[0, width:, :], right[1, width:, :]), cols)
    out = []
    for i in range(len(lefts)):
        at = slice(i * width, (i + 1) * width)
        out.append((first[at, :width], first[at, width:], second[:, at]))
    return out


def combine(*terms, unit=0.0):
    width = terms[0][1][0].shape[0]
    row = lax.broadcasted_iota(jnp.int32, (width, width), 0)
    col = lax.broadcasted_iota(jnp.int32, (width, width), 1)
    diagonal = jnp.where(row == col, unit, 0.0)
    out = []
    for i in range(3):
        value = functools.reduce(jnp.add, [factor * matrix[i] for factor, matrix in terms])
        out.append(value if i == 1 else value + diagonal)
    return tuple(out)


def finish_kernel(total_rows, chunk, names, mine, theirs, *refs):
    fields, out_ref = refs[:6], refs[6]
    x_ref, x_held, x_pair, q_pair, u_pair, n_pair, v_pair, z_pair = refs[7:15]
    wide, result, sem, out_sem = refs[15:]
    part = lax.axis_index("cols")
    size = x_ref.shape[0]
    width = size // 2
    half = width // 2
    edge_size = fields[0].shape[0]
    end = wide.shape[0] - edge_size
    starts = [at_end(names[0]) * end, edge_size, at_end(names[1]) * end]
    copies = []
    for i, source in enumerate(fields):
        rows = pl.ds(pl.multiple_of(starts[i % 3], edge_size), source.shape[0])
        side = part if i < 3 else 1 - part
        target = wide.at[rows, pl.ds(pl.multiple_of(side * width, width), width)]
        copies.append(pltpu.make_async_copy(source, target, sem.at[i]))
    for copy in copies:
        copy.start()

    def block(side, index):
        rows = pl.ds(index * half, half)
        return jnp.where(part == side, mine[rows, :], theirs[rows, :])

    def place(row, col, value):
        x_ref[pl.ds(row * half, half), pl.ds(col * half, half)] = value

    for side in range(2):
        across = block(side, 1)
        place(2 * side, 2 * side, block(side, 0))
        place(2 * side, 2 * side + 1, across)
        place(2 * side + 1, 2 * side, across.T)
        place(2 * side + 1, 2 * side + 1, block(side, 2))
        for col in (0, 1):
            part_of = block(side, 3 + col)
            place(side, 2 + col, part_of if side == 0 else part_of.T)

    gram = x_ref[:width, :width], x_ref[:width, width:], x_ref[width:, width:]
    squares = gram[0] * gram[0] + 2.0 * (gram[1] * gram[1]) + gram[2] * gram[2]
    norm = jnp.sqrt(jnp.sum(squares, keepdims=True))

    def set_x(x):
        put(x_pair, x, right=True)
        for i, value in enumerate(x):
            x_held[i] = value

    def two_sweeps(first=False, last=False):
        x = tuple(x_held[i] for i in range(3))
        (q,) = product([x_pair], x_pair)
        put(q_pair, q)
        put(u_pair, combine((0.0625, q), (-0.5625, x), unit=1.6875), right=True)
        (qu,) = product([q_pair], u_pair)
        x = tuple(x_held[i] for i in range(3))
        n = combine((1.0, qu), (-2.4375, x), unit=2.25)
        put(n_pair, n, right=True)
        if last:
            return product([z_pair], n_pair)[0]
        if first:
            z = n
            (v,) = product([x_pair], n_pair)
        else:
            v, z = product([x_pair, z_pair], n_pair)
        put(v_pair, v)
        put(z_pair, z)
        set_x(product([v_pair], n_pair)[0])

    set_x(tuple(value / norm for value in gram))
    two_sweeps(first=True)

    def body(index, carry):
        two_sweeps()
        return carry

    lax.fori_loop(0, ITERS // 2 - 2, body, 0)
    first, across, second = two_sweeps(last=True)
    z_ref = x_ref
    z_ref[:width, :width] = first
    z_ref[:width, width:] = across
    z_ref[width:, :width] = across.T
    z_ref[width:, width:] = second
    own = pl.ds(pl.multiple_of(part * width, width), width)
    rotation = z_ref[:, own].astype(BF16)
    factor = jnp.sqrt(total_rows / norm)
    for copy in copies:
        copy.wait()
    count = wide.shape[0] // chunk
    outs = []
    for i in range(count):
        rows = pl.ds(i * chunk, chunk)
        result[rows, :] = (dot(wide[rows, :], rotation) * factor).astype(BF16)
        outs.append(pltpu.make_async_copy(result.at[rows], out_ref.at[rows], out_sem.at[i]))
        outs[-1].start()
    for out in outs:
        out.wait()


def rotate(mine, theirs, owns, others, total_rows, names):
    width = owns[0].shape[1]
    rows = sum(own.shape[0] for own in owns)
    size = 2 * width
    chunk = min(rows, 512)
    body = functools.partial(finish_kernel, float(total_rows), chunk, names)
    pair = pltpu.VMEM((2, size, size), BF16)
    return pl.pallas_call(
        body,
        in_specs=[VMEM, VMEM] + [ANY] * 6,
        out_specs=ANY,
        out_shape=jax.ShapeDtypeStruct((rows, width), BF16),
        scratch_shapes=[
            pltpu.VMEM((size, size), F32),
            pltpu.VMEM((3, width, width), F32),
            pair, pair, pair, pair, pair, pair,
            pltpu.VMEM((rows, size), BF16),
            pltpu.VMEM((rows, width), BF16),
            pltpu.SemaphoreType.DMA((6,)),
            pltpu.SemaphoreType.DMA((rows // chunk,)),
        ],
        compiler_params=pltpu.CompilerParams(vmem_limit_bytes=28 * 1024 * 1024),
        cost_estimate=pl.CostEstimate(
            flops=21 * 6 * size**3 + 2 * rows * size * width,
            bytes_accessed=3 * rows * width * 2,
            transcendentals=0,
        ),
        name="rotate",
    )(mine, theirs, *owns, *others)


def after(value, *others):
    return lax.optimization_barrier((value, others))[0]


def on_device(vectors, blocks, tile_cols, live_tiles):
    tiles, _, tile, _ = blocks.shape
    width = vectors.shape[1]
    count = lax.axis_size("patch")
    pairs = {
        "even": [(i, i ^ 1) for i in range(count)],
        "odd": [(i, ((i + 1) ^ 1) - 1) for i in range(1, count - 1)],
    }

    def exchange(name, value):
        return lax.ppermute(value, "patch", pairs[name])

    def sibling(value):
        return lax.ppermute(value, "cols", [(0, 1), (1, 0)])

    start = vectors.reshape(tiles, tile, width)
    table = jnp.concatenate([tile_cols.T, jnp.broadcast_to(live_tiles[None], (1, tiles))])

    edges = dict(zip(("even", "odd"), masked_edges(table, start)))
    lead, lag = "odd", "even"
    halo = {lead: exchange(lead, edges[lead])}
    inner, *edge_blocks = load_fields(after(table, edges[lead]), start, blocks)
    halo[lag] = exchange(lag, after(edges[lag], inner))
    stored = dict(zip(("even", "odd"), edge_blocks))
    prev = dict.fromkeys(("even", "odd", "inner"))

    def inner_rows(behind):
        sources = after(edges["even"], behind), edges["odd"], inner
        return tile_rows("inner", table, stored["inner"], sources, prev["inner"], SMALL)

    def edge_rows(name, behind, cost=SMALL):
        sources = after(halo[name], behind), edges[name], inner
        return tile_rows(name, table, stored[name], sources, prev[name], cost)

    for step in range(STEPS):
        final = step == STEPS - 1
        new = {}
        if final:
            new["inner"] = inner_rows(edges["odd"])
            new[lead] = edge_rows(lead, new["inner"])
            flat = [new[name].reshape(-1, width) for name in (lead, "inner")]
            others = [sibling(value) for value in flat]
            new[lag] = edge_rows(lag, new[lead], LARGE)
        else:
            new[lead] = edge_rows(lead, inner)
            halo[lead] = exchange(lead, new[lead])
            new[lag] = edge_rows(lag, new[lead])
            halo[lag] = exchange(lag, new[lag])
            if step == 0:
                stored["inner"] = load_blocks(after(blocks, new[lag]))
            new["inner"] = inner_rows(new[lag])
        prev = dict(edges, inner=inner)
        edges, inner = {name: new[name] for name in edges}, new["inner"]
    last = edges[lag].reshape(-1, width)
    other_last = sibling(last)
    others = [after(other, last) for other in others]
    mine = sum_over_patch(gram_share(last, other_last, gram(flat, others)))
    theirs = sibling(mine)
    total_rows = tiles * tile * count
    return rotate(mine, theirs, flat + [last], others + [other_last], total_rows, (lead, lag))


def solution(mesh):
    in_specs = (P("patch", "cols"), P("patch", None, None, None), P("patch", None), P("patch"))
    return jax.shard_map(
        on_device, mesh=mesh, in_specs=in_specs, out_specs=P("patch", "cols"), check_vma=False
    )
```

```python
import functools

import jax
import jax.numpy as jnp
from jax import lax
from jax.experimental import pallas as pl
from jax.experimental.pallas import tpu as pltpu
from jax.sharding import PartitionSpec as P

HALO_T = 4
STEPS = 3
ITERS = 8
WAYS = 4
LOAD_CUTS = 4
GRAM_ROWS = 1024
GROUP = 12

SMALL = pl.CostEstimate(flops=1000, bytes_accessed=1000, transcendentals=0)
LARGE = pl.CostEstimate(flops=10**11, bytes_accessed=1000, transcendentals=0)
SMALL_VMEM = pltpu.CompilerParams(vmem_limit_bytes=8 * 1024 * 1024)
ANY = pl.BlockSpec(memory_space=pl.ANY)
HBM = pl.BlockSpec(memory_space=pltpu.HBM)
VMEM = pl.BlockSpec(memory_space=pltpu.VMEM)
EDGES_MB, FIELDS_MB, BLOCKS_MB = 53, 50, 44
SMEM = pl.BlockSpec(memory_space=pltpu.SMEM)
F32, BF16 = jnp.float32, jnp.bfloat16


def dot(a, b):
    return jnp.dot(a, b, preferred_element_type=F32)


def tile_row(blocks, listed, field):
    wide = jnp.concatenate([blocks(n) for n in range(len(listed))], axis=1)
    tall = jnp.concatenate([field(tile) for tile in listed], axis=0)
    return dot(wide, tall)


def finish(acc, prev, alive):
    value = acc if prev is None else 2.0 * acc - prev.astype(F32)
    return jnp.where(alive, value, 0.0).astype(BF16)


def at_end(name):
    odd = lax.axis_index("patch") % 2
    return 1 - odd if name == "even" else odd


def live_count(table):
    return table[table.shape[0] - 1, 0]


def edges_kernel(table_ref, whole_ref, even_ref, odd_ref, sem, table):
    edge, tiles = HALO_T, whole_ref.shape[0]
    outs = {"even": even_ref, "odd": odd_ref}
    firsts = {name: at_end(name) * (tiles - edge) for name in outs}
    load([(whole_ref, firsts[name], outs[name]) for name in outs], sem, (table_ref, table))
    for name in outs:
        clear_dead(outs[name], firsts[name], live_count(table))


def clear_dead(ref, first, live):
    def clear(index, carry):
        ref[index] = jnp.zeros(ref.shape[1:], BF16)
        return carry

    count = ref.shape[0]
    lax.fori_loop(jnp.clip(live - first, 0, count), count, clear, 0)


def load(moves, sem, *whole):
    copies = []
    for source, first, target in moves:
        count = target.shape[0] // LOAD_CUTS
        for cut in range(LOAD_CUTS):
            copies.append(
                pltpu.make_async_copy(
                    source.at[pl.ds(first + cut * count, count)],
                    target.at[pl.ds(cut * count, count)],
                    sem.at[len(copies)],
                )
            )
    for source, target in whole:
        copies.append(pltpu.make_async_copy(source, target, sem.at[len(copies)]))
    for copy in copies:
        copy.start()
    for copy in copies:
        copy.wait()


def fields_kernel(
    table_ref, whole_ref, blocks_ref, inner_ref, even_blocks, odd_blocks, sem, table
):
    last = whole_ref.shape[0] - HALO_T
    moves = [
        (blocks_ref, at_end("even") * last, even_blocks),
        (blocks_ref, at_end("odd") * last, odd_blocks),
        (whole_ref, HALO_T, inner_ref),
    ]
    load(moves, sem, (table_ref, table))
    clear_dead(inner_ref, HALO_T, live_count(table))


def blocks_kernel(blocks_ref, inner_blocks, sem):
    load([(blocks_ref, HALO_T, inner_blocks)], sem)


def load_call(body, name, args, shapes, megabytes, table=()):
    return pl.pallas_call(
        body,
        in_specs=[VMEM] * len(table) + [HBM] * len(args),
        out_specs=[VMEM] * len(shapes),
        out_shape=shapes,
        scratch_shapes=[pltpu.SemaphoreType.DMA((len(shapes) * LOAD_CUTS + len(table),))]
        + [pltpu.SMEM(array.shape, array.dtype) for array in table],
        compiler_params=pltpu.CompilerParams(vmem_limit_bytes=megabytes * 1024 * 1024),
        cost_estimate=SMALL,
        name=name,
    )(*table, *args)


def masked_edges(table, start):
    shapes = [jax.ShapeDtypeStruct((HALO_T,) + start.shape[1:], BF16)] * 2
    return load_call(edges_kernel, "masked_edges", [start], shapes, EDGES_MB, [table])


def load_fields(table, start, blocks):
    inner = start.shape[0] - 2 * HALO_T
    shapes = [jax.ShapeDtypeStruct((inner,) + start.shape[1:], BF16)]
    shapes += [jax.ShapeDtypeStruct((HALO_T,) + blocks.shape[1:], blocks.dtype)] * 2
    return load_call(fields_kernel, "load_fields", [start, blocks], shapes, FIELDS_MB, [table])


def load_blocks(blocks):
    inner = blocks.shape[0] - 2 * HALO_T
    shapes = [jax.ShapeDtypeStruct((inner,) + blocks.shape[1:], blocks.dtype)]
    return load_call(blocks_kernel, "load_blocks", [blocks], shapes, BLOCKS_MB)[0]


def layout(name, tiles):
    edge, last = HALO_T, tiles - HALO_T
    if name == "inner":
        ends = [at_end(which) for which in ("even", "odd")]
        pieces = [(i, 0, edge, end * last) for i, end in enumerate(ends)]
        return edge, 0, pieces + [(2, 0, tiles - 2 * edge, edge)]
    end = at_end(name)
    pieces = [
        (0, 0, edge, 2 * edge * end), (1, 0, edge, edge), (2, 0, edge, (2 + end) * edge),
        (2, tiles - 3 * edge, edge, 3 * edge * (1 - end)),
    ]
    return end * last, end * last - edge, pieces


def rows_kernel(name, table_ref, *refs):
    sources, (out_ref, held, table, sem) = refs[:3], refs[-4:]
    blocks_ref = refs[-5]
    prev_ref = refs[3] if len(refs) == 9 else None
    fetch = pltpu.make_async_copy(table_ref, table, sem)
    fetch.start()
    nnz, tiles = blocks_ref.shape[1], table.shape[1]
    first, base, pieces = layout(name, tiles)
    for i, begin, count, slot in pieces:
        held[pl.ds(slot, count)] = sources[i][pl.ds(begin, count)]
    fetch.wait()
    live = live_count(table)
    shift = lax.axis_index("patch") * tiles + base
    rows = out_ref.shape[0]
    together = min(GROUP, rows)

    def group(index, carry):
        for r in range(together):
            row = index * together + r
            listed = [table[n, first + row] - shift for n in range(nnz)]
            acc = tile_row(lambda n: blocks_ref[row, n], listed, lambda c: held[c])
            prev = None if prev_ref is None else prev_ref[row]
            out_ref[row] = finish(acc, prev, first + row < live)
        return carry

    lax.fori_loop(0, rows // together, group, 0)


def tile_rows(name, table, blocks, sources, prev, cost):
    rows, _, tile, _ = blocks.shape
    width = sources[0].shape[-1]
    window = table.shape[1] if name == "inner" else 4 * HALO_T
    args = [table] + list(sources) + ([] if prev is None else [prev]) + [blocks]
    return pl.pallas_call(
        functools.partial(rows_kernel, name),
        in_specs=[VMEM] * len(args),
        out_specs=VMEM,
        out_shape=jax.ShapeDtypeStruct((rows, tile, width), BF16),
        scratch_shapes=[
            pltpu.VMEM((window, tile, width), BF16),
            pltpu.SMEM(table.shape, jnp.int32),
            pltpu.SemaphoreType.DMA,
        ],
        compiler_params=SMALL_VMEM,
        cost_estimate=cost,
        name="rows_" + name,
    )(*args)


ACROSS = (((0,), (0,)), ((), ()))


NEAR = (1, 2, 3), (2, 1, 3)
FAR = (2, 3, 1), (3, 2, 1)


def quarter_order():
    own = lax.axis_index("patch") % WAYS
    first_core = lax.axis_index("cols") == 0
    return [own] + [own ^ jnp.where(first_core, one, two) for one, two in zip(*NEAR)]


def add_gram(chunk, own_ref, other_ref, total):
    chunk = min(chunk, own_ref.shape[0])

    def add(index, carry):
        rows = pl.ds(pl.multiple_of(index * chunk, chunk), chunk)
        own = own_ref[rows, :]
        both = jnp.concatenate([own, other_ref[rows, :]], axis=1)
        total[...] += lax.dot_general(own, both, ACROSS, preferred_element_type=F32)
        return carry

    lax.fori_loop(0, own_ref.shape[0] // chunk, add, 0)


def gram_kernel(chunk, *refs):
    count = len(refs) // 2
    refs[-1][...] = jnp.zeros(refs[-1].shape, F32)
    for own_ref, other_ref in zip(refs[:count], refs[count:-1]):
        add_gram(chunk, own_ref, other_ref, refs[-1])


def share_kernel(chunk, own_ref, other_ref, start_ref, *refs):
    outs, (total, share) = refs[:WAYS], refs[WAYS:]
    total[...] = start_ref[...]
    add_gram(chunk, own_ref, other_ref, total)
    width = total.shape[0]
    half = width // 2
    own, other = total[:, :width], total[:, width:]
    first_core = lax.axis_index("cols") == 0
    second = jnp.where(first_core, other[:half, :half], other[:half, half:])
    third = jnp.where(first_core, other[:half, half:], other[half:, half:])
    blocks = [own[:half, :half], own[:half, half:], own[half:, half:], second, third]
    for i, block in enumerate(blocks):
        share[pl.ds(i * half, half), :] = block
    for out, quarter in zip(outs, quarter_order()):
        rows = out.shape[0]
        out[...] = share[pl.ds(pl.multiple_of(quarter * rows, 8), rows), :]


def gram_call(body, name, args, shape, scratch=(), outs=0):
    out_shape = jax.ShapeDtypeStruct(shape, F32)
    return pl.pallas_call(
        body,
        in_specs=[VMEM] * len(args),
        out_specs=[VMEM] * outs if outs else VMEM,
        out_shape=[out_shape] * outs if outs else out_shape,
        scratch_shapes=scratch,
        compiler_params=SMALL_VMEM,
        cost_estimate=SMALL,
        name=name,
    )(*args)


def gram(owns, others):
    width = owns[0].shape[1]
    body = functools.partial(gram_kernel, GRAM_ROWS)
    return gram_call(body, "gram", owns + others, (width, 2 * width))


def gram_share(own, other, start):
    rows, width = own.shape
    half = width // 2
    body = functools.partial(share_kernel, rows)
    scratch = [pltpu.VMEM((width, 2 * width), F32), pltpu.VMEM((5 * half, half), F32)]
    shape = (5 * half // WAYS, half)
    return gram_call(body, "gram_share", [own, other, start], shape, scratch, outs=WAYS)


def add_kernel(a, b, c, d, out):
    out[...] = (a[...] + b[...]) + (c[...] + d[...])


def join_kernel(*refs):
    parts, out = refs[:-1], refs[-1]
    rows = parts[0].shape[0]
    for part, quarter in zip(parts, quarter_order()):
        out[pl.ds(pl.multiple_of(quarter * rows, 8), rows), :] = part[...]


def sum_over_patch(parts):
    count = lax.axis_size("patch")
    rows, columns = parts[0].shape

    def add_four(values):
        return gram_call(add_kernel, "add_four", values, (rows, columns))

    def from_others(values, distances, stride=1):
        got = []
        for value, both in zip(values, zip(*distances)):
            pairs = [
                (core * count + i, core * count + (i ^ (distance * stride)))
                for core, distance in enumerate(both)
                for i in range(count)
            ]
            got.append(lax.ppermute(value, ("cols", "patch"), pairs))
        return got

    total = add_four([parts[0]] + from_others(parts[1:], NEAR))
    stride = WAYS
    while stride < count:
        total = add_four([total] + from_others([total] * (WAYS - 1), FAR, stride))
        stride *= WAYS
    quarters = [total] + from_others([total] * (WAYS - 1), NEAR)
    return gram_call(join_kernel, "join", quarters, (WAYS * rows, columns))


def split(value):
    high = value.astype(BF16)
    return high, (value - high.astype(F32)).astype(BF16)


def put(pair, blocks, right=False):
    width = blocks[0].shape[0]
    places = [(0, 0), (0, 1), (1, 1)]
    if right:
        blocks, places = tuple(blocks) + (blocks[1].T,), places + [(1, 0)]
    for (row, col), block in zip(places, blocks):
        for i, piece in enumerate(split(block)):
            pair[i, pl.ds(row * width, width), pl.ds(col * width, width)] = piece


def product3(left, right):
    return dot(
        jnp.concatenate([left[0], left[0], left[1]], axis=1),
        jnp.concatenate([right[0], right[1], right[0]], axis=0),
    )


def product(lefts, right):
    width = right.shape[1] // 2
    rows = [jnp.concatenate([left[i, :width, :] for left in lefts], axis=0) for i in range(2)]
    cols = [jnp.concatenate([left[i, :, width:] for left in lefts], axis=1) for i in range(2)]
    first = product3(rows, (right[0], right[1]))
    second = product3((right[0, width:, :], right[1, width:, :]), cols)
    out = []
    for i in range(len(lefts)):
        at = slice(i * width, (i + 1) * width)
        out.append((first[at, :width], first[at, width:], second[:, at]))
    return out


def combine(*terms, unit=0.0):
    width = terms[0][1][0].shape[0]
    row = lax.broadcasted_iota(jnp.int32, (width, width), 0)
    col = lax.broadcasted_iota(jnp.int32, (width, width), 1)
    diagonal = jnp.where(row == col, unit, 0.0)
    out = []
    for i in range(3):
        value = functools.reduce(jnp.add, [factor * matrix[i] for factor, matrix in terms])
        out.append(value if i == 1 else value + diagonal)
    return tuple(out)


def finish_kernel(total_rows, chunk, names, mine, theirs, *refs):
    fields, out_ref = refs[:6], refs[6]
    x_ref, x_held, x_pair, q_pair, u_pair, n_pair, v_pair, z_pair = refs[7:15]
    wide, result, sem, out_sem = refs[15:]
    part = lax.axis_index("cols")
    size = x_ref.shape[0]
    width = size // 2
    half = width // 2
    edge_size = fields[0].shape[0]
    end = wide.shape[0] - edge_size
    starts = [at_end(names[0]) * end, edge_size, at_end(names[1]) * end]
    copies = []
    for i, source in enumerate(fields):
        rows = pl.ds(pl.multiple_of(starts[i % 3], edge_size), source.shape[0])
        side = part if i < 3 else 1 - part
        target = wide.at[rows, pl.ds(pl.multiple_of(side * width, width), width)]
        copies.append(pltpu.make_async_copy(source, target, sem.at[i]))
    for copy in copies:
        copy.start()

    def block(side, index):
        rows = pl.ds(index * half, half)
        return jnp.where(part == side, mine[rows, :], theirs[rows, :])

    def place(row, col, value):
        x_ref[pl.ds(row * half, half), pl.ds(col * half, half)] = value

    for side in range(2):
        across = block(side, 1)
        place(2 * side, 2 * side, block(side, 0))
        place(2 * side, 2 * side + 1, across)
        place(2 * side + 1, 2 * side, across.T)
        place(2 * side + 1, 2 * side + 1, block(side, 2))
        for col in (0, 1):
            part_of = block(side, 3 + col)
            place(side, 2 + col, part_of if side == 0 else part_of.T)

    gram = x_ref[:width, :width], x_ref[:width, width:], x_ref[width:, width:]
    squares = gram[0] * gram[0] + 2.0 * (gram[1] * gram[1]) + gram[2] * gram[2]
    norm = jnp.sqrt(jnp.sum(squares, keepdims=True))

    def set_x(x):
        put(x_pair, x, right=True)
        for i, value in enumerate(x):
            x_held[i] = value

    def two_sweeps(first=False, last=False):
        x = tuple(x_held[i] for i in range(3))
        (q,) = product([x_pair], x_pair)
        put(q_pair, q)
        put(u_pair, combine((0.0625, q), (-0.5625, x), unit=1.6875), right=True)
        (qu,) = product([q_pair], u_pair)
        x = tuple(x_held[i] for i in range(3))
        n = combine((1.0, qu), (-2.4375, x), unit=2.25)
        put(n_pair, n, right=True)
        if last:
            return product([z_pair], n_pair)[0]
        if first:
            z = n
            (v,) = product([x_pair], n_pair)
        else:
            v, z = product([x_pair, z_pair], n_pair)
        put(v_pair, v)
        put(z_pair, z)
        set_x(product([v_pair], n_pair)[0])

    set_x(tuple(value / norm for value in gram))
    two_sweeps(first=True)

    def body(index, carry):
        two_sweeps()
        return carry

    lax.fori_loop(0, ITERS // 2 - 2, body, 0)
    first, across, second = two_sweeps(last=True)
    z_ref = x_ref
    z_ref[:width, :width] = first
    z_ref[:width, width:] = across
    z_ref[width:, :width] = across.T
    z_ref[width:, width:] = second
    own = pl.ds(pl.multiple_of(part * width, width), width)
    rotation = z_ref[:, own].astype(BF16)
    factor = jnp.sqrt(total_rows / norm)
    for copy in copies:
        copy.wait()
    count = wide.shape[0] // chunk
    outs = []
    for i in range(count):
        rows = pl.ds(i * chunk, chunk)
        result[rows, :] = (dot(wide[rows, :], rotation) * factor).astype(BF16)
        outs.append(pltpu.make_async_copy(result.at[rows], out_ref.at[rows], out_sem.at[i]))
        outs[-1].start()
    for out in outs:
        out.wait()


def rotate(mine, theirs, owns, others, total_rows, names):
    width = owns[0].shape[1]
    rows = sum(own.shape[0] for own in owns)
    size = 2 * width
    chunk = min(rows, 512)
    body = functools.partial(finish_kernel, float(total_rows), chunk, names)
    pair = pltpu.VMEM((2, size, size), BF16)
    return pl.pallas_call(
        body,
        in_specs=[VMEM, VMEM] + [ANY] * 6,
        out_specs=ANY,
        out_shape=jax.ShapeDtypeStruct((rows, width), BF16),
        scratch_shapes=[
            pltpu.VMEM((size, size), F32),
            pltpu.VMEM((3, width, width), F32),
            pair, pair, pair, pair, pair, pair,
            pltpu.VMEM((rows, size), BF16),
            pltpu.VMEM((rows, width), BF16),
            pltpu.SemaphoreType.DMA((6,)),
            pltpu.SemaphoreType.DMA((rows // chunk,)),
        ],
        compiler_params=pltpu.CompilerParams(vmem_limit_bytes=28 * 1024 * 1024),
        cost_estimate=pl.CostEstimate(
            flops=21 * 6 * size**3 + 2 * rows * size * width,
            bytes_accessed=3 * rows * width * 2,
            transcendentals=0,
        ),
        name="rotate",
    )(mine, theirs, *owns, *others)


def after(value, *others):
    return lax.optimization_barrier((value, others))[0]


def on_device(vectors, blocks, tile_cols, live_tiles):
    tiles, _, tile, _ = blocks.shape
    width = vectors.shape[1]
    count = lax.axis_size("patch")
    pairs = {
        "even": [(i, i ^ 1) for i in range(count)],
        "odd": [(i, ((i + 1) ^ 1) - 1) for i in range(1, count - 1)],
    }

    def exchange(name, value):
        return lax.ppermute(value, "patch", pairs[name])

    def sibling(value):
        return lax.ppermute(value, "cols", [(0, 1), (1, 0)])

    start = vectors.reshape(tiles, tile, width)
    table = jnp.concatenate([tile_cols.T, jnp.broadcast_to(live_tiles[None], (1, tiles))])

    edges = dict(zip(("even", "odd"), masked_edges(table, start)))
    lead, lag = "odd", "even"
    halo = {lead: exchange(lead, edges[lead])}
    inner, *edge_blocks = load_fields(after(table, edges[lead]), start, blocks)
    halo[lag] = exchange(lag, after(edges[lag], inner))
    stored = dict(zip(("even", "odd"), edge_blocks), inner=load_blocks(after(blocks, inner)))
    halo[lead] = after(halo[lead], stored["inner"])
    prev = dict.fromkeys(("even", "odd", "inner"))

    def inner_rows(behind):
        sources = after(edges["even"], behind), edges["odd"], inner
        return tile_rows("inner", table, stored["inner"], sources, prev["inner"], SMALL)

    def edge_rows(name, behind, cost=SMALL):
        sources = after(halo[name], behind), edges[name], inner
        return tile_rows(name, table, stored[name], sources, prev[name], cost)

    for step in range(STEPS):
        final = step == STEPS - 1
        new = {}
        if final:
            new["inner"] = inner_rows(edges["odd"])
            new[lead] = edge_rows(lead, new["inner"])
            flat = [new[name].reshape(-1, width) for name in (lead, "inner")]
            others = [sibling(value) for value in flat]
            new[lag] = edge_rows(lag, new[lead], LARGE)
        else:
            new[lead] = edge_rows(lead, inner)
            halo[lead] = exchange(lead, new[lead])
            new[lag] = edge_rows(lag, new[lead])
            halo[lag] = exchange(lag, new[lag])
            new["inner"] = inner_rows(new[lag])
        prev = dict(edges, inner=inner)
        edges, inner = {name: new[name] for name in edges}, new["inner"]
    last = edges[lag].reshape(-1, width)
    other_last = sibling(last)
    others = [after(other, last) for other in others]
    mine = sum_over_patch(gram_share(last, other_last, gram(flat, others)))
    theirs = sibling(mine)
    total_rows = tiles * tile * count
    return rotate(mine, theirs, flat + [last], others + [other_last], total_rows, (lead, lag))


def solution(mesh):
    in_specs = (P("patch", "cols"), P("patch", None, None, None), P("patch", None), P("patch"))
    return jax.shard_map(
        on_device, mesh=mesh, in_specs=in_specs, out_specs=P("patch", "cols"), check_vma=False
    )
```

```python
import functools

import jax
import jax.numpy as jnp
from jax import lax
from jax.experimental import pallas as pl
from jax.experimental.pallas import tpu as pltpu
from jax.sharding import PartitionSpec as P

HALO_T = 4
STEPS = 3
ITERS = 8
WAYS = 4
LOAD_CUTS = 4
GRAM_ROWS = 1024
GROUP = 12

SMALL = pl.CostEstimate(flops=1000, bytes_accessed=1000, transcendentals=0)
LARGE = pl.CostEstimate(flops=2 * 10**10, bytes_accessed=1000, transcendentals=0)
SMALL_VMEM = pltpu.CompilerParams(vmem_limit_bytes=8 * 1024 * 1024)
ANY = pl.BlockSpec(memory_space=pl.ANY)
HBM = pl.BlockSpec(memory_space=pltpu.HBM)
VMEM = pl.BlockSpec(memory_space=pltpu.VMEM)
EDGES_MB, FIELDS_MB, BLOCKS_MB = 53, 50, 44
SMEM = pl.BlockSpec(memory_space=pltpu.SMEM)
F32, BF16 = jnp.float32, jnp.bfloat16


def dot(a, b):
    return jnp.dot(a, b, preferred_element_type=F32)


def tile_row(blocks, listed, field):
    wide = jnp.concatenate([blocks(n) for n in range(len(listed))], axis=1)
    tall = jnp.concatenate([field(tile) for tile in listed], axis=0)
    return dot(wide, tall)


def finish(acc, prev, alive):
    value = acc if prev is None else 2.0 * acc - prev.astype(F32)
    return jnp.where(alive, value, 0.0).astype(BF16)


def at_end(name):
    odd = lax.axis_index("patch") % 2
    return 1 - odd if name == "even" else odd


def live_count(table):
    return table[table.shape[0] - 1, 0]


def edges_kernel(table_ref, whole_ref, even_ref, odd_ref, sem, table):
    edge, tiles = HALO_T, whole_ref.shape[0]
    outs = {"even": even_ref, "odd": odd_ref}
    firsts = {name: at_end(name) * (tiles - edge) for name in outs}
    load([(whole_ref, firsts[name], outs[name]) for name in outs], sem, (table_ref, table))
    for name in outs:
        clear_dead(outs[name], firsts[name], live_count(table))


def clear_dead(ref, first, live):
    def clear(index, carry):
        ref[index] = jnp.zeros(ref.shape[1:], BF16)
        return carry

    count = ref.shape[0]
    lax.fori_loop(jnp.clip(live - first, 0, count), count, clear, 0)


def load(moves, sem, *whole):
    copies = []
    for source, first, target in moves:
        count = target.shape[0] // LOAD_CUTS
        for cut in range(LOAD_CUTS):
            copies.append(
                pltpu.make_async_copy(
                    source.at[pl.ds(first + cut * count, count)],
                    target.at[pl.ds(cut * count, count)],
                    sem.at[len(copies)],
                )
            )
    for source, target in whole:
        copies.append(pltpu.make_async_copy(source, target, sem.at[len(copies)]))
    for copy in copies:
        copy.start()
    for copy in copies:
        copy.wait()


def fields_kernel(
    table_ref, whole_ref, blocks_ref, inner_ref, even_blocks, odd_blocks, sem, table
):
    last = whole_ref.shape[0] - HALO_T
    moves = [
        (blocks_ref, at_end("even") * last, even_blocks),
        (blocks_ref, at_end("odd") * last, odd_blocks),
        (whole_ref, HALO_T, inner_ref),
    ]
    load(moves, sem, (table_ref, table))
    clear_dead(inner_ref, HALO_T, live_count(table))


def blocks_kernel(blocks_ref, inner_blocks, sem):
    load([(blocks_ref, HALO_T, inner_blocks)], sem)


def load_call(body, name, args, shapes, megabytes, table=()):
    return pl.pallas_call(
        body,
        in_specs=[VMEM] * len(table) + [HBM] * len(args),
        out_specs=[VMEM] * len(shapes),
        out_shape=shapes,
        scratch_shapes=[pltpu.SemaphoreType.DMA((len(shapes) * LOAD_CUTS + len(table),))]
        + [pltpu.SMEM(array.shape, array.dtype) for array in table],
        compiler_params=pltpu.CompilerParams(vmem_limit_bytes=megabytes * 1024 * 1024),
        cost_estimate=SMALL,
        name=name,
    )(*table, *args)


def masked_edges(table, start):
    shapes = [jax.ShapeDtypeStruct((HALO_T,) + start.shape[1:], BF16)] * 2
    return load_call(edges_kernel, "masked_edges", [start], shapes, EDGES_MB, [table])


def load_fields(table, start, blocks):
    inner = start.shape[0] - 2 * HALO_T
    shapes = [jax.ShapeDtypeStruct((inner,) + start.shape[1:], BF16)]
    shapes += [jax.ShapeDtypeStruct((HALO_T,) + blocks.shape[1:], blocks.dtype)] * 2
    return load_call(fields_kernel, "load_fields", [start, blocks], shapes, FIELDS_MB, [table])


def load_blocks(blocks):
    inner = blocks.shape[0] - 2 * HALO_T
    shapes = [jax.ShapeDtypeStruct((inner,) + blocks.shape[1:], blocks.dtype)]
    return load_call(blocks_kernel, "load_blocks", [blocks], shapes, BLOCKS_MB)[0]


def layout(name, tiles):
    edge, last = HALO_T, tiles - HALO_T
    if name == "inner":
        ends = [at_end(which) for which in ("even", "odd")]
        pieces = [(i, 0, edge, end * last) for i, end in enumerate(ends)]
        return edge, 0, pieces + [(2, 0, tiles - 2 * edge, edge)]
    end = at_end(name)
    pieces = [
        (0, 0, edge, 2 * edge * end), (1, 0, edge, edge), (2, 0, edge, (2 + end) * edge),
        (2, tiles - 3 * edge, edge, 3 * edge * (1 - end)),
    ]
    return end * last, end * last - edge, pieces


def rows_kernel(name, table_ref, *refs):
    sources, (out_ref, held, table, sem) = refs[:3], refs[-4:]
    blocks_ref = refs[-5]
    prev_ref = refs[3] if len(refs) == 9 else None
    fetch = pltpu.make_async_copy(table_ref, table, sem)
    fetch.start()
    nnz, tiles = blocks_ref.shape[1], table.shape[1]
    first, base, pieces = layout(name, tiles)
    for i, begin, count, slot in pieces:
        held[pl.ds(slot, count)] = sources[i][pl.ds(begin, count)]
    fetch.wait()
    live = live_count(table)
    shift = lax.axis_index("patch") * tiles + base
    rows = out_ref.shape[0]
    together = min(GROUP, rows)

    def group(index, carry):
        for r in range(together):
            row = index * together + r
            listed = [table[n, first + row] - shift for n in range(nnz)]
            acc = tile_row(lambda n: blocks_ref[row, n], listed, lambda c: held[c])
            prev = None if prev_ref is None else prev_ref[row]
            out_ref[row] = finish(acc, prev, first + row < live)
        return carry

    lax.fori_loop(0, rows // together, group, 0)


def tile_rows(name, table, blocks, sources, prev, cost):
    rows, _, tile, _ = blocks.shape
    width = sources[0].shape[-1]
    window = table.shape[1] if name == "inner" else 4 * HALO_T
    args = [table] + list(sources) + ([] if prev is None else [prev]) + [blocks]
    return pl.pallas_call(
        functools.partial(rows_kernel, name),
        in_specs=[VMEM] * len(args),
        out_specs=VMEM,
        out_shape=jax.ShapeDtypeStruct((rows, tile, width), BF16),
        scratch_shapes=[
            pltpu.VMEM((window, tile, width), BF16),
            pltpu.SMEM(table.shape, jnp.int32),
            pltpu.SemaphoreType.DMA,
        ],
        compiler_params=SMALL_VMEM,
        cost_estimate=cost,
        name="rows_" + name,
    )(*args)


ACROSS = (((0,), (0,)), ((), ()))


NEAR = (1, 2, 3), (2, 1, 3)
FAR = (1, 3, 2), (1, 2, 3)


def quarter_order():
    own = lax.axis_index("patch") % WAYS
    first_core = lax.axis_index("cols") == 0
    return [own] + [own ^ jnp.where(first_core, one, two) for one, two in zip(*NEAR)]


def add_gram(chunk, own_ref, other_ref, total):
    chunk = min(chunk, own_ref.shape[0])

    def add(index, carry):
        rows = pl.ds(pl.multiple_of(index * chunk, chunk), chunk)
        own = own_ref[rows, :]
        both = jnp.concatenate([own, other_ref[rows, :]], axis=1)
        total[...] += lax.dot_general(own, both, ACROSS, preferred_element_type=F32)
        return carry

    lax.fori_loop(0, own_ref.shape[0] // chunk, add, 0)


def gram_kernel(chunk, *refs):
    count = len(refs) // 2
    refs[-1][...] = jnp.zeros(refs[-1].shape, F32)
    for own_ref, other_ref in zip(refs[:count], refs[count:-1]):
        add_gram(chunk, own_ref, other_ref, refs[-1])


def share_kernel(chunk, own_ref, other_ref, start_ref, *refs):
    outs, (total, share) = refs[:WAYS], refs[WAYS:]
    total[...] = start_ref[...]
    add_gram(chunk, own_ref, other_ref, total)
    width = total.shape[0]
    half = width // 2
    own, other = total[:, :width], total[:, width:]
    first_core = lax.axis_index("cols") == 0
    second = jnp.where(first_core, other[:half, :half], other[:half, half:])
    third = jnp.where(first_core, other[:half, half:], other[half:, half:])
    blocks = [own[:half, :half], own[:half, half:], own[half:, half:], second, third]
    for i, block in enumerate(blocks):
        share[pl.ds(i * half, half), :] = block
    for out, quarter in zip(outs, quarter_order()):
        rows = out.shape[0]
        out[...] = share[pl.ds(pl.multiple_of(quarter * rows, 8), rows), :]


def gram_call(body, name, args, shape, scratch=(), outs=0):
    out_shape = jax.ShapeDtypeStruct(shape, F32)
    return pl.pallas_call(
        body,
        in_specs=[VMEM] * len(args),
        out_specs=[VMEM] * outs if outs else VMEM,
        out_shape=[out_shape] * outs if outs else out_shape,
        scratch_shapes=scratch,
        compiler_params=SMALL_VMEM,
        cost_estimate=SMALL,
        name=name,
    )(*args)


def gram(owns, others):
    width = owns[0].shape[1]
    body = functools.partial(gram_kernel, GRAM_ROWS)
    return gram_call(body, "gram", owns + others, (width, 2 * width))


def gram_share(own, other, start):
    rows, width = own.shape
    half = width // 2
    body = functools.partial(share_kernel, rows)
    scratch = [pltpu.VMEM((width, 2 * width), F32), pltpu.VMEM((5 * half, half), F32)]
    shape = (5 * half // WAYS, half)
    return gram_call(body, "gram_share", [own, other, start], shape, scratch, outs=WAYS)


def add_kernel(a, b, c, d, out):
    out[...] = (a[...] + b[...]) + (c[...] + d[...])


def join_kernel(*refs):
    parts, out = refs[:-1], refs[-1]
    rows = parts[0].shape[0]
    for part, quarter in zip(parts, quarter_order()):
        out[pl.ds(pl.multiple_of(quarter * rows, 8), rows), :] = part[...]


def sum_over_patch(parts):
    count = lax.axis_size("patch")
    rows, columns = parts[0].shape

    def add_four(values):
        return gram_call(add_kernel, "add_four", values, (rows, columns))

    def from_others(values, distances, stride=1):
        got = []
        for value, both in zip(values, zip(*distances)):
            pairs = [
                (core * count + i, core * count + (i ^ (distance * stride)))
                for core, distance in enumerate(both)
                for i in range(count)
            ]
            got.append(lax.ppermute(value, ("cols", "patch"), pairs))
        return got

    total = add_four([parts[0]] + from_others(parts[1:], NEAR))
    stride = WAYS
    while stride < count:
        total = add_four([total] + from_others([total] * (WAYS - 1), FAR, stride))
        stride *= WAYS
    quarters = [total] + from_others([total] * (WAYS - 1), NEAR)
    return gram_call(join_kernel, "join", quarters, (WAYS * rows, columns))


def split(value):
    high = value.astype(BF16)
    return high, (value - high.astype(F32)).astype(BF16)


def put(pair, blocks, right=False):
    width = blocks[0].shape[0]
    places = [(0, 0), (0, 1), (1, 1)]
    if right:
        blocks, places = tuple(blocks) + (blocks[1].T,), places + [(1, 0)]
    for (row, col), block in zip(places, blocks):
        for i, piece in enumerate(split(block)):
            pair[i, pl.ds(row * width, width), pl.ds(col * width, width)] = piece


def product3(left, right):
    return dot(
        jnp.concatenate([left[0], left[0], left[1]], axis=1),
        jnp.concatenate([right[0], right[1], right[0]], axis=0),
    )


def product(lefts, right):
    width = right.shape[1] // 2
    rows = [jnp.concatenate([left[i, :width, :] for left in lefts], axis=0) for i in range(2)]
    cols = [jnp.concatenate([left[i, :, width:] for left in lefts], axis=1) for i in range(2)]
    first = product3(rows, (right[0], right[1]))
    second = product3((right[0, width:, :], right[1, width:, :]), cols)
    out = []
    for i in range(len(lefts)):
        at = slice(i * width, (i + 1) * width)
        out.append((first[at, :width], first[at, width:], second[:, at]))
    return out


def combine(*terms, unit=0.0):
    width = terms[0][1][0].shape[0]
    row = lax.broadcasted_iota(jnp.int32, (width, width), 0)
    col = lax.broadcasted_iota(jnp.int32, (width, width), 1)
    diagonal = jnp.where(row == col, unit, 0.0)
    out = []
    for i in range(3):
        value = functools.reduce(jnp.add, [factor * matrix[i] for factor, matrix in terms])
        out.append(value if i == 1 else value + diagonal)
    return tuple(out)


def finish_kernel(total_rows, chunk, names, mine, theirs, *refs):
    fields, out_ref = refs[:6], refs[6]
    x_ref, x_held, x_pair, q_pair, u_pair, n_pair, v_pair, z_pair = refs[7:15]
    wide, result, sem, out_sem = refs[15:]
    part = lax.axis_index("cols")
    size = x_ref.shape[0]
    width = size // 2
    half = width // 2
    edge_size = fields[0].shape[0]
    end = wide.shape[0] - edge_size
    starts = [at_end(names[0]) * end, edge_size, at_end(names[1]) * end]
    copies = []
    for i, source in enumerate(fields):
        rows = pl.ds(pl.multiple_of(starts[i % 3], edge_size), source.shape[0])
        side = part if i < 3 else 1 - part
        target = wide.at[rows, pl.ds(pl.multiple_of(side * width, width), width)]
        copies.append(pltpu.make_async_copy(source, target, sem.at[i]))
    for copy in copies:
        copy.start()

    def block(side, index):
        rows = pl.ds(index * half, half)
        return jnp.where(part == side, mine[rows, :], theirs[rows, :])

    def place(row, col, value):
        x_ref[pl.ds(row * half, half), pl.ds(col * half, half)] = value

    for side in range(2):
        across = block(side, 1)
        place(2 * side, 2 * side, block(side, 0))
        place(2 * side, 2 * side + 1, across)
        place(2 * side + 1, 2 * side, across.T)
        place(2 * side + 1, 2 * side + 1, block(side, 2))
        for col in (0, 1):
            part_of = block(side, 3 + col)
            place(side, 2 + col, part_of if side == 0 else part_of.T)

    gram = x_ref[:width, :width], x_ref[:width, width:], x_ref[width:, width:]
    squares = gram[0] * gram[0] + 2.0 * (gram[1] * gram[1]) + gram[2] * gram[2]
    norm = jnp.sqrt(jnp.sum(squares, keepdims=True))

    def set_x(x):
        put(x_pair, x, right=True)
        for i, value in enumerate(x):
            x_held[i] = value

    def two_sweeps(first=False, last=False):
        x = tuple(x_held[i] for i in range(3))
        (q,) = product([x_pair], x_pair)
        put(q_pair, q)
        put(u_pair, combine((0.0625, q), (-0.5625, x), unit=1.6875), right=True)
        (qu,) = product([q_pair], u_pair)
        x = tuple(x_held[i] for i in range(3))
        n = combine((1.0, qu), (-2.4375, x), unit=2.25)
        put(n_pair, n, right=True)
        if last:
            return product([z_pair], n_pair)[0]
        if first:
            z = n
            (v,) = product([x_pair], n_pair)
        else:
            v, z = product([x_pair, z_pair], n_pair)
        put(v_pair, v)
        put(z_pair, z)
        set_x(product([v_pair], n_pair)[0])

    set_x(tuple(value / norm for value in gram))
    two_sweeps(first=True)

    def body(index, carry):
        two_sweeps()
        return carry

    lax.fori_loop(0, ITERS // 2 - 2, body, 0)
    first, across, second = two_sweeps(last=True)
    z_ref = x_ref
    z_ref[:width, :width] = first
    z_ref[:width, width:] = across
    z_ref[width:, :width] = across.T
    z_ref[width:, width:] = second
    own = pl.ds(pl.multiple_of(part * width, width), width)
    rotation = z_ref[:, own].astype(BF16)
    factor = jnp.sqrt(total_rows / norm)
    for copy in copies:
        copy.wait()
    count = wide.shape[0] // chunk
    outs = []
    for i in range(count):
        rows = pl.ds(i * chunk, chunk)
        result[rows, :] = (dot(wide[rows, :], rotation) * factor).astype(BF16)
        outs.append(pltpu.make_async_copy(result.at[rows], out_ref.at[rows], out_sem.at[i]))
        outs[-1].start()
    for out in outs:
        out.wait()


def rotate(mine, theirs, owns, others, total_rows, names):
    width = owns[0].shape[1]
    rows = sum(own.shape[0] for own in owns)
    size = 2 * width
    chunk = min(rows, 512)
    body = functools.partial(finish_kernel, float(total_rows), chunk, names)
    pair = pltpu.VMEM((2, size, size), BF16)
    return pl.pallas_call(
        body,
        in_specs=[VMEM, VMEM] + [ANY] * 6,
        out_specs=ANY,
        out_shape=jax.ShapeDtypeStruct((rows, width), BF16),
        scratch_shapes=[
            pltpu.VMEM((size, size), F32),
            pltpu.VMEM((3, width, width), F32),
            pair, pair, pair, pair, pair, pair,
            pltpu.VMEM((rows, size), BF16),
            pltpu.VMEM((rows, width), BF16),
            pltpu.SemaphoreType.DMA((6,)),
            pltpu.SemaphoreType.DMA((rows // chunk,)),
        ],
        compiler_params=pltpu.CompilerParams(vmem_limit_bytes=28 * 1024 * 1024),
        cost_estimate=pl.CostEstimate(
            flops=21 * 6 * size**3 + 2 * rows * size * width,
            bytes_accessed=3 * rows * width * 2,
            transcendentals=0,
        ),
        name="rotate",
    )(mine, theirs, *owns, *others)


def after(value, *others):
    return lax.optimization_barrier((value, others))[0]


def on_device(vectors, blocks, tile_cols, live_tiles):
    tiles, _, tile, _ = blocks.shape
    width = vectors.shape[1]
    count = lax.axis_size("patch")
    pairs = {
        "even": [(i, i ^ 1) for i in range(count)],
        "odd": [(i, ((i + 1) ^ 1) - 1) for i in range(1, count - 1)],
    }

    def exchange(name, value):
        return lax.ppermute(value, "patch", pairs[name])

    def sibling(value):
        return lax.ppermute(value, "cols", [(0, 1), (1, 0)])

    start = vectors.reshape(tiles, tile, width)
    table = jnp.concatenate([tile_cols.T, jnp.broadcast_to(live_tiles[None], (1, tiles))])

    edges = dict(zip(("even", "odd"), masked_edges(table, start)))
    lead, lag = "odd", "even"
    halo = {lead: exchange(lead, edges[lead])}
    inner, *edge_blocks = load_fields(after(table, edges[lead]), start, blocks)
    halo[lag] = exchange(lag, after(edges[lag], inner))
    stored = dict(zip(("even", "odd"), edge_blocks), inner=load_blocks(after(blocks, inner)))
    halo[lead] = after(halo[lead], stored["inner"])
    prev = dict.fromkeys(("even", "odd", "inner"))

    def inner_rows(behind):
        sources = after(edges["even"], behind), edges["odd"], inner
        return tile_rows("inner", table, stored["inner"], sources, prev["inner"], SMALL)

    def edge_rows(name, behind, cost=SMALL):
        sources = after(halo[name], behind), edges[name], inner
        return tile_rows(name, table, stored[name], sources, prev[name], cost)

    ahead = None
    for step in range(STEPS):
        first, final = step == 0, step == STEPS - 1
        new = {}
        if not first:
            new["inner"] = inner_rows(edges["odd"]) if ahead is None else ahead
        cost = LARGE if final else SMALL
        new[lead] = edge_rows(lead, new.get("inner", inner), cost)
        if first:
            new["inner"] = inner_rows(new[lead])
        if final:
            flat = [new[name].reshape(-1, width) for name in (lead, "inner")]
            others = [sibling(value) for value in flat]
        else:
            halo[lead] = exchange(lead, after(new[lead], new["inner"]))
        new[lag] = edge_rows(lag, new[lead], cost)
        prev = dict(edges, inner=inner)
        edges, inner = {name: new[name] for name in edges}, new["inner"]
        if step == STEPS - 2:
            ahead = inner_rows(new[lag])
            halo[lag] = exchange(lag, after(new[lag], ahead))
        elif not final:
            halo[lag] = exchange(lag, new[lag])
    last = edges[lag].reshape(-1, width)
    other_last = sibling(last)
    others = [after(other, last) for other in others]
    mine = sum_over_patch(gram_share(last, other_last, gram(flat, others)))
    theirs = sibling(mine)
    total_rows = tiles * tile * count
    return rotate(mine, theirs, flat + [last], others + [other_last], total_rows, (lead, lag))


def solution(mesh):
    in_specs = (P("patch", "cols"), P("patch", None, None, None), P("patch", None), P("patch"))
    return jax.shard_map(
        on_device, mesh=mesh, in_specs=in_specs, out_specs=P("patch", "cols"), check_vma=False
    )
```

```python
import functools

import jax
import jax.numpy as jnp
from jax import lax
from jax.experimental import pallas as pl
from jax.experimental.pallas import tpu as pltpu
from jax.sharding import PartitionSpec as P

HALO_T = 4
STEPS = 3
ITERS = 8
WAYS = 4
LOAD_CUTS = 4
GRAM_ROWS = 1024
GROUP = 12

SMALL = pl.CostEstimate(flops=1000, bytes_accessed=1000, transcendentals=0)
LARGE = pl.CostEstimate(flops=10**11, bytes_accessed=1000, transcendentals=0)
SMALL_VMEM = pltpu.CompilerParams(vmem_limit_bytes=8 * 1024 * 1024)
ANY = pl.BlockSpec(memory_space=pl.ANY)
HBM = pl.BlockSpec(memory_space=pltpu.HBM)
VMEM = pl.BlockSpec(memory_space=pltpu.VMEM)
EDGES_MB, FIELDS_MB, BLOCKS_MB = 53, 50, 44
SMEM = pl.BlockSpec(memory_space=pltpu.SMEM)
F32, BF16 = jnp.float32, jnp.bfloat16


def dot(a, b):
    return jnp.dot(a, b, preferred_element_type=F32)


def tile_row(blocks, listed, field):
    wide = jnp.concatenate([blocks(n) for n in range(len(listed))], axis=1)
    tall = jnp.concatenate([field(tile) for tile in listed], axis=0)
    return dot(wide, tall)


def finish(acc, prev, alive):
    value = acc if prev is None else 2.0 * acc - prev.astype(F32)
    return jnp.where(alive, value, 0.0).astype(BF16)


def at_end(name):
    odd = lax.axis_index("patch") % 2
    return 1 - odd if name == "even" else odd


def live_count(table):
    return table[table.shape[0] - 1, 0]


def edges_kernel(table_ref, whole_ref, even_ref, odd_ref, sem, table):
    edge, tiles = HALO_T, whole_ref.shape[0]
    outs = {"even": even_ref, "odd": odd_ref}
    firsts = {name: at_end(name) * (tiles - edge) for name in outs}
    load([(whole_ref, firsts[name], outs[name]) for name in outs], sem, (table_ref, table))
    for name in outs:
        clear_dead(outs[name], firsts[name], live_count(table))


def clear_dead(ref, first, live):
    def clear(index, carry):
        ref[index] = jnp.zeros(ref.shape[1:], BF16)
        return carry

    count = ref.shape[0]
    lax.fori_loop(jnp.clip(live - first, 0, count), count, clear, 0)


def load(moves, sem, *whole):
    copies = []
    for source, first, target in moves:
        count = target.shape[0] // LOAD_CUTS
        for cut in range(LOAD_CUTS):
            copies.append(
                pltpu.make_async_copy(
                    source.at[pl.ds(first + cut * count, count)],
                    target.at[pl.ds(cut * count, count)],
                    sem.at[len(copies)],
                )
            )
    for source, target in whole:
        copies.append(pltpu.make_async_copy(source, target, sem.at[len(copies)]))
    for copy in copies:
        copy.start()
    for copy in copies:
        copy.wait()


def fields_kernel(
    table_ref, whole_ref, blocks_ref, inner_ref, even_blocks, odd_blocks, sem, table
):
    last = whole_ref.shape[0] - HALO_T
    moves = [
        (blocks_ref, at_end("even") * last, even_blocks),
        (blocks_ref, at_end("odd") * last, odd_blocks),
        (whole_ref, HALO_T, inner_ref),
    ]
    load(moves, sem, (table_ref, table))
    clear_dead(inner_ref, HALO_T, live_count(table))


def blocks_kernel(blocks_ref, inner_blocks, sem):
    load([(blocks_ref, HALO_T, inner_blocks)], sem)


def load_call(body, name, args, shapes, megabytes, table=()):
    return pl.pallas_call(
        body,
        in_specs=[VMEM] * len(table) + [HBM] * len(args),
        out_specs=[VMEM] * len(shapes),
        out_shape=shapes,
        scratch_shapes=[pltpu.SemaphoreType.DMA((len(shapes) * LOAD_CUTS + len(table),))]
        + [pltpu.SMEM(array.shape, array.dtype) for array in table],
        compiler_params=pltpu.CompilerParams(vmem_limit_bytes=megabytes * 1024 * 1024),
        cost_estimate=SMALL,
        name=name,
    )(*table, *args)


def masked_edges(table, start):
    shapes = [jax.ShapeDtypeStruct((HALO_T,) + start.shape[1:], BF16)] * 2
    return load_call(edges_kernel, "masked_edges", [start], shapes, EDGES_MB, [table])


def load_fields(table, start, blocks):
    inner = start.shape[0] - 2 * HALO_T
    shapes = [jax.ShapeDtypeStruct((inner,) + start.shape[1:], BF16)]
    shapes += [jax.ShapeDtypeStruct((HALO_T,) + blocks.shape[1:], blocks.dtype)] * 2
    return load_call(fields_kernel, "load_fields", [start, blocks], shapes, FIELDS_MB, [table])


def load_blocks(blocks):
    inner = blocks.shape[0] - 2 * HALO_T
    shapes = [jax.ShapeDtypeStruct((inner,) + blocks.shape[1:], blocks.dtype)]
    return load_call(blocks_kernel, "load_blocks", [blocks], shapes, BLOCKS_MB)[0]


def layout(name, tiles):
    edge, last = HALO_T, tiles - HALO_T
    if name == "inner":
        ends = [at_end(which) for which in ("even", "odd")]
        pieces = [(i, 0, edge, end * last) for i, end in enumerate(ends)]
        return edge, 0, pieces + [(2, 0, tiles - 2 * edge, edge)]
    end = at_end(name)
    pieces = [
        (0, 0, edge, 2 * edge * end), (1, 0, edge, edge), (2, 0, edge, (2 + end) * edge),
        (2, tiles - 3 * edge, edge, 3 * edge * (1 - end)),
    ]
    return end * last, end * last - edge, pieces


def rows_kernel(name, table_ref, *refs):
    sources, (out_ref, held, table, sem) = refs[:3], refs[-4:]
    blocks_ref = refs[-5]
    prev_ref = refs[3] if len(refs) == 9 else None
    fetch = pltpu.make_async_copy(table_ref, table, sem)
    fetch.start()
    nnz, tiles = blocks_ref.shape[1], table.shape[1]
    first, base, pieces = layout(name, tiles)
    for i, begin, count, slot in pieces:
        held[pl.ds(slot, count)] = sources[i][pl.ds(begin, count)]
    fetch.wait()
    live = live_count(table)
    shift = lax.axis_index("patch") * tiles + base
    rows = out_ref.shape[0]
    together = min(GROUP, rows)

    def group(index, carry):
        for r in range(together):
            row = index * together + r
            listed = [table[n, first + row] - shift for n in range(nnz)]
            acc = tile_row(lambda n: blocks_ref[row, n], listed, lambda c: held[c])
            prev = None if prev_ref is None else prev_ref[row]
            out_ref[row] = finish(acc, prev, first + row < live)
        return carry

    lax.fori_loop(0, rows // together, group, 0)


def tile_rows(name, table, blocks, sources, prev, cost):
    rows, _, tile, _ = blocks.shape
    width = sources[0].shape[-1]
    window = table.shape[1] if name == "inner" else 4 * HALO_T
    args = [table] + list(sources) + ([] if prev is None else [prev]) + [blocks]
    return pl.pallas_call(
        functools.partial(rows_kernel, name),
        in_specs=[VMEM] * len(args),
        out_specs=VMEM,
        out_shape=jax.ShapeDtypeStruct((rows, tile, width), BF16),
        scratch_shapes=[
            pltpu.VMEM((window, tile, width), BF16),
            pltpu.SMEM(table.shape, jnp.int32),
            pltpu.SemaphoreType.DMA,
        ],
        compiler_params=SMALL_VMEM,
        cost_estimate=cost,
        name="rows_" + name,
    )(*args)


ACROSS = (((0,), (0,)), ((), ()))


NEAR = (1, 2, 3), (2, 1, 3)
FAR = (1, 2, 3), (1, 2, 3)


def quarter_order():
    own = lax.axis_index("patch") % WAYS
    first_core = lax.axis_index("cols") == 0
    return [own] + [own ^ jnp.where(first_core, one, two) for one, two in zip(*NEAR)]


def add_gram(chunk, own_ref, other_ref, total):
    chunk = min(chunk, own_ref.shape[0])

    def add(index, carry):
        rows = pl.ds(pl.multiple_of(index * chunk, chunk), chunk)
        own = own_ref[rows, :]
        both = jnp.concatenate([own, other_ref[rows, :]], axis=1)
        total[...] += lax.dot_general(own, both, ACROSS, preferred_element_type=F32)
        return carry

    lax.fori_loop(0, own_ref.shape[0] // chunk, add, 0)


def gram_kernel(chunk, *refs):
    count = len(refs) // 2
    refs[-1][...] = jnp.zeros(refs[-1].shape, F32)
    for own_ref, other_ref in zip(refs[:count], refs[count:-1]):
        add_gram(chunk, own_ref, other_ref, refs[-1])


def share_kernel(chunk, own_ref, other_ref, start_ref, *refs):
    outs, (total, share) = refs[:WAYS], refs[WAYS:]
    total[...] = start_ref[...]
    add_gram(chunk, own_ref, other_ref, total)
    width = total.shape[0]
    half = width // 2
    own, other = total[:, :width], total[:, width:]
    first_core = lax.axis_index("cols") == 0
    second = jnp.where(first_core, other[:half, :half], other[:half, half:])
    third = jnp.where(first_core, other[:half, half:], other[half:, half:])
    blocks = [own[:half, :half], own[:half, half:], own[half:, half:], second, third]
    for i, block in enumerate(blocks):
        share[pl.ds(i * half, half), :] = block
    for out, quarter in zip(outs, quarter_order()):
        rows = out.shape[0]
        out[...] = share[pl.ds(pl.multiple_of(quarter * rows, 8), rows), :]


def gram_call(body, name, args, shape, scratch=(), outs=0):
    out_shape = jax.ShapeDtypeStruct(shape, F32)
    return pl.pallas_call(
        body,
        in_specs=[VMEM] * len(args),
        out_specs=[VMEM] * outs if outs else VMEM,
        out_shape=[out_shape] * outs if outs else out_shape,
        scratch_shapes=scratch,
        compiler_params=SMALL_VMEM,
        cost_estimate=SMALL,
        name=name,
    )(*args)


def gram(owns, others):
    width = owns[0].shape[1]
    body = functools.partial(gram_kernel, GRAM_ROWS)
    return gram_call(body, "gram", owns + others, (width, 2 * width))


def gram_share(own, other, start):
    rows, width = own.shape
    half = width // 2
    body = functools.partial(share_kernel, rows)
    scratch = [pltpu.VMEM((width, 2 * width), F32), pltpu.VMEM((5 * half, half), F32)]
    shape = (5 * half // WAYS, half)
    return gram_call(body, "gram_share", [own, other, start], shape, scratch, outs=WAYS)


def add_kernel(a, b, c, d, out):
    out[...] = (a[...] + b[...]) + (c[...] + d[...])


def join_kernel(*refs):
    parts, out = refs[:-1], refs[-1]
    rows = parts[0].shape[0]
    for part, quarter in zip(parts, quarter_order()):
        out[pl.ds(pl.multiple_of(quarter * rows, 8), rows), :] = part[...]


def sum_over_patch(parts):
    count = lax.axis_size("patch")
    rows, columns = parts[0].shape

    def add_four(values):
        return gram_call(add_kernel, "add_four", values, (rows, columns))

    def from_others(values, distances, stride=1):
        got = []
        for value, both in zip(values, zip(*distances)):
            pairs = [
                (core * count + i, core * count + (i ^ (distance * stride)))
                for core, distance in enumerate(both)
                for i in range(count)
            ]
            got.append(lax.ppermute(value, ("cols", "patch"), pairs))
        return got

    total = add_four([parts[0]] + from_others(parts[1:], NEAR))
    stride = WAYS
    while stride < count:
        total = add_four([total] + from_others([total] * (WAYS - 1), FAR, stride))
        stride *= WAYS
    quarters = [total] + from_others([total] * (WAYS - 1), NEAR)
    return gram_call(join_kernel, "join", quarters, (WAYS * rows, columns))


def split(value):
    high = value.astype(BF16)
    return high, (value - high.astype(F32)).astype(BF16)


def put(pair, blocks, right=False):
    width = blocks[0].shape[0]
    places = [(0, 0), (0, 1), (1, 1)]
    if right:
        blocks, places = tuple(blocks) + (blocks[1].T,), places + [(1, 0)]
    for (row, col), block in zip(places, blocks):
        for i, piece in enumerate(split(block)):
            pair[i, pl.ds(row * width, width), pl.ds(col * width, width)] = piece


def product3(left, right):
    return dot(
        jnp.concatenate([left[0], left[0], left[1]], axis=1),
        jnp.concatenate([right[0], right[1], right[0]], axis=0),
    )


def product(lefts, right):
    width = right.shape[1] // 2
    rows = [jnp.concatenate([left[i, :width, :] for left in lefts], axis=0) for i in range(2)]
    cols = [jnp.concatenate([left[i, :, width:] for left in lefts], axis=1) for i in range(2)]
    first = product3(rows, (right[0], right[1]))
    second = product3((right[0, width:, :], right[1, width:, :]), cols)
    out = []
    for i in range(len(lefts)):
        at = slice(i * width, (i + 1) * width)
        out.append((first[at, :width], first[at, width:], second[:, at]))
    return out


def combine(*terms, unit=0.0):
    width = terms[0][1][0].shape[0]
    row = lax.broadcasted_iota(jnp.int32, (width, width), 0)
    col = lax.broadcasted_iota(jnp.int32, (width, width), 1)
    diagonal = jnp.where(row == col, unit, 0.0)
    out = []
    for i in range(3):
        value = functools.reduce(jnp.add, [factor * matrix[i] for factor, matrix in terms])
        out.append(value if i == 1 else value + diagonal)
    return tuple(out)


def finish_kernel(total_rows, chunk, names, mine, theirs, *refs):
    fields, out_ref = refs[:6], refs[6]
    x_ref, x_held, x_pair, q_pair, u_pair, n_pair, v_pair, z_pair = refs[7:15]
    wide, result, sem, out_sem = refs[15:]
    part = lax.axis_index("cols")
    size = x_ref.shape[0]
    width = size // 2
    half = width // 2
    edge_size = fields[0].shape[0]
    end = wide.shape[0] - edge_size
    starts = [at_end(names[0]) * end, edge_size, at_end(names[1]) * end]
    copies = []
    for i, source in enumerate(fields):
        rows = pl.ds(pl.multiple_of(starts[i % 3], edge_size), source.shape[0])
        side = part if i < 3 else 1 - part
        target = wide.at[rows, pl.ds(pl.multiple_of(side * width, width), width)]
        copies.append(pltpu.make_async_copy(source, target, sem.at[i]))
    for copy in copies:
        copy.start()

    def block(side, index):
        rows = pl.ds(index * half, half)
        return jnp.where(part == side, mine[rows, :], theirs[rows, :])

    def place(row, col, value):
        x_ref[pl.ds(row * half, half), pl.ds(col * half, half)] = value

    for side in range(2):
        across = block(side, 1)
        place(2 * side, 2 * side, block(side, 0))
        place(2 * side, 2 * side + 1, across)
        place(2 * side + 1, 2 * side, across.T)
        place(2 * side + 1, 2 * side + 1, block(side, 2))
        for col in (0, 1):
            part_of = block(side, 3 + col)
            place(side, 2 + col, part_of if side == 0 else part_of.T)

    gram = x_ref[:width, :width], x_ref[:width, width:], x_ref[width:, width:]
    squares = gram[0] * gram[0] + 2.0 * (gram[1] * gram[1]) + gram[2] * gram[2]
    norm = jnp.sqrt(jnp.sum(squares, keepdims=True))

    def set_x(x):
        put(x_pair, x, right=True)
        for i, value in enumerate(x):
            x_held[i] = value

    def two_sweeps(first=False, last=False):
        x = tuple(x_held[i] for i in range(3))
        (q,) = product([x_pair], x_pair)
        put(q_pair, q)
        put(u_pair, combine((0.0625, q), (-0.5625, x), unit=1.6875), right=True)
        (qu,) = product([q_pair], u_pair)
        x = tuple(x_held[i] for i in range(3))
        n = combine((1.0, qu), (-2.4375, x), unit=2.25)
        put(n_pair, n, right=True)
        if last:
            return product([z_pair], n_pair)[0]
        if first:
            z = n
            (v,) = product([x_pair], n_pair)
        else:
            v, z = product([x_pair, z_pair], n_pair)
        put(v_pair, v)
        put(z_pair, z)
        set_x(product([v_pair], n_pair)[0])

    set_x(tuple(value / norm for value in gram))
    two_sweeps(first=True)

    def body(index, carry):
        two_sweeps()
        return carry

    lax.fori_loop(0, ITERS // 2 - 2, body, 0)
    first, across, second = two_sweeps(last=True)
    z_ref = x_ref
    z_ref[:width, :width] = first
    z_ref[:width, width:] = across
    z_ref[width:, :width] = across.T
    z_ref[width:, width:] = second
    own = pl.ds(pl.multiple_of(part * width, width), width)
    rotation = z_ref[:, own].astype(BF16)
    factor = jnp.sqrt(total_rows / norm)
    for copy in copies:
        copy.wait()
    count = wide.shape[0] // chunk
    outs = []
    for i in range(count):
        rows = pl.ds(i * chunk, chunk)
        result[rows, :] = (dot(wide[rows, :], rotation) * factor).astype(BF16)
        outs.append(pltpu.make_async_copy(result.at[rows], out_ref.at[rows], out_sem.at[i]))
        outs[-1].start()
    for out in outs:
        out.wait()


def rotate(mine, theirs, owns, others, total_rows, names):
    width = owns[0].shape[1]
    rows = sum(own.shape[0] for own in owns)
    size = 2 * width
    chunk = min(rows, 512)
    body = functools.partial(finish_kernel, float(total_rows), chunk, names)
    pair = pltpu.VMEM((2, size, size), BF16)
    return pl.pallas_call(
        body,
        in_specs=[VMEM, VMEM] + [ANY] * 6,
        out_specs=ANY,
        out_shape=jax.ShapeDtypeStruct((rows, width), BF16),
        scratch_shapes=[
            pltpu.VMEM((size, size), F32),
            pltpu.VMEM((3, width, width), F32),
            pair, pair, pair, pair, pair, pair,
            pltpu.VMEM((rows, size), BF16),
            pltpu.VMEM((rows, width), BF16),
            pltpu.SemaphoreType.DMA((6,)),
            pltpu.SemaphoreType.DMA((rows // chunk,)),
        ],
        compiler_params=pltpu.CompilerParams(vmem_limit_bytes=28 * 1024 * 1024),
        cost_estimate=pl.CostEstimate(
            flops=21 * 6 * size**3 + 2 * rows * size * width,
            bytes_accessed=3 * rows * width * 2,
            transcendentals=0,
        ),
        name="rotate",
    )(mine, theirs, *owns, *others)


def after(value, *others):
    return lax.optimization_barrier((value, others))[0]


def on_device(vectors, blocks, tile_cols, live_tiles):
    tiles, _, tile, _ = blocks.shape
    width = vectors.shape[1]
    count = lax.axis_size("patch")
    pairs = {
        "even": [(i, i ^ 1) for i in range(count)],
        "odd": [(i, ((i + 1) ^ 1) - 1) for i in range(1, count - 1)],
    }

    def exchange(name, value):
        return lax.ppermute(value, "patch", pairs[name])

    def sibling(value):
        return lax.ppermute(value, "cols", [(0, 1), (1, 0)])

    start = vectors.reshape(tiles, tile, width)
    table = jnp.concatenate([tile_cols.T, jnp.broadcast_to(live_tiles[None], (1, tiles))])

    edges = dict(zip(("even", "odd"), masked_edges(table, start)))
    lead, lag = "even", "odd"
    halo = {lead: exchange(lead, edges[lead])}
    inner, *edge_blocks = load_fields(after(table, edges[lead]), start, blocks)
    halo[lag] = exchange(lag, after(edges[lag], inner))
    stored = dict(zip(("even", "odd"), edge_blocks))
    prev = dict.fromkeys(("even", "odd", "inner"))

    def inner_rows(behind):
        sources = after(edges["even"], behind), edges["odd"], inner
        return tile_rows("inner", table, stored["inner"], sources, prev["inner"], SMALL)

    def edge_rows(name, behind, cost=SMALL):
        sources = after(halo[name], behind), edges[name], inner
        return tile_rows(name, table, stored[name], sources, prev[name], cost)

    for step in range(STEPS):
        final = step == STEPS - 1
        new = {}
        if final:
            new["inner"] = inner_rows(edges["odd"])
            new[lead] = edge_rows(lead, new["inner"])
            flat = [new[name].reshape(-1, width) for name in (lead, "inner")]
            others = [sibling(value) for value in flat]
            new[lag] = edge_rows(lag, new[lead], LARGE)
        else:
            new[lead] = edge_rows(lead, inner)
            halo[lead] = exchange(lead, new[lead])
            if step == 0:
                stored["inner"] = load_blocks(after(blocks, new[lead]))
            new["inner"] = inner_rows(new[lead])
            new[lag] = edge_rows(lag, new["inner"])
            halo[lag] = exchange(lag, new[lag])
            halo[lead] = after(halo[lead], new[lag])
        prev = dict(edges, inner=inner)
        edges, inner = {name: new[name] for name in edges}, new["inner"]
    last = edges[lag].reshape(-1, width)
    other_last = sibling(last)
    others = [after(other, last) for other in others]
    mine = sum_over_patch(gram_share(last, other_last, gram(flat, others)))
    theirs = sibling(mine)
    total_rows = tiles * tile * count
    return rotate(mine, theirs, flat + [last], others + [other_last], total_rows, (lead, lag))


def solution(mesh):
    in_specs = (P("patch", "cols"), P("patch", None, None, None), P("patch", None), P("patch"))
    return jax.shard_map(
        on_device, mesh=mesh, in_specs=in_specs, out_specs=P("patch", "cols"), check_vma=False
    )
```

```python
import functools

import jax
import jax.numpy as jnp
from jax import lax
from jax.experimental import pallas as pl
from jax.experimental.pallas import tpu as pltpu
from jax.sharding import PartitionSpec as P

HALO_T = 4
STEPS = 3
ITERS = 8
WAYS = 4
LOAD_CUTS = 4
GRAM_ROWS = 1024
GROUP = 12

SMALL = pl.CostEstimate(flops=1000, bytes_accessed=1000, transcendentals=0)
LARGE = pl.CostEstimate(flops=10**11, bytes_accessed=1000, transcendentals=0)
SMALL_VMEM = pltpu.CompilerParams(vmem_limit_bytes=8 * 1024 * 1024)
ANY = pl.BlockSpec(memory_space=pl.ANY)
HBM = pl.BlockSpec(memory_space=pltpu.HBM)
VMEM = pl.BlockSpec(memory_space=pltpu.VMEM)
EDGES_MB, FIELDS_MB, BLOCKS_MB = 53, 50, 44
SMEM = pl.BlockSpec(memory_space=pltpu.SMEM)
F32, BF16 = jnp.float32, jnp.bfloat16


def dot(a, b):
    return jnp.dot(a, b, preferred_element_type=F32)


def tile_row(blocks, listed, field):
    wide = jnp.concatenate([blocks(n) for n in range(len(listed))], axis=1)
    tall = jnp.concatenate([field(tile) for tile in listed], axis=0)
    return dot(wide, tall)


def finish(acc, prev, alive):
    value = acc if prev is None else 2.0 * acc - prev.astype(F32)
    return jnp.where(alive, value, 0.0).astype(BF16)


def at_end(name):
    odd = lax.axis_index("patch") % 2
    return 1 - odd if name == "even" else odd


def live_count(table):
    return table[table.shape[0] - 1, 0]


def edges_kernel(table_ref, whole_ref, even_ref, odd_ref, sem, table):
    edge, tiles = HALO_T, whole_ref.shape[0]
    outs = {"even": even_ref, "odd": odd_ref}
    firsts = {name: at_end(name) * (tiles - edge) for name in outs}
    load([(whole_ref, firsts[name], outs[name]) for name in outs], sem, (table_ref, table))
    for name in outs:
        clear_dead(outs[name], firsts[name], live_count(table))


def clear_dead(ref, first, live):
    def clear(index, carry):
        ref[index] = jnp.zeros(ref.shape[1:], BF16)
        return carry

    count = ref.shape[0]
    lax.fori_loop(jnp.clip(live - first, 0, count), count, clear, 0)


def load(moves, sem, *whole):
    copies = []
    for source, first, target in moves:
        count = target.shape[0] // LOAD_CUTS
        for cut in range(LOAD_CUTS):
            copies.append(
                pltpu.make_async_copy(
                    source.at[pl.ds(first + cut * count, count)],
                    target.at[pl.ds(cut * count, count)],
                    sem.at[len(copies)],
                )
            )
    for source, target in whole:
        copies.append(pltpu.make_async_copy(source, target, sem.at[len(copies)]))
    for copy in copies:
        copy.start()
    for copy in copies:
        copy.wait()


def fields_kernel(
    table_ref, whole_ref, blocks_ref, inner_ref, even_blocks, odd_blocks, sem, table
):
    last = whole_ref.shape[0] - HALO_T
    moves = [
        (blocks_ref, at_end("even") * last, even_blocks),
        (blocks_ref, at_end("odd") * last, odd_blocks),
        (whole_ref, HALO_T, inner_ref),
    ]
    load(moves, sem, (table_ref, table))
    clear_dead(inner_ref, HALO_T, live_count(table))


def blocks_kernel(blocks_ref, inner_blocks, sem):
    load([(blocks_ref, HALO_T, inner_blocks)], sem)


def load_call(body, name, args, shapes, megabytes, table=()):
    return pl.pallas_call(
        body,
        in_specs=[VMEM] * len(table) + [HBM] * len(args),
        out_specs=[VMEM] * len(shapes),
        out_shape=shapes,
        scratch_shapes=[pltpu.SemaphoreType.DMA((len(shapes) * LOAD_CUTS + len(table),))]
        + [pltpu.SMEM(array.shape, array.dtype) for array in table],
        compiler_params=pltpu.CompilerParams(vmem_limit_bytes=megabytes * 1024 * 1024),
        cost_estimate=SMALL,
        name=name,
    )(*table, *args)


def masked_edges(table, start):
    shapes = [jax.ShapeDtypeStruct((HALO_T,) + start.shape[1:], BF16)] * 2
    return load_call(edges_kernel, "masked_edges", [start], shapes, EDGES_MB, [table])


def load_fields(table, start, blocks):
    inner = start.shape[0] - 2 * HALO_T
    shapes = [jax.ShapeDtypeStruct((inner,) + start.shape[1:], BF16)]
    shapes += [jax.ShapeDtypeStruct((HALO_T,) + blocks.shape[1:], blocks.dtype)] * 2
    return load_call(fields_kernel, "load_fields", [start, blocks], shapes, FIELDS_MB, [table])


def load_blocks(blocks):
    inner = blocks.shape[0] - 2 * HALO_T
    shapes = [jax.ShapeDtypeStruct((inner,) + blocks.shape[1:], blocks.dtype)]
    return load_call(blocks_kernel, "load_blocks", [blocks], shapes, BLOCKS_MB)[0]


def layout(name, tiles):
    edge, last = HALO_T, tiles - HALO_T
    if name == "inner":
        ends = [at_end(which) for which in ("even", "odd")]
        pieces = [(i, 0, edge, end * last) for i, end in enumerate(ends)]
        return edge, 0, pieces + [(2, 0, tiles - 2 * edge, edge)]
    end = at_end(name)
    pieces = [
        (0, 0, edge, 2 * edge * end), (1, 0, edge, edge), (2, 0, edge, (2 + end) * edge),
        (2, tiles - 3 * edge, edge, 3 * edge * (1 - end)),
    ]
    return end * last, end * last - edge, pieces


def rows_kernel(name, table_ref, *refs):
    sources, (out_ref, held, table, sem) = refs[:3], refs[-4:]
    blocks_ref = refs[-5]
    prev_ref = refs[3] if len(refs) == 9 else None
    fetch = pltpu.make_async_copy(table_ref, table, sem)
    fetch.start()
    nnz, tiles = blocks_ref.shape[1], table.shape[1]
    first, base, pieces = layout(name, tiles)
    for i, begin, count, slot in pieces:
        held[pl.ds(slot, count)] = sources[i][pl.ds(begin, count)]
    fetch.wait()
    live = live_count(table)
    shift = lax.axis_index("patch") * tiles + base
    rows = out_ref.shape[0]
    together = min(GROUP, rows)

    def group(index, carry):
        for r in range(together):
            row = index * together + r
            listed = [table[n, first + row] - shift for n in range(nnz)]
            acc = tile_row(lambda n: blocks_ref[row, n], listed, lambda c: held[c])
            prev = None if prev_ref is None else prev_ref[row]
            out_ref[row] = finish(acc, prev, first + row < live)
        return carry

    lax.fori_loop(0, rows // together, group, 0)


def tile_rows(name, table, blocks, sources, prev, cost):
    rows, _, tile, _ = blocks.shape
    width = sources[0].shape[-1]
    window = table.shape[1] if name == "inner" else 4 * HALO_T
    args = [table] + list(sources) + ([] if prev is None else [prev]) + [blocks]
    return pl.pallas_call(
        functools.partial(rows_kernel, name),
        in_specs=[VMEM] * len(args),
        out_specs=VMEM,
        out_shape=jax.ShapeDtypeStruct((rows, tile, width), BF16),
        scratch_shapes=[
            pltpu.VMEM((window, tile, width), BF16),
            pltpu.SMEM(table.shape, jnp.int32),
            pltpu.SemaphoreType.DMA,
        ],
        compiler_params=SMALL_VMEM,
        cost_estimate=cost,
        name="rows_" + name,
    )(*args)


ACROSS = (((0,), (0,)), ((), ()))


SPREAD = (2, 3, 1), (1, 3, 2)
ACROSS_GROUPS = (3, 2, 1), (2, 3, 1)
GATHER = (3, 1, 2), (3, 2, 1)


def quarter_order(distances):
    own = lax.axis_index("patch") % WAYS
    first_core = lax.axis_index("cols") == 0
    return [own] + [own ^ jnp.where(first_core, one, two) for one, two in zip(*distances)]


def add_gram(chunk, own_ref, other_ref, total):
    chunk = min(chunk, own_ref.shape[0])

    def add(index, carry):
        rows = pl.ds(pl.multiple_of(index * chunk, chunk), chunk)
        own = own_ref[rows, :]
        both = jnp.concatenate([own, other_ref[rows, :]], axis=1)
        total[...] += lax.dot_general(own, both, ACROSS, preferred_element_type=F32)
        return carry

    lax.fori_loop(0, own_ref.shape[0] // chunk, add, 0)


def gram_kernel(chunk, *refs):
    count = len(refs) // 2
    refs[-1][...] = jnp.zeros(refs[-1].shape, F32)
    for own_ref, other_ref in zip(refs[:count], refs[count:-1]):
        add_gram(chunk, own_ref, other_ref, refs[-1])


def share_kernel(chunk, own_ref, other_ref, start_ref, *refs):
    outs, (total, share) = refs[:WAYS], refs[WAYS:]
    total[...] = start_ref[...]
    add_gram(chunk, own_ref, other_ref, total)
    width = total.shape[0]
    half = width // 2
    own, other = total[:, :width], total[:, width:]
    first_core = lax.axis_index("cols") == 0
    second = jnp.where(first_core, other[:half, :half], other[:half, half:])
    third = jnp.where(first_core, other[:half, half:], other[half:, half:])
    blocks = [own[:half, :half], own[:half, half:], own[half:, half:], second, third]
    for i, block in enumerate(blocks):
        share[pl.ds(i * half, half), :] = block
    for out, quarter in zip(outs, quarter_order(SPREAD)):
        rows = out.shape[0]
        out[...] = share[pl.ds(pl.multiple_of(quarter * rows, 8), rows), :]


def gram_call(body, name, args, shape, scratch=(), outs=0):
    out_shape = jax.ShapeDtypeStruct(shape, F32)
    return pl.pallas_call(
        body,
        in_specs=[VMEM] * len(args),
        out_specs=[VMEM] * outs if outs else VMEM,
        out_shape=[out_shape] * outs if outs else out_shape,
        scratch_shapes=scratch,
        compiler_params=SMALL_VMEM,
        cost_estimate=SMALL,
        name=name,
    )(*args)


def gram(owns, others):
    width = owns[0].shape[1]
    body = functools.partial(gram_kernel, GRAM_ROWS)
    return gram_call(body, "gram", owns + others, (width, 2 * width))


def gram_share(own, other, start):
    rows, width = own.shape
    half = width // 2
    body = functools.partial(share_kernel, rows)
    scratch = [pltpu.VMEM((width, 2 * width), F32), pltpu.VMEM((5 * half, half), F32)]
    shape = (5 * half // WAYS, half)
    return gram_call(body, "gram_share", [own, other, start], shape, scratch, outs=WAYS)


def add_kernel(a, b, c, d, out):
    out[...] = (a[...] + b[...]) + (c[...] + d[...])


def join_kernel(*refs):
    parts, out = refs[:-1], refs[-1]
    rows = parts[0].shape[0]
    for part, quarter in zip(parts, quarter_order(GATHER)):
        out[pl.ds(pl.multiple_of(quarter * rows, 8), rows), :] = part[...]


def sum_over_patch(parts):
    count = lax.axis_size("patch")
    rows, columns = parts[0].shape

    def add_four(values):
        return gram_call(add_kernel, "add_four", values, (rows, columns))

    def from_others(values, distances, stride=1):
        got = []
        for value, both in zip(values, zip(*distances)):
            pairs = [
                (core * count + i, core * count + (i ^ (distance * stride)))
                for core, distance in enumerate(both)
                for i in range(count)
            ]
            got.append(lax.ppermute(value, ("cols", "patch"), pairs))
        return got

    total = add_four([parts[0]] + from_others(parts[1:], SPREAD))
    stride = WAYS
    while stride < count:
        total = add_four([total] + from_others([total] * (WAYS - 1), ACROSS_GROUPS, stride))
        stride *= WAYS
    quarters = [total] + from_others([total] * (WAYS - 1), GATHER)
    return gram_call(join_kernel, "join", quarters, (WAYS * rows, columns))


def split(value):
    high = value.astype(BF16)
    return high, (value - high.astype(F32)).astype(BF16)


def put(pair, blocks, right=False):
    width = blocks[0].shape[0]
    places = [(0, 0), (0, 1), (1, 1)]
    if right:
        blocks, places = tuple(blocks) + (blocks[1].T,), places + [(1, 0)]
    for (row, col), block in zip(places, blocks):
        for i, piece in enumerate(split(block)):
            pair[i, pl.ds(row * width, width), pl.ds(col * width, width)] = piece


def product3(left, right):
    return dot(
        jnp.concatenate([left[0], left[0], left[1]], axis=1),
        jnp.concatenate([right[0], right[1], right[0]], axis=0),
    )


def product(lefts, right):
    width = right.shape[1] // 2
    rows = [jnp.concatenate([left[i, :width, :] for left in lefts], axis=0) for i in range(2)]
    cols = [jnp.concatenate([left[i, :, width:] for left in lefts], axis=1) for i in range(2)]
    first = product3(rows, (right[0], right[1]))
    second = product3((right[0, width:, :], right[1, width:, :]), cols)
    out = []
    for i in range(len(lefts)):
        at = slice(i * width, (i + 1) * width)
        out.append((first[at, :width], first[at, width:], second[:, at]))
    return out


def combine(*terms, unit=0.0):
    width = terms[0][1][0].shape[0]
    row = lax.broadcasted_iota(jnp.int32, (width, width), 0)
    col = lax.broadcasted_iota(jnp.int32, (width, width), 1)
    diagonal = jnp.where(row == col, unit, 0.0)
    out = []
    for i in range(3):
        value = functools.reduce(jnp.add, [factor * matrix[i] for factor, matrix in terms])
        out.append(value if i == 1 else value + diagonal)
    return tuple(out)


def finish_kernel(total_rows, chunk, names, mine, theirs, *refs):
    fields, out_ref = refs[:6], refs[6]
    x_ref, x_held, x_pair, q_pair, u_pair, n_pair, v_pair, z_pair = refs[7:15]
    wide, result, sem, out_sem = refs[15:]
    part = lax.axis_index("cols")
    size = x_ref.shape[0]
    width = size // 2
    half = width // 2
    edge_size = fields[0].shape[0]
    end = wide.shape[0] - edge_size
    starts = [at_end(names[0]) * end, edge_size, at_end(names[1]) * end]
    copies = []
    for i, source in enumerate(fields):
        rows = pl.ds(pl.multiple_of(starts[i % 3], edge_size), source.shape[0])
        side = part if i < 3 else 1 - part
        target = wide.at[rows, pl.ds(pl.multiple_of(side * width, width), width)]
        copies.append(pltpu.make_async_copy(source, target, sem.at[i]))
    for copy in copies:
        copy.start()

    def block(side, index):
        rows = pl.ds(index * half, half)
        return jnp.where(part == side, mine[rows, :], theirs[rows, :])

    def place(row, col, value):
        x_ref[pl.ds(row * half, half), pl.ds(col * half, half)] = value

    for side in range(2):
        across = block(side, 1)
        place(2 * side, 2 * side, block(side, 0))
        place(2 * side, 2 * side + 1, across)
        place(2 * side + 1, 2 * side, across.T)
        place(2 * side + 1, 2 * side + 1, block(side, 2))
        for col in (0, 1):
            part_of = block(side, 3 + col)
            place(side, 2 + col, part_of if side == 0 else part_of.T)

    gram = x_ref[:width, :width], x_ref[:width, width:], x_ref[width:, width:]
    squares = gram[0] * gram[0] + 2.0 * (gram[1] * gram[1]) + gram[2] * gram[2]
    norm = jnp.sqrt(jnp.sum(squares, keepdims=True))

    def set_x(x):
        put(x_pair, x, right=True)
        for i, value in enumerate(x):
            x_held[i] = value

    def two_sweeps(first=False, last=False):
        x = tuple(x_held[i] for i in range(3))
        (q,) = product([x_pair], x_pair)
        put(q_pair, q)
        put(u_pair, combine((0.0625, q), (-0.5625, x), unit=1.6875), right=True)
        (qu,) = product([q_pair], u_pair)
        x = tuple(x_held[i] for i in range(3))
        n = combine((1.0, qu), (-2.4375, x), unit=2.25)
        put(n_pair, n, right=True)
        if last:
            return product([z_pair], n_pair)[0]
        if first:
            z = n
            (v,) = product([x_pair], n_pair)
        else:
            v, z = product([x_pair, z_pair], n_pair)
        put(v_pair, v)
        put(z_pair, z)
        set_x(product([v_pair], n_pair)[0])

    set_x(tuple(value / norm for value in gram))
    two_sweeps(first=True)

    def body(index, carry):
        two_sweeps()
        return carry

    lax.fori_loop(0, ITERS // 2 - 2, body, 0)
    first, across, second = two_sweeps(last=True)
    z_ref = x_ref
    z_ref[:width, :width] = first
    z_ref[:width, width:] = across
    z_ref[width:, :width] = across.T
    z_ref[width:, width:] = second
    own = pl.ds(pl.multiple_of(part * width, width), width)
    rotation = z_ref[:, own].astype(BF16)
    factor = jnp.sqrt(total_rows / norm)
    for copy in copies:
        copy.wait()
    count = wide.shape[0] // chunk
    outs = []
    for i in range(count):
        rows = pl.ds(i * chunk, chunk)
        result[rows, :] = (dot(wide[rows, :], rotation) * factor).astype(BF16)
        outs.append(pltpu.make_async_copy(result.at[rows], out_ref.at[rows], out_sem.at[i]))
        outs[-1].start()
    for out in outs:
        out.wait()


def rotate(mine, theirs, owns, others, total_rows, names):
    width = owns[0].shape[1]
    rows = sum(own.shape[0] for own in owns)
    size = 2 * width
    chunk = min(rows, 512)
    body = functools.partial(finish_kernel, float(total_rows), chunk, names)
    pair = pltpu.VMEM((2, size, size), BF16)
    return pl.pallas_call(
        body,
        in_specs=[VMEM, VMEM] + [ANY] * 6,
        out_specs=ANY,
        out_shape=jax.ShapeDtypeStruct((rows, width), BF16),
        scratch_shapes=[
            pltpu.VMEM((size, size), F32),
            pltpu.VMEM((3, width, width), F32),
            pair, pair, pair, pair, pair, pair,
            pltpu.VMEM((rows, size), BF16),
            pltpu.VMEM((rows, width), BF16),
            pltpu.SemaphoreType.DMA((6,)),
            pltpu.SemaphoreType.DMA((rows // chunk,)),
        ],
        compiler_params=pltpu.CompilerParams(vmem_limit_bytes=28 * 1024 * 1024),
        cost_estimate=pl.CostEstimate(
            flops=21 * 6 * size**3 + 2 * rows * size * width,
            bytes_accessed=3 * rows * width * 2,
            transcendentals=0,
        ),
        name="rotate",
    )(mine, theirs, *owns, *others)


def after(value, *others):
    return lax.optimization_barrier((value, others))[0]


def on_device(vectors, blocks, tile_cols, live_tiles):
    tiles, _, tile, _ = blocks.shape
    width = vectors.shape[1]
    count = lax.axis_size("patch")
    pairs = {
        "even": [(i, i ^ 1) for i in range(count)],
        "odd": [(i, ((i + 1) ^ 1) - 1) for i in range(1, count - 1)],
    }

    def exchange(name, value):
        return lax.ppermute(value, "patch", pairs[name])

    def sibling(value):
        return lax.ppermute(value, "cols", [(0, 1), (1, 0)])

    start = vectors.reshape(tiles, tile, width)
    table = jnp.concatenate([tile_cols.T, jnp.broadcast_to(live_tiles[None], (1, tiles))])

    edges = dict(zip(("even", "odd"), masked_edges(table, start)))
    lead, lag = "even", "odd"
    halo = {lead: exchange(lead, edges[lead])}
    inner, *edge_blocks = load_fields(after(table, edges[lead]), start, blocks)
    halo[lag] = exchange(lag, after(edges[lag], inner))
    stored = dict(zip(("even", "odd"), edge_blocks))
    prev = dict.fromkeys(("even", "odd", "inner"))

    def inner_rows(behind):
        sources = after(edges["even"], behind), edges["odd"], inner
        return tile_rows("inner", table, stored["inner"], sources, prev["inner"], SMALL)

    def edge_rows(name, behind, cost=SMALL):
        sources = after(halo[name], behind), edges[name], inner
        return tile_rows(name, table, stored[name], sources, prev[name], cost)

    for step in range(STEPS):
        final = step == STEPS - 1
        new = {}
        if final:
            new["inner"] = inner_rows(edges["odd"])
            new[lead] = edge_rows(lead, new["inner"])
            flat = [new[name].reshape(-1, width) for name in (lead, "inner")]
            others = [sibling(value) for value in flat]
            new[lag] = edge_rows(lag, new[lead], LARGE)
        else:
            new[lead] = edge_rows(lead, inner)
            halo[lead] = exchange(lead, new[lead])
            if step == 0:
                stored["inner"] = load_blocks(after(blocks, new[lead]))
            new["inner"] = inner_rows(new[lead])
            new[lag] = edge_rows(lag, new["inner"])
            halo[lag] = exchange(lag, new[lag])
            halo[lead] = after(halo[lead], new[lag])
        prev = dict(edges, inner=inner)
        edges, inner = {name: new[name] for name in edges}, new["inner"]
    last = edges[lag].reshape(-1, width)
    other_last = sibling(last)
    others = [after(other, last) for other in others]
    mine = sum_over_patch(gram_share(last, other_last, gram(flat, others)))
    theirs = sibling(mine)
    total_rows = tiles * tile * count
    return rotate(mine, theirs, flat + [last], others + [other_last], total_rows, (lead, lag))


def solution(mesh):
    in_specs = (P("patch", "cols"), P("patch", None, None, None), P("patch", None), P("patch"))
    return jax.shard_map(
        on_device, mesh=mesh, in_specs=in_specs, out_specs=P("patch", "cols"), check_vma=False
    )
```

```python
import functools

import jax
import jax.numpy as jnp
from jax import lax
from jax.experimental import pallas as pl
from jax.experimental.pallas import tpu as pltpu
from jax.sharding import PartitionSpec as P

HALO_T = 4
STEPS = 3
ITERS = 8
WAYS = 4
LOAD_CUTS = 4
GRAM_ROWS = 1536
GROUP = 12

SMALL = pl.CostEstimate(flops=1000, bytes_accessed=1000, transcendentals=0)
LARGE = pl.CostEstimate(flops=10**11, bytes_accessed=1000, transcendentals=0)
SMALL_VMEM = pltpu.CompilerParams(vmem_limit_bytes=8 * 1024 * 1024)
ANY = pl.BlockSpec(memory_space=pl.ANY)
HBM = pl.BlockSpec(memory_space=pltpu.HBM)
VMEM = pl.BlockSpec(memory_space=pltpu.VMEM)
EDGES_MB, FIELDS_MB, BLOCKS_MB = 53, 50, 44
SMEM = pl.BlockSpec(memory_space=pltpu.SMEM)
F32, BF16 = jnp.float32, jnp.bfloat16


def dot(a, b):
    return jnp.dot(a, b, preferred_element_type=F32)


def tile_row(blocks, listed, field):
    wide = jnp.concatenate([blocks(n) for n in range(len(listed))], axis=1)
    tall = jnp.concatenate([field(tile) for tile in listed], axis=0)
    return dot(wide, tall)


def finish(acc, prev, alive):
    value = acc if prev is None else 2.0 * acc - prev.astype(F32)
    return jnp.where(alive, value, 0.0).astype(BF16)


def at_end(name):
    odd = lax.axis_index("patch") % 2
    return 1 - odd if name == "even" else odd


def live_count(table):
    return table[table.shape[0] - 1, 0]


def edges_kernel(table_ref, whole_ref, even_ref, odd_ref, sem, table):
    edge, tiles = HALO_T, whole_ref.shape[0]
    outs = {"even": even_ref, "odd": odd_ref}
    firsts = {name: at_end(name) * (tiles - edge) for name in outs}
    load([(whole_ref, firsts[name], outs[name]) for name in outs], sem, (table_ref, table))
    for name in outs:
        clear_dead(outs[name], firsts[name], live_count(table))


def clear_dead(ref, first, live):
    def clear(index, carry):
        ref[index] = jnp.zeros(ref.shape[1:], BF16)
        return carry

    count = ref.shape[0]
    lax.fori_loop(jnp.clip(live - first, 0, count), count, clear, 0)


def load(moves, sem, *whole):
    copies = []
    for source, first, target in moves:
        count = target.shape[0] // LOAD_CUTS
        for cut in range(LOAD_CUTS):
            copies.append(
                pltpu.make_async_copy(
                    source.at[pl.ds(first + cut * count, count)],
                    target.at[pl.ds(cut * count, count)],
                    sem.at[len(copies)],
                )
            )
    for source, target in whole:
        copies.append(pltpu.make_async_copy(source, target, sem.at[len(copies)]))
    for copy in copies:
        copy.start()
    for copy in copies:
        copy.wait()


def fields_kernel(
    table_ref, whole_ref, blocks_ref, inner_ref, even_blocks, odd_blocks, sem, table
):
    last = whole_ref.shape[0] - HALO_T
    moves = [
        (blocks_ref, at_end("even") * last, even_blocks),
        (blocks_ref, at_end("odd") * last, odd_blocks),
        (whole_ref, HALO_T, inner_ref),
    ]
    load(moves, sem, (table_ref, table))
    clear_dead(inner_ref, HALO_T, live_count(table))


def blocks_kernel(blocks_ref, inner_blocks, sem):
    load([(blocks_ref, HALO_T, inner_blocks)], sem)


def load_call(body, name, args, shapes, megabytes, table=()):
    return pl.pallas_call(
        body,
        in_specs=[VMEM] * len(table) + [HBM] * len(args),
        out_specs=[VMEM] * len(shapes),
        out_shape=shapes,
        scratch_shapes=[pltpu.SemaphoreType.DMA((len(shapes) * LOAD_CUTS + len(table),))]
        + [pltpu.SMEM(array.shape, array.dtype) for array in table],
        compiler_params=pltpu.CompilerParams(vmem_limit_bytes=megabytes * 1024 * 1024),
        cost_estimate=SMALL,
        name=name,
    )(*table, *args)


def masked_edges(table, start):
    shapes = [jax.ShapeDtypeStruct((HALO_T,) + start.shape[1:], BF16)] * 2
    return load_call(edges_kernel, "masked_edges", [start], shapes, EDGES_MB, [table])


def load_fields(table, start, blocks):
    inner = start.shape[0] - 2 * HALO_T
    shapes = [jax.ShapeDtypeStruct((inner,) + start.shape[1:], BF16)]
    shapes += [jax.ShapeDtypeStruct((HALO_T,) + blocks.shape[1:], blocks.dtype)] * 2
    return load_call(fields_kernel, "load_fields", [start, blocks], shapes, FIELDS_MB, [table])


def load_blocks(blocks):
    inner = blocks.shape[0] - 2 * HALO_T
    shapes = [jax.ShapeDtypeStruct((inner,) + blocks.shape[1:], blocks.dtype)]
    return load_call(blocks_kernel, "load_blocks", [blocks], shapes, BLOCKS_MB)[0]


def layout(name, tiles):
    edge, last = HALO_T, tiles - HALO_T
    if name == "inner":
        ends = [at_end(which) for which in ("even", "odd")]
        pieces = [(i, 0, edge, end * last) for i, end in enumerate(ends)]
        return edge, 0, pieces + [(2, 0, tiles - 2 * edge, edge)]
    end = at_end(name)
    pieces = [
        (0, 0, edge, 2 * edge * end), (1, 0, edge, edge), (2, 0, edge, (2 + end) * edge),
        (2, tiles - 3 * edge, edge, 3 * edge * (1 - end)),
    ]
    return end * last, end * last - edge, pieces


def rows_kernel(name, table_ref, *refs):
    sources, (out_ref, held, table, sem) = refs[:3], refs[-4:]
    blocks_ref = refs[-5]
    prev_ref = refs[3] if len(refs) == 9 else None
    fetch = pltpu.make_async_copy(table_ref, table, sem)
    fetch.start()
    nnz, tiles = blocks_ref.shape[1], table.shape[1]
    first, base, pieces = layout(name, tiles)
    for i, begin, count, slot in pieces:
        held[pl.ds(slot, count)] = sources[i][pl.ds(begin, count)]
    fetch.wait()
    live = live_count(table)
    shift = lax.axis_index("patch") * tiles + base
    rows = out_ref.shape[0]
    together = min(GROUP, rows)

    def group(index, carry):
        for r in range(together):
            row = index * together + r
            listed = [table[n, first + row] - shift for n in range(nnz)]
            acc = tile_row(lambda n: blocks_ref[row, n], listed, lambda c: held[c])
            prev = None if prev_ref is None else prev_ref[row]
            out_ref[row] = finish(acc, prev, first + row < live)
        return carry

    lax.fori_loop(0, rows // together, group, 0)


def tile_rows(name, table, blocks, sources, prev, cost):
    rows, _, tile, _ = blocks.shape
    width = sources[0].shape[-1]
    window = table.shape[1] if name == "inner" else 4 * HALO_T
    args = [table] + list(sources) + ([] if prev is None else [prev]) + [blocks]
    return pl.pallas_call(
        functools.partial(rows_kernel, name),
        in_specs=[VMEM] * len(args),
        out_specs=VMEM,
        out_shape=jax.ShapeDtypeStruct((rows, tile, width), BF16),
        scratch_shapes=[
            pltpu.VMEM((window, tile, width), BF16),
            pltpu.SMEM(table.shape, jnp.int32),
            pltpu.SemaphoreType.DMA,
        ],
        compiler_params=SMALL_VMEM,
        cost_estimate=cost,
        name="rows_" + name,
    )(*args)


ACROSS = (((0,), (0,)), ((), ()))


SPREAD = (2, 3, 1), (1, 3, 2)
ACROSS_GROUPS = (3, 2, 1), (3, 2, 1)
GATHER = (3, 1, 2), (3, 2, 1)


def quarter_order(distances):
    own = lax.axis_index("patch") % WAYS
    first_core = lax.axis_index("cols") == 0
    return [own] + [own ^ jnp.where(first_core, one, two) for one, two in zip(*distances)]


def add_gram(chunk, own_ref, other_ref, total):
    chunk = min(chunk, own_ref.shape[0])

    def add(index, carry):
        rows = pl.ds(pl.multiple_of(index * chunk, chunk), chunk)
        own = own_ref[rows, :]
        both = jnp.concatenate([own, other_ref[rows, :]], axis=1)
        total[...] += lax.dot_general(own, both, ACROSS, preferred_element_type=F32)
        return carry

    lax.fori_loop(0, own_ref.shape[0] // chunk, add, 0)


def gram_kernel(chunk, *refs):
    count = len(refs) // 2
    refs[-1][...] = jnp.zeros(refs[-1].shape, F32)
    for own_ref, other_ref in zip(refs[:count], refs[count:-1]):
        add_gram(chunk, own_ref, other_ref, refs[-1])


def share_kernel(chunk, own_ref, other_ref, start_ref, *refs):
    outs, (total, share) = refs[:WAYS], refs[WAYS:]
    total[...] = start_ref[...]
    add_gram(chunk, own_ref, other_ref, total)
    width = total.shape[0]
    half = width // 2
    own, other = total[:, :width], total[:, width:]
    first_core = lax.axis_index("cols") == 0
    second = jnp.where(first_core, other[:half, :half], other[:half, half:])
    third = jnp.where(first_core, other[:half, half:], other[half:, half:])
    blocks = [own[:half, :half], own[:half, half:], own[half:, half:], second, third]
    for i, block in enumerate(blocks):
        share[pl.ds(i * half, half), :] = block
    for out, quarter in zip(outs, quarter_order(SPREAD)):
        rows = out.shape[0]
        out[...] = share[pl.ds(pl.multiple_of(quarter * rows, 8), rows), :]


def gram_call(body, name, args, shape, scratch=(), outs=0):
    out_shape = jax.ShapeDtypeStruct(shape, F32)
    return pl.pallas_call(
        body,
        in_specs=[VMEM] * len(args),
        out_specs=[VMEM] * outs if outs else VMEM,
        out_shape=[out_shape] * outs if outs else out_shape,
        scratch_shapes=scratch,
        compiler_params=SMALL_VMEM,
        cost_estimate=SMALL,
        name=name,
    )(*args)


def gram(owns, others):
    width = owns[0].shape[1]
    body = functools.partial(gram_kernel, GRAM_ROWS)
    return gram_call(body, "gram", owns + others, (width, 2 * width))


def gram_share(own, other, start):
    rows, width = own.shape
    half = width // 2
    body = functools.partial(share_kernel, rows)
    scratch = [pltpu.VMEM((width, 2 * width), F32), pltpu.VMEM((5 * half, half), F32)]
    shape = (5 * half // WAYS, half)
    return gram_call(body, "gram_share", [own, other, start], shape, scratch, outs=WAYS)


def add_kernel(a, b, c, d, out):
    out[...] = (a[...] + b[...]) + (c[...] + d[...])


def join_kernel(*refs):
    parts, out = refs[:-1], refs[-1]
    rows = parts[0].shape[0]
    for part, quarter in zip(parts, quarter_order(GATHER)):
        out[pl.ds(pl.multiple_of(quarter * rows, 8), rows), :] = part[...]


def sum_over_patch(parts):
    count = lax.axis_size("patch")
    rows, columns = parts[0].shape

    def add_four(values):
        return gram_call(add_kernel, "add_four", values, (rows, columns))

    def from_others(values, distances, stride=1):
        got = []
        for value, both in zip(values, zip(*distances)):
            pairs = [
                (core * count + i, core * count + (i ^ (distance * stride)))
                for core, distance in enumerate(both)
                for i in range(count)
            ]
            got.append(lax.ppermute(value, ("cols", "patch"), pairs))
        return got

    total = add_four([parts[0]] + from_others(parts[1:], SPREAD))
    stride = WAYS
    while stride < count:
        total = add_four([total] + from_others([total] * (WAYS - 1), ACROSS_GROUPS, stride))
        stride *= WAYS
    quarters = [total] + from_others([total] * (WAYS - 1), GATHER)
    return gram_call(join_kernel, "join", quarters, (WAYS * rows, columns))


def split(value):
    high = value.astype(BF16)
    return high, (value - high.astype(F32)).astype(BF16)


def put(pair, blocks, right=False):
    width = blocks[0].shape[0]
    places = [(0, 0), (0, 1), (1, 1)]
    if right:
        blocks, places = tuple(blocks) + (blocks[1].T,), places + [(1, 0)]
    for (row, col), block in zip(places, blocks):
        for i, piece in enumerate(split(block)):
            pair[i, pl.ds(row * width, width), pl.ds(col * width, width)] = piece


def product3(left, right):
    return dot(
        jnp.concatenate([left[0], left[0], left[1]], axis=1),
        jnp.concatenate([right[0], right[1], right[0]], axis=0),
    )


def product(lefts, right):
    width = right.shape[1] // 2
    rows = [jnp.concatenate([left[i, :width, :] for left in lefts], axis=0) for i in range(2)]
    cols = [jnp.concatenate([left[i, :, width:] for left in lefts], axis=1) for i in range(2)]
    first = product3(rows, (right[0], right[1]))
    second = product3((right[0, width:, :], right[1, width:, :]), cols)
    out = []
    for i in range(len(lefts)):
        at = slice(i * width, (i + 1) * width)
        out.append((first[at, :width], first[at, width:], second[:, at]))
    return out


def combine(*terms, unit=0.0):
    width = terms[0][1][0].shape[0]
    row = lax.broadcasted_iota(jnp.int32, (width, width), 0)
    col = lax.broadcasted_iota(jnp.int32, (width, width), 1)
    diagonal = jnp.where(row == col, unit, 0.0)
    out = []
    for i in range(3):
        value = functools.reduce(jnp.add, [factor * matrix[i] for factor, matrix in terms])
        out.append(value if i == 1 else value + diagonal)
    return tuple(out)


def finish_kernel(total_rows, chunk, names, mine, theirs, *refs):
    fields, out_ref = refs[:6], refs[6]
    x_ref, x_held, x_pair, q_pair, u_pair, n_pair, v_pair, z_pair = refs[7:15]
    wide, result, sem, out_sem = refs[15:]
    part = lax.axis_index("cols")
    size = x_ref.shape[0]
    width = size // 2
    half = width // 2
    edge_size = fields[0].shape[0]
    end = wide.shape[0] - edge_size
    starts = [at_end(names[0]) * end, edge_size, at_end(names[1]) * end]
    copies = []
    for i, source in enumerate(fields):
        rows = pl.ds(pl.multiple_of(starts[i % 3], edge_size), source.shape[0])
        side = part if i < 3 else 1 - part
        target = wide.at[rows, pl.ds(pl.multiple_of(side * width, width), width)]
        copies.append(pltpu.make_async_copy(source, target, sem.at[i]))
    for copy in copies:
        copy.start()

    def block(side, index):
        rows = pl.ds(index * half, half)
        return jnp.where(part == side, mine[rows, :], theirs[rows, :])

    def place(row, col, value):
        x_ref[pl.ds(row * half, half), pl.ds(col * half, half)] = value

    for side in range(2):
        across = block(side, 1)
        place(2 * side, 2 * side, block(side, 0))
        place(2 * side, 2 * side + 1, across)
        place(2 * side + 1, 2 * side, across.T)
        place(2 * side + 1, 2 * side + 1, block(side, 2))
        for col in (0, 1):
            part_of = block(side, 3 + col)
            place(side, 2 + col, part_of if side == 0 else part_of.T)

    gram = x_ref[:width, :width], x_ref[:width, width:], x_ref[width:, width:]
    squares = gram[0] * gram[0] + 2.0 * (gram[1] * gram[1]) + gram[2] * gram[2]
    norm = jnp.sqrt(jnp.sum(squares, keepdims=True))

    def set_x(x):
        put(x_pair, x, right=True)
        for i, value in enumerate(x):
            x_held[i] = value

    def two_sweeps(first=False, last=False):
        x = tuple(x_held[i] for i in range(3))
        (q,) = product([x_pair], x_pair)
        put(q_pair, q)
        put(u_pair, combine((0.0625, q), (-0.5625, x), unit=1.6875), right=True)
        (qu,) = product([q_pair], u_pair)
        x = tuple(x_held[i] for i in range(3))
        n = combine((1.0, qu), (-2.4375, x), unit=2.25)
        put(n_pair, n, right=True)
        if last:
            return product([z_pair], n_pair)[0]
        if first:
            z = n
            (v,) = product([x_pair], n_pair)
        else:
            v, z = product([x_pair, z_pair], n_pair)
        put(v_pair, v)
        put(z_pair, z)
        set_x(product([v_pair], n_pair)[0])

    set_x(tuple(value / norm for value in gram))
    two_sweeps(first=True)

    def body(index, carry):
        two_sweeps()
        return carry

    lax.fori_loop(0, ITERS // 2 - 2, body, 0)
    first, across, second = two_sweeps(last=True)
    z_ref = x_ref
    z_ref[:width, :width] = first
    z_ref[:width, width:] = across
    z_ref[width:, :width] = across.T
    z_ref[width:, width:] = second
    own = pl.ds(pl.multiple_of(part * width, width), width)
    rotation = z_ref[:, own].astype(BF16)
    factor = jnp.sqrt(total_rows / norm)
    for copy in copies:
        copy.wait()
    count = wide.shape[0] // chunk
    outs = []
    for i in range(count):
        rows = pl.ds(i * chunk, chunk)
        result[rows, :] = (dot(wide[rows, :], rotation) * factor).astype(BF16)
        outs.append(pltpu.make_async_copy(result.at[rows], out_ref.at[rows], out_sem.at[i]))
        outs[-1].start()
    for out in outs:
        out.wait()


def rotate(mine, theirs, owns, others, total_rows, names):
    width = owns[0].shape[1]
    rows = sum(own.shape[0] for own in owns)
    size = 2 * width
    chunk = min(rows, 512)
    body = functools.partial(finish_kernel, float(total_rows), chunk, names)
    pair = pltpu.VMEM((2, size, size), BF16)
    return pl.pallas_call(
        body,
        in_specs=[VMEM, VMEM] + [ANY] * 6,
        out_specs=ANY,
        out_shape=jax.ShapeDtypeStruct((rows, width), BF16),
        scratch_shapes=[
            pltpu.VMEM((size, size), F32),
            pltpu.VMEM((3, width, width), F32),
            pair, pair, pair, pair, pair, pair,
            pltpu.VMEM((rows, size), BF16),
            pltpu.VMEM((rows, width), BF16),
            pltpu.SemaphoreType.DMA((6,)),
            pltpu.SemaphoreType.DMA((rows // chunk,)),
        ],
        compiler_params=pltpu.CompilerParams(vmem_limit_bytes=28 * 1024 * 1024),
        cost_estimate=pl.CostEstimate(
            flops=21 * 6 * size**3 + 2 * rows * size * width,
            bytes_accessed=3 * rows * width * 2,
            transcendentals=0,
        ),
        name="rotate",
    )(mine, theirs, *owns, *others)


def after(value, *others):
    return lax.optimization_barrier((value, others))[0]


def on_device(vectors, blocks, tile_cols, live_tiles):
    tiles, _, tile, _ = blocks.shape
    width = vectors.shape[1]
    count = lax.axis_size("patch")
    pairs = {
        "even": [(i, i ^ 1) for i in range(count)],
        "odd": [(i, ((i + 1) ^ 1) - 1) for i in range(1, count - 1)],
    }

    def exchange(name, value):
        return lax.ppermute(value, "patch", pairs[name])

    def sibling(value):
        return lax.ppermute(value, "cols", [(0, 1), (1, 0)])

    start = vectors.reshape(tiles, tile, width)
    table = jnp.concatenate([tile_cols.T, jnp.broadcast_to(live_tiles[None], (1, tiles))])

    edges = dict(zip(("even", "odd"), masked_edges(table, start)))
    lead, lag = "even", "odd"
    halo = {lead: exchange(lead, edges[lead])}
    inner, *edge_blocks = load_fields(after(table, edges[lead]), start, blocks)
    halo[lag] = exchange(lag, after(edges[lag], inner))
    stored = dict(zip(("even", "odd"), edge_blocks))
    prev = dict.fromkeys(("even", "odd", "inner"))

    def inner_rows(behind):
        sources = after(edges["even"], behind), edges["odd"], inner
        return tile_rows("inner", table, stored["inner"], sources, prev["inner"], SMALL)

    def edge_rows(name, behind, cost=SMALL):
        sources = after(halo[name], behind), edges[name], inner
        return tile_rows(name, table, stored[name], sources, prev[name], cost)

    for step in range(STEPS):
        final = step == STEPS - 1
        new = {}
        if final:
            new["inner"] = inner_rows(edges["odd"])
            new[lead] = edge_rows(lead, new["inner"])
            flat = [new[name].reshape(-1, width) for name in (lead, "inner")]
            others = [sibling(value) for value in flat]
            new[lag] = edge_rows(lag, new[lead], LARGE)
        else:
            new[lead] = edge_rows(lead, inner)
            halo[lead] = exchange(lead, new[lead])
            if step == 0:
                stored["inner"] = load_blocks(after(blocks, new[lead]))
            new["inner"] = inner_rows(new[lead])
            new[lag] = edge_rows(lag, new["inner"])
            halo[lag] = exchange(lag, new[lag])
            halo[lead] = after(halo[lead], new[lag])
        prev = dict(edges, inner=inner)
        edges, inner = {name: new[name] for name in edges}, new["inner"]
    last = edges[lag].reshape(-1, width)
    other_last = sibling(last)
    others = [after(other, last) for other in others]
    mine = sum_over_patch(gram_share(last, other_last, gram(flat, others)))
    theirs = sibling(mine)
    total_rows = tiles * tile * count
    return rotate(mine, theirs, flat + [last], others + [other_last], total_rows, (lead, lag))


def solution(mesh):
    in_specs = (P("patch", "cols"), P("patch", None, None, None), P("patch", None), P("patch"))
    return jax.shard_map(
        on_device, mesh=mesh, in_specs=in_specs, out_specs=P("patch", "cols"), check_vma=False
    )
```

```python
import functools

import jax
import jax.numpy as jnp
from jax import lax
from jax.experimental import pallas as pl
from jax.experimental.pallas import tpu as pltpu
from jax.sharding import PartitionSpec as P

HALO_T = 4
STEPS = 3
ITERS = 8
WAYS = 4
LOAD_CUTS = 4
GRAM_ROWS = 1536
GROUP = 12

SMALL = pl.CostEstimate(flops=1000, bytes_accessed=1000, transcendentals=0)
LARGE = pl.CostEstimate(flops=10**11, bytes_accessed=1000, transcendentals=0)
SMALL_VMEM = pltpu.CompilerParams(vmem_limit_bytes=8 * 1024 * 1024)
ANY = pl.BlockSpec(memory_space=pl.ANY)
HBM = pl.BlockSpec(memory_space=pltpu.HBM)
VMEM = pl.BlockSpec(memory_space=pltpu.VMEM)
EDGES_MB, FIELDS_MB, BLOCKS_MB = 53, 50, 44
SMEM = pl.BlockSpec(memory_space=pltpu.SMEM)
F32, BF16 = jnp.float32, jnp.bfloat16


def dot(a, b):
    return jnp.dot(a, b, preferred_element_type=F32)


def tile_row(blocks, listed, field):
    wide = jnp.concatenate([blocks(n) for n in range(len(listed))], axis=1)
    tall = jnp.concatenate([field(tile) for tile in listed], axis=0)
    return dot(wide, tall)


def finish(acc, prev, alive):
    value = acc if prev is None else 2.0 * acc - prev.astype(F32)
    return jnp.where(alive, value, 0.0).astype(BF16)


def at_end(name):
    odd = lax.axis_index("patch") % 2
    return 1 - odd if name == "even" else odd


def live_count(table):
    return table[table.shape[0] - 1, 0]


def edges_kernel(table_ref, whole_ref, even_ref, odd_ref, sem, table):
    edge, tiles = HALO_T, whole_ref.shape[0]
    outs = {"even": even_ref, "odd": odd_ref}
    firsts = {name: at_end(name) * (tiles - edge) for name in outs}
    load([(whole_ref, firsts[name], outs[name]) for name in outs], sem, (table_ref, table))
    for name in outs:
        clear_dead(outs[name], firsts[name], live_count(table))


def clear_dead(ref, first, live):
    def clear(index, carry):
        ref[index] = jnp.zeros(ref.shape[1:], BF16)
        return carry

    count = ref.shape[0]
    lax.fori_loop(jnp.clip(live - first, 0, count), count, clear, 0)


def load(moves, sem, *whole):
    copies = []
    for source, first, target in moves:
        count = target.shape[0] // LOAD_CUTS
        for cut in range(LOAD_CUTS):
            copies.append(
                pltpu.make_async_copy(
                    source.at[pl.ds(first + cut * count, count)],
                    target.at[pl.ds(cut * count, count)],
                    sem.at[len(copies)],
                )
            )
    for source, target in whole:
        copies.append(pltpu.make_async_copy(source, target, sem.at[len(copies)]))
    for copy in copies:
        copy.start()
    for copy in copies:
        copy.wait()


def fields_kernel(
    table_ref, whole_ref, blocks_ref, inner_ref, even_blocks, odd_blocks, sem, table
):
    last = whole_ref.shape[0] - HALO_T
    moves = [
        (blocks_ref, at_end("even") * last, even_blocks),
        (blocks_ref, at_end("odd") * last, odd_blocks),
        (whole_ref, HALO_T, inner_ref),
    ]
    load(moves, sem, (table_ref, table))
    clear_dead(inner_ref, HALO_T, live_count(table))


def blocks_kernel(blocks_ref, inner_blocks, sem):
    load([(blocks_ref, HALO_T, inner_blocks)], sem)


def load_call(body, name, args, shapes, megabytes, table=()):
    return pl.pallas_call(
        body,
        in_specs=[VMEM] * len(table) + [HBM] * len(args),
        out_specs=[VMEM] * len(shapes),
        out_shape=shapes,
        scratch_shapes=[pltpu.SemaphoreType.DMA((len(shapes) * LOAD_CUTS + len(table),))]
        + [pltpu.SMEM(array.shape, array.dtype) for array in table],
        compiler_params=pltpu.CompilerParams(vmem_limit_bytes=megabytes * 1024 * 1024),
        cost_estimate=SMALL,
        name=name,
    )(*table, *args)


def masked_edges(table, start):
    shapes = [jax.ShapeDtypeStruct((HALO_T,) + start.shape[1:], BF16)] * 2
    return load_call(edges_kernel, "masked_edges", [start], shapes, EDGES_MB, [table])


def load_fields(table, start, blocks):
    inner = start.shape[0] - 2 * HALO_T
    shapes = [jax.ShapeDtypeStruct((inner,) + start.shape[1:], BF16)]
    shapes += [jax.ShapeDtypeStruct((HALO_T,) + blocks.shape[1:], blocks.dtype)] * 2
    return load_call(fields_kernel, "load_fields", [start, blocks], shapes, FIELDS_MB, [table])


def load_blocks(blocks):
    inner = blocks.shape[0] - 2 * HALO_T
    shapes = [jax.ShapeDtypeStruct((inner,) + blocks.shape[1:], blocks.dtype)]
    return load_call(blocks_kernel, "load_blocks", [blocks], shapes, BLOCKS_MB)[0]


def layout(name, tiles):
    edge, last = HALO_T, tiles - HALO_T
    if name == "inner":
        ends = [at_end(which) for which in ("even", "odd")]
        pieces = [(i, 0, edge, end * last) for i, end in enumerate(ends)]
        return edge, 0, pieces + [(2, 0, tiles - 2 * edge, edge)]
    end = at_end(name)
    pieces = [
        (0, 0, edge, 2 * edge * end), (1, 0, edge, edge), (2, 0, edge, (2 + end) * edge),
        (2, tiles - 3 * edge, edge, 3 * edge * (1 - end)),
    ]
    return end * last, end * last - edge, pieces


def rows_kernel(name, table_ref, *refs):
    sources, (out_ref, held, table, sem) = refs[:3], refs[-4:]
    blocks_ref = refs[-5]
    prev_ref = refs[3] if len(refs) == 9 else None
    fetch = pltpu.make_async_copy(table_ref, table, sem)
    fetch.start()
    nnz, tiles = blocks_ref.shape[1], table.shape[1]
    first, base, pieces = layout(name, tiles)
    for i, begin, count, slot in pieces:
        held[pl.ds(slot, count)] = sources[i][pl.ds(begin, count)]
    fetch.wait()
    live = live_count(table)
    shift = lax.axis_index("patch") * tiles + base
    rows = out_ref.shape[0]
    together = min(GROUP, rows)

    def group(index, carry):
        for r in range(together):
            row = index * together + r
            listed = [table[n, first + row] - shift for n in range(nnz)]
            acc = tile_row(lambda n: blocks_ref[row, n], listed, lambda c: held[c])
            prev = None if prev_ref is None else prev_ref[row]
            out_ref[row] = finish(acc, prev, first + row < live)
        return carry

    lax.fori_loop(0, rows // together, group, 0)


def tile_rows(name, table, blocks, sources, prev, cost):
    rows, _, tile, _ = blocks.shape
    width = sources[0].shape[-1]
    window = table.shape[1] if name == "inner" else 4 * HALO_T
    args = [table] + list(sources) + ([] if prev is None else [prev]) + [blocks]
    return pl.pallas_call(
        functools.partial(rows_kernel, name),
        in_specs=[VMEM] * len(args),
        out_specs=VMEM,
        out_shape=jax.ShapeDtypeStruct((rows, tile, width), BF16),
        scratch_shapes=[
            pltpu.VMEM((window, tile, width), BF16),
            pltpu.SMEM(table.shape, jnp.int32),
            pltpu.SemaphoreType.DMA,
        ],
        compiler_params=SMALL_VMEM,
        cost_estimate=cost,
        name="rows_" + name,
    )(*args)


ACROSS = (((0,), (0,)), ((), ()))


SPREAD = (2, 3, 1), (1, 3, 2)
ACROSS_GROUPS = (3, 2, 1), (3, 2, 1)
GATHER = (3, 1, 2), (3, 2, 1)


def quarter_order(distances):
    own = lax.axis_index("patch") % WAYS
    first_core = lax.axis_index("cols") == 0
    return [own] + [own ^ jnp.where(first_core, one, two) for one, two in zip(*distances)]


def add_gram(chunk, own_ref, other_ref, total):
    chunk = min(chunk, own_ref.shape[0])

    def add(index, carry):
        rows = pl.ds(pl.multiple_of(index * chunk, chunk), chunk)
        own = own_ref[rows, :]
        both = jnp.concatenate([own, other_ref[rows, :]], axis=1)
        total[...] += lax.dot_general(own, both, ACROSS, preferred_element_type=F32)
        return carry

    lax.fori_loop(0, own_ref.shape[0] // chunk, add, 0)


def gram_kernel(chunk, *refs):
    count = len(refs) // 2
    refs[-1][...] = jnp.zeros(refs[-1].shape, F32)
    for own_ref, other_ref in zip(refs[:count], refs[count:-1]):
        add_gram(chunk, own_ref, other_ref, refs[-1])


def share_kernel(chunk, own_ref, other_ref, start_ref, *refs):
    outs, (total, share) = refs[:WAYS], refs[WAYS:]
    total[...] = start_ref[...]
    add_gram(chunk, own_ref, other_ref, total)
    width = total.shape[0]
    half = width // 2
    own, other = total[:, :width], total[:, width:]
    first_core = lax.axis_index("cols") == 0
    second = jnp.where(first_core, other[:half, :half], other[:half, half:])
    third = jnp.where(first_core, other[:half, half:], other[half:, half:])
    blocks = [own[:half, :half], own[:half, half:], own[half:, half:], second, third]
    for i, block in enumerate(blocks):
        share[pl.ds(i * half, half), :] = block
    for out, quarter in zip(outs, quarter_order(SPREAD)):
        rows = out.shape[0]
        out[...] = share[pl.ds(pl.multiple_of(quarter * rows, 8), rows), :]


def gram_call(body, name, args, shape, scratch=(), outs=0):
    out_shape = jax.ShapeDtypeStruct(shape, F32)
    return pl.pallas_call(
        body,
        in_specs=[VMEM] * len(args),
        out_specs=[VMEM] * outs if outs else VMEM,
        out_shape=[out_shape] * outs if outs else out_shape,
        scratch_shapes=scratch,
        compiler_params=SMALL_VMEM,
        cost_estimate=SMALL,
        name=name,
    )(*args)


def gram(owns, others):
    width = owns[0].shape[1]
    body = functools.partial(gram_kernel, GRAM_ROWS)
    return gram_call(body, "gram", owns + others, (width, 2 * width))


def gram_share(own, other, start):
    rows, width = own.shape
    half = width // 2
    body = functools.partial(share_kernel, rows)
    scratch = [pltpu.VMEM((width, 2 * width), F32), pltpu.VMEM((5 * half, half), F32)]
    shape = (5 * half // WAYS, half)
    return gram_call(body, "gram_share", [own, other, start], shape, scratch, outs=WAYS)


def add_kernel(a, b, c, d, out):
    out[...] = (a[...] + b[...]) + (c[...] + d[...])


def join_kernel(*refs):
    parts, out = refs[:-1], refs[-1]
    rows = parts[0].shape[0]
    for part, quarter in zip(parts, quarter_order(GATHER)):
        out[pl.ds(pl.multiple_of(quarter * rows, 8), rows), :] = part[...]


def sum_over_patch(parts):
    count = lax.axis_size("patch")
    rows, columns = parts[0].shape

    def add_four(values):
        return gram_call(add_kernel, "add_four", values, (rows, columns))

    def from_others(values, distances, stride=1):
        got = []
        for value, both in zip(values, zip(*distances)):
            pairs = [
                (core * count + i, core * count + (i ^ (distance * stride)))
                for core, distance in enumerate(both)
                for i in range(count)
            ]
            got.append(lax.ppermute(value, ("cols", "patch"), pairs))
        return got

    total = add_four([parts[0]] + from_others(parts[1:], SPREAD))
    stride = WAYS
    while stride < count:
        total = add_four([total] + from_others([total] * (WAYS - 1), ACROSS_GROUPS, stride))
        stride *= WAYS
    quarters = [total] + from_others([total] * (WAYS - 1), GATHER)
    return gram_call(join_kernel, "join", quarters, (WAYS * rows, columns))


def split(value):
    high = value.astype(BF16)
    return high, (value - high.astype(F32)).astype(BF16)


def put(pair, blocks, right=False):
    width = blocks[0].shape[0]
    places = [(0, 0), (0, 1), (1, 1)]
    if right:
        blocks, places = tuple(blocks) + (blocks[1].T,), places + [(1, 0)]
    for (row, col), block in zip(places, blocks):
        for i, piece in enumerate(split(block)):
            pair[i, pl.ds(row * width, width), pl.ds(col * width, width)] = piece


def product3(left, right):
    return dot(
        jnp.concatenate([left[0], left[0], left[1]], axis=1),
        jnp.concatenate([right[0], right[1], right[0]], axis=0),
    )


def product(lefts, right):
    width = right.shape[1] // 2
    rows = [jnp.concatenate([left[i, :width, :] for left in lefts], axis=0) for i in range(2)]
    cols = [jnp.concatenate([left[i, :, width:] for left in lefts], axis=1) for i in range(2)]
    first = product3(rows, (right[0], right[1]))
    second = product3((right[0, width:, :], right[1, width:, :]), cols)
    out = []
    for i in range(len(lefts)):
        at = slice(i * width, (i + 1) * width)
        out.append((first[at, :width], first[at, width:], second[:, at]))
    return out


def combine(*terms, unit=0.0):
    width = terms[0][1][0].shape[0]
    row = lax.broadcasted_iota(jnp.int32, (width, width), 0)
    col = lax.broadcasted_iota(jnp.int32, (width, width), 1)
    diagonal = jnp.where(row == col, unit, 0.0)
    out = []
    for i in range(3):
        value = functools.reduce(jnp.add, [factor * matrix[i] for factor, matrix in terms])
        out.append(value if i == 1 else value + diagonal)
    return tuple(out)


def finish_kernel(total_rows, chunk, names, mine, theirs, *refs):
    fields, out_ref = refs[:6], refs[6]
    x_ref, x_held, x_pair, q_pair, u_pair, n_pair, v_pair, z_pair = refs[7:15]
    wide, result, sem, out_sem = refs[15:]
    part = lax.axis_index("cols")
    size = x_ref.shape[0]
    width = size // 2
    half = width // 2
    edge_size = fields[0].shape[0]
    end = wide.shape[0] - edge_size
    starts = [at_end(names[0]) * end, edge_size, at_end(names[1]) * end]
    copies = []
    for i, source in enumerate(fields):
        rows = pl.ds(pl.multiple_of(starts[i % 3], edge_size), source.shape[0])
        side = part if i < 3 else 1 - part
        target = wide.at[rows, pl.ds(pl.multiple_of(side * width, width), width)]
        copies.append(pltpu.make_async_copy(source, target, sem.at[i]))
    for copy in copies:
        copy.start()

    def block(side, index):
        rows = pl.ds(index * half, half)
        return jnp.where(part == side, mine[rows, :], theirs[rows, :])

    def place(row, col, value):
        x_ref[pl.ds(row * half, half), pl.ds(col * half, half)] = value

    for side in range(2):
        across = block(side, 1)
        place(2 * side, 2 * side, block(side, 0))
        place(2 * side, 2 * side + 1, across)
        place(2 * side + 1, 2 * side, across.T)
        place(2 * side + 1, 2 * side + 1, block(side, 2))
        for col in (0, 1):
            part_of = block(side, 3 + col)
            place(side, 2 + col, part_of if side == 0 else part_of.T)

    gram = x_ref[:width, :width], x_ref[:width, width:], x_ref[width:, width:]
    squares = gram[0] * gram[0] + 2.0 * (gram[1] * gram[1]) + gram[2] * gram[2]
    norm = jnp.sqrt(jnp.sum(squares, keepdims=True))

    def set_x(x):
        put(x_pair, x, right=True)
        for i, value in enumerate(x):
            x_held[i] = value

    def two_sweeps(first=False, last=False):
        x = tuple(x_held[i] for i in range(3))
        (q,) = product([x_pair], x_pair)
        put(q_pair, q)
        put(u_pair, combine((0.0625, q), (-0.5625, x), unit=1.6875), right=True)
        (qu,) = product([q_pair], u_pair)
        x = tuple(x_held[i] for i in range(3))
        n = combine((1.0, qu), (-2.4375, x), unit=2.25)
        put(n_pair, n, right=True)
        if last:
            return product([z_pair], n_pair)[0]
        if first:
            z = n
            (v,) = product([x_pair], n_pair)
        else:
            v, z = product([x_pair, z_pair], n_pair)
        put(v_pair, v)
        put(z_pair, z)
        set_x(product([v_pair], n_pair)[0])

    set_x(tuple(value / norm for value in gram))
    two_sweeps(first=True)

    def body(index, carry):
        two_sweeps()
        return carry

    lax.fori_loop(0, ITERS // 2 - 2, body, 0)
    first, across, second = two_sweeps(last=True)
    z_ref = x_ref
    z_ref[:width, :width] = first
    z_ref[:width, width:] = across
    z_ref[width:, :width] = across.T
    z_ref[width:, width:] = second
    own = pl.ds(pl.multiple_of(part * width, width), width)
    rotation = z_ref[:, own].astype(BF16)
    factor = jnp.sqrt(total_rows / norm)
    for copy in copies:
        copy.wait()
    count = wide.shape[0] // chunk
    outs = []
    for i in range(count):
        rows = pl.ds(i * chunk, chunk)
        result[rows, :] = (dot(wide[rows, :], rotation) * factor).astype(BF16)
        outs.append(pltpu.make_async_copy(result.at[rows], out_ref.at[rows], out_sem.at[i]))
        outs[-1].start()
    for out in outs:
        out.wait()


def rotate(mine, theirs, owns, others, total_rows, names):
    width = owns[0].shape[1]
    rows = sum(own.shape[0] for own in owns)
    size = 2 * width
    chunk = min(rows, 512)
    body = functools.partial(finish_kernel, float(total_rows), chunk, names)
    pair = pltpu.VMEM((2, size, size), BF16)
    return pl.pallas_call(
        body,
        in_specs=[VMEM, VMEM] + [ANY] * 6,
        out_specs=ANY,
        out_shape=jax.ShapeDtypeStruct((rows, width), BF16),
        scratch_shapes=[
            pltpu.VMEM((size, size), F32),
            pltpu.VMEM((3, width, width), F32),
            pair, pair, pair, pair, pair, pair,
            pltpu.VMEM((rows, size), BF16),
            pltpu.VMEM((rows, width), BF16),
            pltpu.SemaphoreType.DMA((6,)),
            pltpu.SemaphoreType.DMA((rows // chunk,)),
        ],
        compiler_params=pltpu.CompilerParams(vmem_limit_bytes=28 * 1024 * 1024),
        cost_estimate=pl.CostEstimate(
            flops=21 * 6 * size**3 + 2 * rows * size * width,
            bytes_accessed=3 * rows * width * 2,
            transcendentals=0,
        ),
        name="rotate",
    )(mine, theirs, *owns, *others)


def after(value, *others):
    return lax.optimization_barrier((value, others))[0]


def on_device(vectors, blocks, tile_cols, live_tiles):
    tiles, _, tile, _ = blocks.shape
    width = vectors.shape[1]
    count = lax.axis_size("patch")
    pairs = {
        "even": [(i, i ^ 1) for i in range(count)],
        "odd": [(i, ((i + 1) ^ 1) - 1) for i in range(1, count - 1)],
    }

    def exchange(name, value):
        return lax.ppermute(value, "patch", pairs[name])

    def sibling(value):
        return lax.ppermute(value, "cols", [(0, 1), (1, 0)])

    start = vectors.reshape(tiles, tile, width)
    table = jnp.concatenate([tile_cols.T, jnp.broadcast_to(live_tiles[None], (1, tiles))])

    edges = dict(zip(("even", "odd"), masked_edges(table, start)))
    lead, lag = "even", "odd"
    halo = {lead: exchange(lead, edges[lead])}
    inner, *edge_blocks = load_fields(after(table, edges[lead]), start, blocks)
    halo[lag] = exchange(lag, after(edges[lag], inner))
    stored = dict(zip(("even", "odd"), edge_blocks))
    prev = dict.fromkeys(("even", "odd", "inner"))

    def inner_rows(behind):
        sources = after(edges["even"], behind), edges["odd"], inner
        return tile_rows("inner", table, stored["inner"], sources, prev["inner"], SMALL)

    def edge_rows(name, behind, cost=SMALL):
        sources = after(halo[name], behind), edges[name], inner
        return tile_rows(name, table, stored[name], sources, prev[name], cost)

    for step in range(STEPS):
        final = step == STEPS - 1
        new = {}
        if final:
            new["inner"] = inner_rows(edges["odd"])
            new[lead] = edge_rows(lead, new["inner"])
            flat = [new[name].reshape(-1, width) for name in (lead, "inner")]
            others = [sibling(value) for value in flat]
            new[lag] = edge_rows(lag, new[lead], LARGE)
        else:
            new[lead] = edge_rows(lead, inner)
            halo[lead] = exchange(lead, new[lead])
            if step == 0:
                stored["inner"] = load_blocks(after(blocks, new[lead]))
                new[lag] = edge_rows(lag, stored["inner"])
                new["inner"] = inner_rows(new[lag])
            else:
                new["inner"] = inner_rows(new[lead])
                new[lag] = edge_rows(lag, new["inner"])
            halo[lag] = exchange(lag, new[lag])
            halo[lead] = after(halo[lead], new[lag], new["inner"])
        prev = dict(edges, inner=inner)
        edges, inner = {name: new[name] for name in edges}, new["inner"]
    last = edges[lag].reshape(-1, width)
    other_last = sibling(last)
    others = [after(other, last) for other in others]
    mine = sum_over_patch(gram_share(last, other_last, gram(flat, others)))
    theirs = sibling(mine)
    total_rows = tiles * tile * count
    return rotate(mine, theirs, flat + [last], others + [other_last], total_rows, (lead, lag))


def solution(mesh):
    in_specs = (P("patch", "cols"), P("patch", None, None, None), P("patch", None), P("patch"))
    return jax.shard_map(
        on_device, mesh=mesh, in_specs=in_specs, out_specs=P("patch", "cols"), check_vma=False
    )
```

```python
import functools

import jax
import jax.numpy as jnp
from jax import lax
from jax.experimental import pallas as pl
from jax.experimental.pallas import tpu as pltpu
from jax.sharding import PartitionSpec as P

HALO_T = 4
STEPS = 3
ITERS = 8
WAYS = 4
LOAD_CUTS = 4
GRAM_ROWS = 1536
GROUP = 12

SMALL = pl.CostEstimate(flops=1000, bytes_accessed=1000, transcendentals=0)
LARGE = pl.CostEstimate(flops=10**11, bytes_accessed=1000, transcendentals=0)
SMALL_VMEM = pltpu.CompilerParams(vmem_limit_bytes=8 * 1024 * 1024)
ANY = pl.BlockSpec(memory_space=pl.ANY)
HBM = pl.BlockSpec(memory_space=pltpu.HBM)
VMEM = pl.BlockSpec(memory_space=pltpu.VMEM)
EDGES_MB, FIELDS_MB, BLOCKS_MB = 53, 50, 44
SMEM = pl.BlockSpec(memory_space=pltpu.SMEM)
F32, BF16 = jnp.float32, jnp.bfloat16


def dot(a, b):
    return jnp.dot(a, b, preferred_element_type=F32)


def tile_row(blocks, listed, field):
    wide = jnp.concatenate([blocks(n) for n in range(len(listed))], axis=1)
    tall = jnp.concatenate([field(tile) for tile in listed], axis=0)
    return dot(wide, tall)


def finish(acc, prev, alive):
    value = acc if prev is None else 2.0 * acc - prev.astype(F32)
    return jnp.where(alive, value, 0.0).astype(BF16)


def at_end(name):
    odd = lax.axis_index("patch") % 2
    return 1 - odd if name == "even" else odd


def live_count(table):
    return table[table.shape[0] - 1, 0]


def edges_kernel(table_ref, whole_ref, even_ref, odd_ref, sem, table):
    edge, tiles = HALO_T, whole_ref.shape[0]
    outs = {"even": even_ref, "odd": odd_ref}
    firsts = {name: at_end(name) * (tiles - edge) for name in outs}
    load([(whole_ref, firsts[name], outs[name]) for name in outs], sem, (table_ref, table))
    for name in outs:
        clear_dead(outs[name], firsts[name], live_count(table))


def clear_dead(ref, first, live):
    def clear(index, carry):
        ref[index] = jnp.zeros(ref.shape[1:], BF16)
        return carry

    count = ref.shape[0]
    lax.fori_loop(jnp.clip(live - first, 0, count), count, clear, 0)


def load(moves, sem, *whole):
    copies = []
    for source, first, target in moves:
        count = target.shape[0] // LOAD_CUTS
        for cut in range(LOAD_CUTS):
            copies.append(
                pltpu.make_async_copy(
                    source.at[pl.ds(first + cut * count, count)],
                    target.at[pl.ds(cut * count, count)],
                    sem.at[len(copies)],
                )
            )
    for source, target in whole:
        copies.append(pltpu.make_async_copy(source, target, sem.at[len(copies)]))
    for copy in copies:
        copy.start()
    for copy in copies:
        copy.wait()


def fields_kernel(
    table_ref, whole_ref, blocks_ref, inner_ref, even_blocks, odd_blocks, sem, table
):
    last = whole_ref.shape[0] - HALO_T
    moves = [
        (blocks_ref, at_end("even") * last, even_blocks),
        (blocks_ref, at_end("odd") * last, odd_blocks),
        (whole_ref, HALO_T, inner_ref),
    ]
    load(moves, sem, (table_ref, table))
    clear_dead(inner_ref, HALO_T, live_count(table))


def blocks_kernel(blocks_ref, inner_blocks, sem):
    load([(blocks_ref, HALO_T, inner_blocks)], sem)


def load_call(body, name, args, shapes, megabytes, table=()):
    return pl.pallas_call(
        body,
        in_specs=[VMEM] * len(table) + [HBM] * len(args),
        out_specs=[VMEM] * len(shapes),
        out_shape=shapes,
        scratch_shapes=[pltpu.SemaphoreType.DMA((len(shapes) * LOAD_CUTS + len(table),))]
        + [pltpu.SMEM(array.shape, array.dtype) for array in table],
        compiler_params=pltpu.CompilerParams(vmem_limit_bytes=megabytes * 1024 * 1024),
        cost_estimate=SMALL,
        name=name,
    )(*table, *args)


def masked_edges(table, start):
    shapes = [jax.ShapeDtypeStruct((HALO_T,) + start.shape[1:], BF16)] * 2
    return load_call(edges_kernel, "masked_edges", [start], shapes, EDGES_MB, [table])


def load_fields(table, start, blocks):
    inner = start.shape[0] - 2 * HALO_T
    shapes = [jax.ShapeDtypeStruct((inner,) + start.shape[1:], BF16)]
    shapes += [jax.ShapeDtypeStruct((HALO_T,) + blocks.shape[1:], blocks.dtype)] * 2
    return load_call(fields_kernel, "load_fields", [start, blocks], shapes, FIELDS_MB, [table])


def load_blocks(blocks):
    inner = blocks.shape[0] - 2 * HALO_T
    shapes = [jax.ShapeDtypeStruct((inner,) + blocks.shape[1:], blocks.dtype)]
    return load_call(blocks_kernel, "load_blocks", [blocks], shapes, BLOCKS_MB)[0]


def layout(name, tiles):
    edge, last = HALO_T, tiles - HALO_T
    if name == "inner":
        ends = [at_end(which) for which in ("even", "odd")]
        pieces = [(i, 0, edge, end * last) for i, end in enumerate(ends)]
        return edge, 0, pieces + [(2, 0, tiles - 2 * edge, edge)]
    end = at_end(name)
    pieces = [
        (0, 0, edge, 2 * edge * end), (1, 0, edge, edge), (2, 0, edge, (2 + end) * edge),
        (2, tiles - 3 * edge, edge, 3 * edge * (1 - end)),
    ]
    return end * last, end * last - edge, pieces


def rows_kernel(name, table_ref, *refs):
    sources, (out_ref, held, table, sem) = refs[:3], refs[-4:]
    blocks_ref = refs[-5]
    prev_ref = refs[3] if len(refs) == 9 else None
    fetch = pltpu.make_async_copy(table_ref, table, sem)
    fetch.start()
    nnz, tiles = blocks_ref.shape[1], table.shape[1]
    first, base, pieces = layout(name, tiles)
    for i, begin, count, slot in pieces:
        held[pl.ds(slot, count)] = sources[i][pl.ds(begin, count)]
    fetch.wait()
    live = live_count(table)
    shift = lax.axis_index("patch") * tiles + base
    rows = out_ref.shape[0]
    together = min(GROUP, rows)

    def group(index, carry):
        for r in range(together):
            row = index * together + r
            listed = [table[n, first + row] - shift for n in range(nnz)]
            acc = tile_row(lambda n: blocks_ref[row, n], listed, lambda c: held[c])
            prev = None if prev_ref is None else prev_ref[row]
            out_ref[row] = finish(acc, prev, first + row < live)
        return carry

    lax.fori_loop(0, rows // together, group, 0)


def tile_rows(name, table, blocks, sources, prev, cost):
    rows, _, tile, _ = blocks.shape
    width = sources[0].shape[-1]
    window = table.shape[1] if name == "inner" else 4 * HALO_T
    args = [table] + list(sources) + ([] if prev is None else [prev]) + [blocks]
    return pl.pallas_call(
        functools.partial(rows_kernel, name),
        in_specs=[VMEM] * len(args),
        out_specs=VMEM,
        out_shape=jax.ShapeDtypeStruct((rows, tile, width), BF16),
        scratch_shapes=[
            pltpu.VMEM((window, tile, width), BF16),
            pltpu.SMEM(table.shape, jnp.int32),
            pltpu.SemaphoreType.DMA,
        ],
        compiler_params=SMALL_VMEM,
        cost_estimate=cost,
        name="rows_" + name,
    )(*args)


ACROSS = (((0,), (0,)), ((), ()))


SPREAD = (2, 3, 1), (1, 3, 2)
ACROSS_GROUPS = (3, 2, 1), (3, 2, 1)
GATHER = (3, 1, 2), (3, 2, 1)


def quarter_order(distances):
    own = lax.axis_index("patch") % WAYS
    first_core = lax.axis_index("cols") == 0
    return [own] + [own ^ jnp.where(first_core, one, two) for one, two in zip(*distances)]


def add_gram(chunk, own_ref, other_ref, total):
    chunk = min(chunk, own_ref.shape[0])

    def add(index, carry):
        rows = pl.ds(pl.multiple_of(index * chunk, chunk), chunk)
        own = own_ref[rows, :]
        both = jnp.concatenate([own, other_ref[rows, :]], axis=1)
        total[...] += lax.dot_general(own, both, ACROSS, preferred_element_type=F32)
        return carry

    lax.fori_loop(0, own_ref.shape[0] // chunk, add, 0)


def gram_kernel(chunk, *refs):
    count = len(refs) // 2
    refs[-1][...] = jnp.zeros(refs[-1].shape, F32)
    for own_ref, other_ref in zip(refs[:count], refs[count:-1]):
        add_gram(chunk, own_ref, other_ref, refs[-1])


def share_kernel(chunk, own_ref, other_ref, start_ref, *refs):
    outs, (total, share) = refs[:WAYS], refs[WAYS:]
    total[...] = start_ref[...]
    add_gram(chunk, own_ref, other_ref, total)
    width = total.shape[0]
    half = width // 2
    own, other = total[:, :width], total[:, width:]
    first_core = lax.axis_index("cols") == 0
    second = jnp.where(first_core, other[:half, :half], other[:half, half:])
    third = jnp.where(first_core, other[:half, half:], other[half:, half:])
    blocks = [own[:half, :half], own[:half, half:], own[half:, half:], second, third]
    for i, block in enumerate(blocks):
        share[pl.ds(i * half, half), :] = block
    for out, quarter in zip(outs, quarter_order(SPREAD)):
        rows = out.shape[0]
        out[...] = share[pl.ds(pl.multiple_of(quarter * rows, 8), rows), :]


def gram_call(body, name, args, shape, scratch=(), outs=0):
    out_shape = jax.ShapeDtypeStruct(shape, F32)
    return pl.pallas_call(
        body,
        in_specs=[VMEM] * len(args),
        out_specs=[VMEM] * outs if outs else VMEM,
        out_shape=[out_shape] * outs if outs else out_shape,
        scratch_shapes=scratch,
        compiler_params=SMALL_VMEM,
        cost_estimate=SMALL,
        name=name,
    )(*args)


def gram(owns, others):
    width = owns[0].shape[1]
    body = functools.partial(gram_kernel, GRAM_ROWS)
    return gram_call(body, "gram", owns + others, (width, 2 * width))


def gram_share(own, other, start):
    rows, width = own.shape
    half = width // 2
    body = functools.partial(share_kernel, rows)
    scratch = [pltpu.VMEM((width, 2 * width), F32), pltpu.VMEM((5 * half, half), F32)]
    shape = (5 * half // WAYS, half)
    return gram_call(body, "gram_share", [own, other, start], shape, scratch, outs=WAYS)


def add_kernel(a, b, c, d, out):
    out[...] = (a[...] + b[...]) + (c[...] + d[...])


def join_kernel(*refs):
    parts, out = refs[:-1], refs[-1]
    rows = parts[0].shape[0]
    for part, quarter in zip(parts, quarter_order(GATHER)):
        out[pl.ds(pl.multiple_of(quarter * rows, 8), rows), :] = part[...]


def sum_over_patch(parts):
    count = lax.axis_size("patch")
    rows, columns = parts[0].shape

    def add_four(values):
        return gram_call(add_kernel, "add_four", values, (rows, columns))

    def from_others(values, distances, stride=1):
        got = []
        for value, both in zip(values, zip(*distances)):
            pairs = [
                (core * count + i, core * count + (i ^ (distance * stride)))
                for core, distance in enumerate(both)
                for i in range(count)
            ]
            got.append(lax.ppermute(value, ("cols", "patch"), pairs))
        return got

    total = add_four([parts[0]] + from_others(parts[1:], SPREAD))
    stride = WAYS
    while stride < count:
        total = add_four([total] + from_others([total] * (WAYS - 1), ACROSS_GROUPS, stride))
        stride *= WAYS
    quarters = [total] + from_others([total] * (WAYS - 1), GATHER)
    return gram_call(join_kernel, "join", quarters, (WAYS * rows, columns))


def split(value):
    high = value.astype(BF16)
    return high, (value - high.astype(F32)).astype(BF16)


def put(pair, blocks, right=False):
    width = blocks[0].shape[0]
    places = [(0, 0), (0, 1), (1, 1)]
    if right:
        blocks, places = tuple(blocks) + (blocks[1].T,), places + [(1, 0)]
    for (row, col), block in zip(places, blocks):
        for i, piece in enumerate(split(block)):
            pair[i, pl.ds(row * width, width), pl.ds(col * width, width)] = piece


def product3(left, right):
    return dot(
        jnp.concatenate([left[0], left[0], left[1]], axis=1),
        jnp.concatenate([right[0], right[1], right[0]], axis=0),
    )


def product(lefts, right):
    width = right.shape[1] // 2
    rows = [jnp.concatenate([left[i, :width, :] for left in lefts], axis=0) for i in range(2)]
    cols = [jnp.concatenate([left[i, :, width:] for left in lefts], axis=1) for i in range(2)]
    first = product3(rows, (right[0], right[1]))
    second = product3((right[0, width:, :], right[1, width:, :]), cols)
    out = []
    for i in range(len(lefts)):
        at = slice(i * width, (i + 1) * width)
        out.append((first[at, :width], first[at, width:], second[:, at]))
    return out


def combine(*terms, unit=0.0):
    width = terms[0][1][0].shape[0]
    row = lax.broadcasted_iota(jnp.int32, (width, width), 0)
    col = lax.broadcasted_iota(jnp.int32, (width, width), 1)
    diagonal = jnp.where(row == col, unit, 0.0)
    out = []
    for i in range(3):
        value = functools.reduce(jnp.add, [factor * matrix[i] for factor, matrix in terms])
        out.append(value if i == 1 else value + diagonal)
    return tuple(out)


def finish_kernel(total_rows, chunk, names, mine, theirs, *refs):
    fields, out_ref = refs[:6], refs[6]
    x_ref, x_held, x_pair, q_pair, u_pair, n_pair, v_pair, z_pair = refs[7:15]
    wide, result, sem, out_sem = refs[15:]
    part = lax.axis_index("cols")
    size = x_ref.shape[0]
    width = size // 2
    half = width // 2
    edge_size = fields[0].shape[0]
    end = wide.shape[0] - edge_size
    starts = [at_end(names[0]) * end, edge_size, at_end(names[1]) * end]
    copies = []
    for i, source in enumerate(fields):
        rows = pl.ds(pl.multiple_of(starts[i % 3], edge_size), source.shape[0])
        side = part if i < 3 else 1 - part
        target = wide.at[rows, pl.ds(pl.multiple_of(side * width, width), width)]
        copies.append(pltpu.make_async_copy(source, target, sem.at[i]))
    for copy in copies:
        copy.start()

    def block(side, index):
        rows = pl.ds(index * half, half)
        return jnp.where(part == side, mine[rows, :], theirs[rows, :])

    def place(row, col, value):
        x_ref[pl.ds(row * half, half), pl.ds(col * half, half)] = value

    for side in range(2):
        across = block(side, 1)
        place(2 * side, 2 * side, block(side, 0))
        place(2 * side, 2 * side + 1, across)
        place(2 * side + 1, 2 * side, across.T)
        place(2 * side + 1, 2 * side + 1, block(side, 2))
        for col in (0, 1):
            part_of = block(side, 3 + col)
            place(side, 2 + col, part_of if side == 0 else part_of.T)

    gram = x_ref[:width, :width], x_ref[:width, width:], x_ref[width:, width:]
    squares = gram[0] * gram[0] + 2.0 * (gram[1] * gram[1]) + gram[2] * gram[2]
    norm = jnp.sqrt(jnp.sum(squares, keepdims=True))

    def set_x(x):
        put(x_pair, x, right=True)
        for i, value in enumerate(x):
            x_held[i] = value

    def two_sweeps(first=False, last=False):
        x = tuple(x_held[i] for i in range(3))
        (q,) = product([x_pair], x_pair)
        put(q_pair, q)
        put(u_pair, combine((0.0625, q), (-0.5625, x), unit=1.6875), right=True)
        (qu,) = product([q_pair], u_pair)
        x = tuple(x_held[i] for i in range(3))
        n = combine((1.0, qu), (-2.4375, x), unit=2.25)
        put(n_pair, n, right=True)
        if last:
            return product([z_pair], n_pair)[0]
        if first:
            z = n
            (v,) = product([x_pair], n_pair)
        else:
            v, z = product([x_pair, z_pair], n_pair)
        put(v_pair, v)
        put(z_pair, z)
        set_x(product([v_pair], n_pair)[0])

    set_x(tuple(value / norm for value in gram))
    two_sweeps(first=True)

    def body(index, carry):
        two_sweeps()
        return carry

    lax.fori_loop(0, ITERS // 2 - 2, body, 0)
    first, across, second = two_sweeps(last=True)
    z_ref = x_ref
    z_ref[:width, :width] = first
    z_ref[:width, width:] = across
    z_ref[width:, :width] = across.T
    z_ref[width:, width:] = second
    own = pl.ds(pl.multiple_of(part * width, width), width)
    rotation = z_ref[:, own].astype(BF16)
    factor = jnp.sqrt(total_rows / norm)
    for copy in copies:
        copy.wait()
    count = wide.shape[0] // chunk
    outs = []
    for i in range(count):
        rows = pl.ds(i * chunk, chunk)
        result[rows, :] = (dot(wide[rows, :], rotation) * factor).astype(BF16)
        outs.append(pltpu.make_async_copy(result.at[rows], out_ref.at[rows], out_sem.at[i]))
        outs[-1].start()
    for out in outs:
        out.wait()


def rotate(mine, theirs, owns, others, total_rows, names):
    width = owns[0].shape[1]
    rows = sum(own.shape[0] for own in owns)
    size = 2 * width
    chunk = min(rows, 512)
    body = functools.partial(finish_kernel, float(total_rows), chunk, names)
    pair = pltpu.VMEM((2, size, size), BF16)
    return pl.pallas_call(
        body,
        in_specs=[VMEM, VMEM] + [ANY] * 6,
        out_specs=ANY,
        out_shape=jax.ShapeDtypeStruct((rows, width), BF16),
        scratch_shapes=[
            pltpu.VMEM((size, size), F32),
            pltpu.VMEM((3, width, width), F32),
            pair, pair, pair, pair, pair, pair,
            pltpu.VMEM((rows, size), BF16),
            pltpu.VMEM((rows, width), BF16),
            pltpu.SemaphoreType.DMA((6,)),
            pltpu.SemaphoreType.DMA((rows // chunk,)),
        ],
        compiler_params=pltpu.CompilerParams(vmem_limit_bytes=28 * 1024 * 1024),
        cost_estimate=pl.CostEstimate(
            flops=21 * 6 * size**3 + 2 * rows * size * width,
            bytes_accessed=3 * rows * width * 2,
            transcendentals=0,
        ),
        name="rotate",
    )(mine, theirs, *owns, *others)


def after(value, *others):
    return lax.optimization_barrier((value, others))[0]


def on_device(vectors, blocks, tile_cols, live_tiles):
    tiles, _, tile, _ = blocks.shape
    width = vectors.shape[1]
    count = lax.axis_size("patch")
    pairs = {
        "even": [(i, i ^ 1) for i in range(count)],
        "odd": [(i, ((i + 1) ^ 1) - 1) for i in range(1, count - 1)],
    }

    def exchange(name, value):
        return lax.ppermute(value, "patch", pairs[name])

    def sibling(value):
        return lax.ppermute(value, "cols", [(0, 1), (1, 0)])

    start = vectors.reshape(tiles, tile, width)
    table = jnp.concatenate([tile_cols.T, jnp.broadcast_to(live_tiles[None], (1, tiles))])

    edges = dict(zip(("even", "odd"), masked_edges(table, start)))
    lead, lag = "even", "odd"
    halo = {lead: exchange(lead, edges[lead])}
    inner, *edge_blocks = load_fields(after(table, edges[lead]), start, blocks)
    halo[lag] = exchange(lag, edges[lag])
    stored = dict(zip(("even", "odd"), edge_blocks))
    prev = dict.fromkeys(("even", "odd", "inner"))

    def inner_rows(behind):
        sources = after(edges["even"], behind), edges["odd"], inner
        return tile_rows("inner", table, stored["inner"], sources, prev["inner"], SMALL)

    def edge_rows(name, behind, cost=SMALL):
        sources = after(halo[name], behind), edges[name], inner
        return tile_rows(name, table, stored[name], sources, prev[name], cost)

    for step in range(STEPS):
        final = step == STEPS - 1
        new = {}
        if final:
            new["inner"] = inner_rows(edges["odd"])
            new[lead] = edge_rows(lead, new["inner"])
            flat = [new[name].reshape(-1, width) for name in (lead, "inner")]
            others = [sibling(value) for value in flat]
            new[lag] = edge_rows(lag, new[lead], LARGE)
        else:
            new[lead] = edge_rows(lead, inner)
            halo[lead] = exchange(lead, new[lead])
            if step == 0:
                stored["inner"] = load_blocks(after(blocks, new[lead]))
                new[lag] = edge_rows(lag, stored["inner"])
                new["inner"] = inner_rows(new[lag])
            else:
                new["inner"] = inner_rows(new[lead])
                new[lag] = edge_rows(lag, new["inner"])
            halo[lag] = exchange(lag, new[lag])
            halo[lead] = after(halo[lead], new[lag], new["inner"])
        prev = dict(edges, inner=inner)
        edges, inner = {name: new[name] for name in edges}, new["inner"]
    last = edges[lag].reshape(-1, width)
    other_last = sibling(last)
    others = [after(other, last) for other in others]
    mine = sum_over_patch(gram_share(last, other_last, gram(flat, others)))
    theirs = sibling(mine)
    total_rows = tiles * tile * count
    return rotate(mine, theirs, flat + [last], others + [other_last], total_rows, (lead, lag))


def solution(mesh):
    in_specs = (P("patch", "cols"), P("patch", None, None, None), P("patch", None), P("patch"))
    return jax.shard_map(
        on_device, mesh=mesh, in_specs=in_specs, out_specs=P("patch", "cols"), check_vma=False
    )
```
